32 devices in a mesh: wide: 8 (over y, x, core), narrow: 4 (over z).
Axes of the slice: x: 2, y: 2, z: 4, core: 2. Of those that a mesh axis runs over, the one named last changes fastest.
Arguments:
- text_in: bfloat16 [8, 4, 512, 768], P(None, 'narrow', 'wide'), may hold values from -6 to 6
- patch_in: bfloat16 [8, 4, 576, 768], P('wide', None, 'narrow'), may hold values from -6 to 6
- res_class: int32 [8, 4], P('wide', 'narrow'), may hold values from 0 to 1, as said below
- text_len: int32 [8, 4], P('wide', 'narrow'), may hold values from 128 to 512, as said below
- pos_line: int32 [8, 4, 1088], P('wide', 'narrow'), may hold values from 0 to 63
- pos_x: int32 [8, 4, 1088], P('wide', 'narrow'), may hold values from 0 to 127
- pos_y: int32 [8, 4, 1088], P('wide', 'narrow'), may hold values from 0 to 127
- query_weight: bfloat16 [768, 768], replicated, may hold values from -0.21875 to 0.21875
- query_bias: float32 [768], replicated, may hold values from -1.8 to 1.8
- key_weight: bfloat16 [768, 768], replicated, may hold values from -0.21875 to 0.21875
- value_weight: bfloat16 [768, 768], replicated, may hold values from -0.21875 to 0.21875
- value_bias: float32 [768], replicated, may hold values from -1.8 to 1.8
- output_weight: bfloat16 [768, 768], replicated, may hold values from -0.875 to 0.875
- output_bias: float32 [768], replicated, may hold values from -3 to 3
- norm_gain: float32 [768], replicated, may hold values from 0.5 to 1.5
- norm_shift: float32 [768], replicated, may hold values from -1.8 to 1.8
- up_weight: bfloat16 [768, 3072], replicated, may hold values from -0.21875 to 0.21875
- up_bias: float32 [3072], replicated, may hold values from -3 to 3
- down_weight: bfloat16 [3072, 768], replicated, may hold values from -0.21875 to 0.21875
- down_bias: float32 [768], replicated, may hold values from -3 to 3
- final_gain: float32 [768], replicated, may hold values from 0.5 to 1.5
- final_shift: float32 [768], replicated, may hold values from -1.8 to 1.8
- line_table: float32 [33, 12], replicated, may hold values from -3 to 3
- width_table: float32 [65, 12], replicated, may hold values from -3 to 3
- height_table: float32 [65, 12], replicated, may hold values from -3 to 3
- cot_text: bfloat16 [8, 4, 512, 768], P(None, 'narrow', 'wide'), may hold values from -6 to 6
- cot_patch: bfloat16 [8, 4, 576, 768], P('wide', None, 'narrow'), may hold values from -6 to 6
Outputs:
- text_out: bfloat16 [8, 4, 512, 768], P(None, 'narrow', 'wide')
- patch_out: bfloat16 [8, 4, 576, 768], P('wide', None, 'narrow')
- text_grad: bfloat16 [8, 4, 512, 768], P(None, 'narrow', 'wide')
- patch_grad: bfloat16 [8, 4, 576, 768], P('wide', None, 'narrow')
- query_weight_grad: float32 [768, 768], replicated
- query_bias_grad: float32 [768], replicated
- key_weight_grad: float32 [768, 768], replicated
- value_weight_grad: float32 [768, 768], replicated
- value_bias_grad: float32 [768], replicated
- output_weight_grad: float32 [768, 768], replicated
- output_bias_grad: float32 [768], replicated
- norm_gain_grad: float32 [768], replicated
- norm_shift_grad: float32 [768], replicated
- up_weight_grad: float32 [768, 3072], replicated
- up_bias_grad: float32 [3072], replicated
- down_weight_grad: float32 [3072, 768], replicated
- down_bias_grad: float32 [768], replicated
- final_gain_grad: float32 [768], replicated
- final_shift_grad: float32 [768], replicated
- line_table_grad: float32 [33, 12], replicated
- width_table_grad: float32 [65, 12], replicated
- height_table_grad: float32 [65, 12], replicated
The draws below stay inside these ranges and needn't reach their ends.
Inputs may be any that keep to these rules, and one draw needn't show every extreme that they name: `res_class`: 0 for a page of 196 patches, 1 for one of 576; some page is of class 1 in every draw. `text_len`: the CLS row is always live; some page has all 512 text rows live in every draw.
All inputs are finite; a program needn't handle non-finite values.
Results may differ from the reference program's by a relative error of at most 0.018.
Values may be sent and summed in bfloat16 or wider, within the bound.
No kernel may reach another device: no remote copies, remote signals or barrier semaphores. Data moves between devices by JAX's collectives and lax.ppermute only.
A program may use at most 384 MiB of HBM per device.

```python
import jax
import jax.numpy as jnp
from jax import lax

D = 768
HEADS = 12
FF = 3072
TEXT = 512
PATCH = 576
SMALL_PATCH = 196
LINE_REACH = 16
BOX_REACH = 32
PAGES_A = 8
PAGES_B = 4
SEQ = 1088


def draw_res_class(key, part):
    key = jax.random.fold_in(key, 11)
    count = PAGES_A * PAGES_B
    classes = jax.random.randint(key, (count,), 0, 2)
    chosen = jax.random.randint(jax.random.fold_in(key, 1), (), 0, count)
    classes = jnp.where(jnp.arange(count) == chosen, 1, classes)
    return classes.reshape(PAGES_A, PAGES_B).astype(jnp.int32)


def draw_text_len(key, part):
    key = jax.random.fold_in(key, 23)
    count = PAGES_A * PAGES_B
    lengths = jax.random.randint(key, (count,), TEXT // 4, TEXT + 1)
    chosen = jax.random.randint(jax.random.fold_in(key, 1), (), 0, count)
    lengths = jnp.where(jnp.arange(count) == chosen, TEXT, lengths)
    return lengths.reshape(PAGES_A, PAGES_B).astype(jnp.int32)


def set_ends(entries, stream_key, smallest, largest):
    shape = entries.shape
    index_at = [jax.random.randint(jax.random.fold_in(stream_key, axis), (), 0, shape[axis]) for axis in range(len(shape))]
    entries = entries.at[tuple(index_at)].set(smallest)
    longest = shape.index(max(shape))
    index_at[longest] = (index_at[longest] + 1) % shape[longest]
    return entries.at[tuple(index_at)].set(largest)


def levels(stream_key, extent, cuts, least, high):
    level, own = 1.0, jax.random.fold_in(stream_key, 6)
    for position, shards_of in cuts:
        steps = jnp.exp(jax.random.uniform(jax.random.fold_in(own, position), (shards_of,), jnp.float32, least / len(cuts), high / len(cuts)))
        level = level * jnp.repeat(steps, extent[position] // shards_of).reshape([-1 if axis == position else 1 for axis in range(len(extent))])
    return level


def normal_values(stream_key, dims, deviation, most, pieces=(), held_as=jnp.bfloat16):
    drawn = deviation * jax.random.normal(stream_key, dims, jnp.float32)
    if pieces:
        drawn = drawn * levels(stream_key, dims, pieces, -0.22, 0.18)
    return jnp.clip(drawn, -most, most).astype(held_as)


def setup_inputs(seed: int = 0) -> dict:
    key_of = jax.random.split(jax.random.key(seed), 28)
    text_in = normal_values(key_of[0], (PAGES_A, PAGES_B, TEXT, D), 1.0, 6.0, ((1, 4), (2, 8)))
    patch_in = normal_values(key_of[1], (PAGES_A, PAGES_B, PATCH, D), 1.0, 6.0, ((0, 8), (2, 4)))
    res_class = draw_res_class(jax.random.fold_in(key_of[27], 71), 0)
    text_len = draw_text_len(jax.random.fold_in(key_of[27], 71), 0)
    pos_line = set_ends(jax.random.randint(key_of[4], (PAGES_A, PAGES_B, SEQ), 0, 4 * LINE_REACH), jax.random.fold_in(key_of[4], 1), 0, (4 * LINE_REACH) - 1).astype(jnp.int32)
    pos_x = set_ends(jax.random.randint(key_of[5], (PAGES_A, PAGES_B, SEQ), 0, 4 * BOX_REACH), jax.random.fold_in(key_of[5], 1), 0, (4 * BOX_REACH) - 1).astype(jnp.int32)
    pos_y = set_ends(jax.random.randint(key_of[6], (PAGES_A, PAGES_B, SEQ), 0, 4 * BOX_REACH), jax.random.fold_in(key_of[6], 1), 0, (4 * BOX_REACH) - 1).astype(jnp.int32)
    query_weight = normal_values(key_of[7], (D, D), D ** -0.5, 0.21875)
    query_bias = normal_values(key_of[8], (D,), 0.3, 1.8, (), jnp.float32)
    key_weight = normal_values(key_of[9], (D, D), D ** -0.5, 0.21875)
    value_weight = normal_values(key_of[10], (D, D), D ** -0.5, 0.21875)
    value_bias = normal_values(key_of[11], (D,), 0.3, 1.8, (), jnp.float32)
    output_weight = normal_values(key_of[12], (D, D), (D // 16) ** -0.5, 0.875)
    output_bias = normal_values(key_of[13], (D,), 0.5, 3.0, (), jnp.float32)
    norm_gain = jnp.clip(1.0 + 0.1 * jax.random.normal(key_of[14], (D,), jnp.float32), 0.5, 1.5)
    norm_shift = normal_values(key_of[15], (D,), 0.3, 1.8, (), jnp.float32)
    up_weight = normal_values(key_of[16], (D, FF), D ** -0.5, 0.21875)
    up_bias = normal_values(key_of[17], (FF,), 0.5, 3.0, (), jnp.float32)
    down_weight = normal_values(key_of[18], (FF, D), (FF // 4) ** -0.5, 0.21875)
    down_bias = normal_values(key_of[19], (D,), 0.5, 3.0, (), jnp.float32)
    final_gain = jnp.clip(1.0 + 0.1 * jax.random.normal(key_of[20], (D,), jnp.float32), 0.5, 1.5)
    final_shift = normal_values(key_of[21], (D,), 0.3, 1.8, (), jnp.float32)
    line_table = normal_values(key_of[22], (2 * LINE_REACH + 1, HEADS), 0.5, 3.0, (), jnp.float32)
    width_table = normal_values(key_of[23], (2 * BOX_REACH + 1, HEADS), 0.5, 3.0, (), jnp.float32)
    height_table = normal_values(key_of[24], (2 * BOX_REACH + 1, HEADS), 0.5, 3.0, (), jnp.float32)
    cot_text = normal_values(key_of[25], (PAGES_A, PAGES_B, TEXT, D), 1.0, 6.0, ((1, 4), (2, 8)))
    cot_patch = normal_values(key_of[26], (PAGES_A, PAGES_B, PATCH, D), 1.0, 6.0, ((0, 8), (2, 4)))
    return dict(text_in=text_in, patch_in=patch_in, res_class=res_class, text_len=text_len, pos_line=pos_line, pos_x=pos_x, pos_y=pos_y, query_weight=query_weight, query_bias=query_bias, key_weight=key_weight, value_weight=value_weight, value_bias=value_bias, output_weight=output_weight, output_bias=output_bias, norm_gain=norm_gain, norm_shift=norm_shift, up_weight=up_weight, up_bias=up_bias, down_weight=down_weight, down_bias=down_bias, final_gain=final_gain, final_shift=final_shift, line_table=line_table, width_table=width_table, height_table=height_table, cot_text=cot_text, cot_patch=cot_patch)


@jax.custom_vjp
def low(v):
    return lax.optimization_barrier(v.astype(jnp.bfloat16)).astype(jnp.float32)

@jax.custom_vjp
def low_back(v):
    return v

def low_keep(v):
    return (low(v), None)

def low_pass(kept, grad):
    return (grad,)

def back_keep(v):
    return (v, None)

def back_low(kept, grad):
    return (low(grad),)
low.defvjp(low_keep, low_pass)
low_back.defvjp(back_keep, back_low)
HIGH = lax.Precision.HIGHEST

def layer_norm(rows, gain, shift):
    mean = lax.optimization_barrier(jnp.mean(rows, axis=-1, keepdims=True))
    centred = rows - mean
    spread = lax.optimization_barrier(jnp.mean(centred * centred, axis=-1, keepdims=True))
    return centred * lax.rsqrt(spread + 1e-05) * gain + shift

def bucket_bias(line_q, line_k, width_q, width_k, height_q, height_k, line_table, width_table, height_table):
    line_reach = (line_table.shape[0] - 1) // 2
    box_reach = (width_table.shape[0] - 1) // 2
    line_idx = jnp.clip(line_q[:, None] - line_k[None, :], -line_reach, line_reach) + line_reach
    width_idx = jnp.clip(width_q[:, None] - width_k[None, :], -box_reach, box_reach) + box_reach
    height_idx = jnp.clip(height_q[:, None] - height_k[None, :], -box_reach, box_reach) + box_reach
    return jnp.take(line_table.T, line_idx, axis=1) + jnp.take(width_table.T, width_idx, axis=1) + jnp.take(height_table.T, height_idx, axis=1)

def page_forward(params, rows, key_valid, line_pos, width_pos, height_pos):
    query_weight, query_bias, key_weight, value_weight, value_bias, output_weight, output_bias, norm_gain, norm_shift, up_weight, up_bias, down_weight, down_bias, final_gain, final_shift, line_table, width_table, height_table = params
    seq, dim = rows.shape
    head = dim // HEADS
    query = low_back(low(jnp.dot(rows, query_weight, precision=HIGH) + query_bias))
    keys = low_back(low(jnp.dot(rows, key_weight, precision=HIGH)))
    values = low_back(low(jnp.dot(rows, value_weight, precision=HIGH) + value_bias))
    query = query.reshape(seq, HEADS, head)
    keys = keys.reshape(seq, HEADS, head)
    values = values.reshape(seq, HEADS, head)
    bias = bucket_bias(line_pos, line_pos, width_pos, width_pos, height_pos, height_pos, line_table, width_table, height_table)
    raw = jnp.einsum('qhd,khd->hqk', query, keys, precision=HIGH) * head ** (-0.5) + bias
    scores = low_back(jnp.where(key_valid[None, None, :], raw, -1e+30))
    probs = low(jax.nn.softmax(scores, axis=-1))
    context = jnp.einsum('hqk,khd->qhd', probs, values, precision=HIGH).reshape(seq, dim)
    context = low_back(low(context))
    attn = low_back(jnp.dot(context, output_weight, precision=HIGH) + output_bias)
    normed = layer_norm(rows + attn, norm_gain, norm_shift)
    pre = low_back(jnp.dot(low(normed), up_weight, precision=HIGH) + up_bias)
    act = low(jax.nn.gelu(pre, approximate=False))
    branch = low_back(jnp.dot(act, down_weight, precision=HIGH) + down_bias)
    return layer_norm(normed + branch, final_gain, final_shift)

def reference(text_in, patch_in, res_class, text_len, pos_line, pos_x, pos_y, query_weight, query_bias, key_weight, value_weight, value_bias, output_weight, output_bias, norm_gain, norm_shift, up_weight, up_bias, down_weight, down_bias, final_gain, final_shift, line_table, width_table, height_table, cot_text, cot_patch):
    pages_a, pages_b, text_rows, dim = text_in.shape
    patch_rows = patch_in.shape[2]
    count = pages_a * pages_b
    seq = text_rows + patch_rows
    rows = jnp.concatenate([text_in, patch_in], axis=2).astype(jnp.float32).reshape(count, seq, dim)
    cot = jnp.concatenate([cot_text, cot_patch], axis=2).astype(jnp.float32).reshape(count, seq, dim)
    live_patch = jnp.where(res_class == 1, patch_rows, SMALL_PATCH).reshape(count)
    text_live = jnp.arange(text_rows, dtype=jnp.int32)[None, :] < text_len.reshape(count)[:, None]
    patch_live = jnp.arange(patch_rows, dtype=jnp.int32)[None, :] < live_patch[:, None]
    key_valid = jnp.concatenate([text_live, patch_live], axis=1)
    params = tuple((p.astype(jnp.float32) for p in (query_weight, query_bias, key_weight, value_weight, value_bias, output_weight, output_bias, norm_gain, norm_shift, up_weight, up_bias, down_weight, down_bias, final_gain, final_shift, line_table, width_table, height_table)))

    def step(carry, page):
        page_rows, page_cot, valid, line_pos, width_pos, height_pos = page

        def forward(prm, r):
            return page_forward(prm, r, valid, line_pos, width_pos, height_pos)
        out, back = jax.vjp(forward, params, page_rows)
        grad_params, grad_rows = back(page_cot)
        carry = jax.tree.map(lambda a, b: a + b, carry, grad_params)
        return (carry, (out.astype(jnp.bfloat16), grad_rows.astype(jnp.bfloat16)))
    start = jax.tree.map(jnp.zeros_like, params)
    pages = (rows, cot, key_valid, pos_line.reshape(count, seq), pos_x.reshape(count, seq), pos_y.reshape(count, seq))
    grads, (outs, row_grads) = lax.scan(step, start, pages)
    outs = outs.reshape(pages_a, pages_b, seq, dim)
    row_grads = row_grads.reshape(pages_a, pages_b, seq, dim)
    return (outs[:, :, :text_rows], outs[:, :, text_rows:], row_grads[:, :, :text_rows], row_grads[:, :, text_rows:], grads[0], grads[1], grads[2], grads[3], grads[4], grads[5], grads[6], grads[7], grads[8], grads[9], grads[10], grads[11], grads[12], grads[13], grads[14], grads[15], grads[16], grads[17])
```

```python
from functools import partial

import jax
import jax.numpy as jnp
from jax import lax
from jax.experimental import pallas as pl
from jax.experimental.pallas import tpu as pltpu
from jax.sharding import PartitionSpec as P

HEADS = 12
TEXT = 512
PATCH = 576
SMALL_PATCH = 196
BF = jnp.bfloat16
F32 = jnp.float32
VMEM_BYTES = 60 * 2**20


def mm(left, right):
    return lax.dot_general(left, right, (((1,), (0,)), ((), ())), preferred_element_type=F32)


def inner(left, right):
    return lax.dot_general(left, right, (((0,), (0,)), ((), ())), preferred_element_type=F32)


def against(left, right):
    return lax.dot_general(left, right, (((1,), (1,)), ((), ())), preferred_element_type=F32)


def layer_norm(rows, gain, shift):
    mean = jnp.mean(rows, axis=-1, keepdims=True)
    centred = rows - mean
    spread = jnp.mean(centred * centred, axis=-1, keepdims=True)
    return centred * lax.rsqrt(spread + 1e-05) * gain + shift


def attend_kernel(
    k_ref, qt_ref, vt_ref, hot_ref, mask_ref, hott_ref, line_ref, width_ref, height_ref,
    exp_ref, ctx_ref, inv_ref, keys, queries, values,
):
    seq = k_ref.shape[0]
    lanes = qt_ref.shape[1]

    @pl.when(pl.program_id(0) == 0)
    def _():
        keys[:, 0:320] = hot_ref[0:seq, :]
        keys[:, 320:640] = hot_ref[0:seq, :]
        values[64:80, :] = jnp.ones((16, seq), BF)

    lane = lax.broadcasted_iota(jnp.int32, (seq, 128), 1)
    for h in range(2):
        mine = (lane < 64) if h == 0 else (lane >= 64)
        own, other = (640, 704) if h == 0 else (704, 640)
        keys[:, 640:768] = jnp.where(
            mine, k_ref[...].astype(F32), mask_ref[...].astype(F32)
        ).astype(BF)
        queries[own : own + 64, :] = qt_ref[h * 64 : h * 64 + 64, :]
        queries[other : other + 64, :] = jnp.ones((64, lanes), BF)
        values[0:64, :] = vt_ref[h * 64 : h * 64 + 64, :]
        near = mm(line_ref[h], hott_ref[0:64, :]).astype(BF)
        queries[0:64, :] = near[0:64]
        queries[320:384, :] = near[64:128]
        near = mm(width_ref[h], hott_ref[64:192, :]).astype(BF)
        queries[64:192, :] = near[0:128]
        queries[384:512, :] = near[128:256]
        near = mm(height_ref[h], hott_ref[192:320, :]).astype(BF)
        queries[192:320, :] = near[0:128]
        queries[512:640, :] = near[128:256]
        scores = mm(keys[...], queries[...])
        peak = jnp.max(scores, axis=0, keepdims=True)
        weights = jnp.exp(scores - peak).astype(BF)
        exp_ref[h] = weights
        ctx = mm(values[...], weights)
        inverse = 1.0 / ctx[64:65]
        inv_ref[h] = inverse
        ctx_ref[h * 64 : h * 64 + 64, :] = (ctx[0:64] * inverse).astype(BF)


def attend(k, q_t, v_t, hot, mask, hot_t, line, width, height):
    seq = k.shape[0]
    dim, lanes = q_t.shape

    def whole(a):
        return pl.BlockSpec(a.shape, lambda p: (0,) * a.ndim)

    def pair(a):
        return pl.BlockSpec((2,) + a.shape[1:], lambda p: (p, 0, 0))

    return pl.pallas_call(
        attend_kernel,
        grid=(HEADS // 2,),
        in_specs=[
            pl.BlockSpec((seq, 128), lambda p: (0, p)),
            pl.BlockSpec((128, lanes), lambda p: (p, 0)),
            pl.BlockSpec((128, seq), lambda p: (p, 0)),
            whole(hot),
            whole(mask),
            whole(hot_t),
            pair(line),
            pair(width),
            pair(height),
        ],
        out_specs=[
            pl.BlockSpec((2, seq, lanes), lambda p: (p, 0, 0)),
            pl.BlockSpec((128, lanes), lambda p: (p, 0)),
            pl.BlockSpec((2, 1, lanes), lambda p: (p, 0, 0)),
        ],
        out_shape=[
            jax.ShapeDtypeStruct((HEADS, seq, lanes), BF),
            jax.ShapeDtypeStruct((dim, lanes), BF),
            jax.ShapeDtypeStruct((HEADS, 1, lanes), F32),
        ],
        scratch_shapes=[
            pltpu.VMEM((seq, 768), BF),
            pltpu.VMEM((768, lanes), BF),
            pltpu.VMEM((80, seq), BF),
        ],
        compiler_params=pltpu.CompilerParams(vmem_limit_bytes=VMEM_BYTES),
    )(k, q_t, v_t, hot, mask, hot_t, line, width, height)


def attend_back_kernel(
    exp_ref, ctx_ref, v_ref, kt_ref, q_ref, dc_ref, dct_ref, hot_ref, hott_ref,
    dqt_ref, dk_ref, dv_ref, gwidth_ref, gheight_ref, gline_ref, values, dctx, lefts, rights, ds,
):
    seq = v_ref.shape[0]
    lanes = dct_ref.shape[1]

    @pl.when(pl.program_id(0) == 0)
    def _():
        for h in range(2):
            lefts[h, 64:192, :] = hott_ref[64:192, 0:seq]
            rights[h, :, 128:256] = hot_ref[:, 192:320]

    lane = lax.broadcasted_iota(jnp.int32, (seq, 128), 1)
    query_lane = lax.broadcasted_iota(jnp.int32, (lanes, 128), 1)
    row = lax.broadcasted_iota(jnp.int32, (64, lanes), 0)
    line_hot = jnp.concatenate([hot_ref[:, 0:64], hot_ref[:, 0:64]], axis=1).astype(F32)
    results = []
    for h in range(2):
        mine = (lane < 64) if h == 0 else (lane >= 64)
        query_mine = (query_lane < 64) if h == 0 else (query_lane >= 64)
        own, other = (0, 64) if h == 0 else (64, 0)
        part = slice(h * 64, h * 64 + 64)
        values[h] = jnp.where(mine, v_ref[...].astype(F32), 1.0).astype(BF)
        d_rows = dct_ref[part, :]
        delta = -jnp.sum(
            d_rows.astype(F32) * ctx_ref[part, :].astype(F32), axis=0, keepdims=True
        )
        high = delta.astype(BF).astype(F32)
        extra = jnp.where(row == 0, high, jnp.where(row == 1, delta - high, 0.0))
        dctx[h, own : own + 64, :] = d_rows
        dctx[h, other : other + 64, :] = extra.astype(BF)
        lefts[h, 0:64, :] = kt_ref[part, :]
        rights[h, :, 0:128] = jnp.where(query_mine, q_ref[...].astype(F32), line_hot).astype(BF)
        d_scores = mm(values[h], dctx[h])
        ds[h] = (exp_ref[h].astype(F32) * d_scores).astype(BF)
        by_query = mm(lefts[h], ds[h])
        dqt_ref[part, :] = (by_query[0:64] * 0.125).astype(BF)
        gwidth_ref[h] = mm(by_query[64:192].astype(BF), hot_ref[:, 64:192])
        by_key = mm(ds[h], rights[h])
        near = mm(hott_ref[0:64, 0:seq], by_key[:, 0:128].astype(BF))
        gline_ref[h] = near[:, 64:128] if h == 0 else near[:, 0:64]
        gheight_ref[h] = mm(hott_ref[192:320, 0:seq], by_key[:, 128:256].astype(BF))
        results.append((by_key[:, 0:128], mm(exp_ref[h], dc_ref[...])))
    dk_ref[...] = jnp.where(lane < 64, results[0][0], results[1][0]).astype(BF)
    dv_ref[...] = jnp.where(lane < 64, results[0][1], results[1][1]).astype(BF)


def attend_back(exps, ctx_t, v, k_t, q, d_ctx, d_ctx_t, hot, hot_t):
    seq, dim = v.shape
    lanes = d_ctx_t.shape[1]

    def whole(a):
        return pl.BlockSpec(a.shape, lambda p: (0,) * a.ndim)

    def columns(rows):
        return pl.BlockSpec((rows, 128), lambda p: (0, p))

    def rows(length):
        return pl.BlockSpec((128, length), lambda p: (p, 0))

    def pair(*shape):
        return pl.BlockSpec((2,) + shape, lambda p: (p, 0, 0))

    shape = jax.ShapeDtypeStruct
    return pl.pallas_call(
        attend_back_kernel,
        grid=(HEADS // 2,),
        in_specs=[
            pair(seq, lanes),
            rows(lanes),
            columns(seq),
            rows(seq),
            columns(lanes),
            columns(lanes),
            rows(lanes),
            whole(hot),
            whole(hot_t),
        ],
        out_specs=[
            rows(lanes),
            columns(seq),
            columns(seq),
            pair(128, 128),
            pair(128, 128),
            pair(64, 64),
        ],
        out_shape=[
            shape((dim, lanes), BF),
            shape((seq, dim), BF),
            shape((seq, dim), BF),
            shape((HEADS, 128, 128), F32),
            shape((HEADS, 128, 128), F32),
            shape((HEADS, 64, 64), F32),
        ],
        scratch_shapes=[
            pltpu.VMEM((2, seq, 128), BF),
            pltpu.VMEM((2, 128, lanes), BF),
            pltpu.VMEM((2, 192, seq), BF),
            pltpu.VMEM((2, lanes, 256), BF),
            pltpu.VMEM((2, seq, lanes), BF),
        ],
        compiler_params=pltpu.CompilerParams(vmem_limit_bytes=VMEM_BYTES),
    )(exps, ctx_t, v, k_t, q, d_ctx, d_ctx_t, hot, hot_t)


def bucket_select(table):
    reach = (table.shape[0] - 1) // 2
    spots = jnp.arange(4 * reach, dtype=jnp.int32)
    bucket = jnp.clip(spots[None, :] - spots[:, None], -reach, reach) + reach
    return bucket[None] == jnp.arange(2 * reach + 1, dtype=jnp.int32)[:, None, None]


def spread_table(table):
    span = 2 * (table.shape[0] - 1)
    high = table.astype(BF)
    low = (table - high.astype(F32)).astype(BF)
    both = jnp.stack([high, low], axis=2).reshape(table.shape[0], -1)
    spread = lax.dot_general(
        both,
        bucket_select(table).astype(BF).reshape(table.shape[0], -1),
        (((0,), (0,)), ((), ())),
        preferred_element_type=F32,
    )
    return spread.astype(BF).reshape(HEADS, 2 * span, span)


def gather_table(grads, table):
    select = bucket_select(table).astype(F32).reshape(table.shape[0], -1)
    return lax.dot_general(
        select,
        grads.reshape(HEADS, -1),
        (((1,), (1,)), ((), ())),
        precision=lax.Precision.HIGHEST,
        preferred_element_type=F32,
    )


def row_pass(rows_in, ctx_t, cot, inverse, weights):
    (
        output_weight,
        output_bias,
        norm_gain,
        norm_shift,
        up_weight,
        up_bias,
        down_weight,
        down_bias,
        final_gain,
        final_shift,
    ) = weights
    seq = rows_in.shape[0]
    lanes = inverse.shape[2]
    attn = inner(ctx_t, output_weight)[:seq] + output_bias
    mid = rows_in.astype(F32) + attn
    normed, norm_back = jax.vjp(layer_norm, mid, norm_gain, norm_shift)
    normed_low = normed.astype(BF)
    pre = mm(normed_low, up_weight) + up_bias
    act, gelu_back = jax.vjp(partial(jax.nn.gelu, approximate=False), pre)
    act_low = act.astype(BF)
    branch = mm(act_low, down_weight) + down_bias
    final, final_back = jax.vjp(layer_norm, normed + branch, final_gain, final_shift)
    final_low = final.astype(BF)
    d_sum, final_gain_grad, final_shift_grad = final_back(cot)
    d_branch = d_sum.astype(BF)
    down_weight_grad = inner(act_low, d_branch)
    down_bias_grad = jnp.sum(d_branch.astype(F32), axis=0)
    d_act = against(d_branch, down_weight)
    (d_pre,) = gelu_back(d_act)
    d_pre_low = d_pre.astype(BF)
    up_weight_grad = inner(normed_low, d_pre_low)
    up_bias_grad = jnp.sum(d_pre_low.astype(F32), axis=0)
    d_normed = d_sum + against(d_pre_low, up_weight)
    d_mid, norm_gain_grad, norm_shift_grad = norm_back(d_normed)
    d_attn = d_mid.astype(BF)
    output_weight_grad = mm(ctx_t[:, :seq], d_attn)
    output_bias_grad = jnp.sum(d_attn.astype(F32), axis=0)
    d_attn_long = jnp.pad(d_attn, ((0, lanes - seq), (0, 0)))
    d_ctx_t = against(output_weight, d_attn_long).reshape(HEADS, -1, lanes) * inverse
    d_ctx_t = d_ctx_t.astype(BF).reshape(-1, lanes)
    grads = (
        output_weight_grad,
        output_bias_grad,
        norm_gain_grad,
        norm_shift_grad,
        up_weight_grad,
        up_bias_grad,
        down_weight_grad,
        down_bias_grad,
        final_gain_grad,
        final_shift_grad,
    )
    return (final_low, d_mid, d_ctx_t, grads)


def text_home(rows):
    pages, _, part, dim = rows.shape
    moved = lax.all_to_all(
        rows.reshape(pages, part, dim), "wide", split_axis=0, concat_axis=0, tiled=True
    )
    return moved.reshape(-1, dim)


def patch_home(rows):
    _, pages, part, dim = rows.shape
    moved = lax.all_to_all(
        rows.reshape(pages, part, dim), "narrow", split_axis=0, concat_axis=0, tiled=True
    )
    return moved.reshape(-1, dim)


def text_away(rows, shape):
    pages, _, part, dim = shape
    moved = lax.all_to_all(
        rows.reshape(pages, part, dim), "wide", split_axis=0, concat_axis=0, tiled=True
    )
    return moved.reshape(shape)


def patch_away(rows, shape):
    _, pages, part, dim = shape
    moved = lax.all_to_all(
        rows.reshape(pages, part, dim), "narrow", split_axis=0, concat_axis=0, tiled=True
    )
    return moved.reshape(shape)


def body(
    text_in,
    patch_in,
    res_class,
    text_len,
    pos_line,
    pos_x,
    pos_y,
    query_weight,
    query_bias,
    key_weight,
    value_weight,
    value_bias,
    output_weight,
    output_bias,
    norm_gain,
    norm_shift,
    up_weight,
    up_bias,
    down_weight,
    down_bias,
    final_gain,
    final_shift,
    line_table,
    width_table,
    height_table,
    cot_text,
    cot_patch,
):
    text_shape = text_in.shape
    patch_shape = patch_in.shape
    dim = text_shape[3]
    seq = TEXT + PATCH
    lanes = -(-seq // 128) * 128
    weights = (
        output_weight,
        output_bias,
        norm_gain,
        norm_shift,
        up_weight,
        up_bias,
        down_weight,
        down_bias,
        final_gain,
        final_shift,
    )
    rows_in = jnp.concatenate([text_home(text_in), patch_home(patch_in)], axis=0)
    cot = jnp.concatenate([text_home(cot_text), patch_home(cot_patch)], axis=0).astype(F32)

    line = spread_table(line_table)
    width = spread_table(width_table)
    height = spread_table(height_table)
    hots = []
    hots_t = []
    for spots, table in ((pos_line, line_table), (pos_x, width_table), (pos_y, height_table)):
        span = jnp.arange(2 * (table.shape[0] - 1), dtype=jnp.int32)
        long = jnp.pad(spots.reshape(-1), (0, lanes - seq), constant_values=-1)
        hots.append((long[:, None] == span[None, :]).astype(BF))
        hots_t.append((long[None, :] == span[:, None]).astype(BF))
    hot = jnp.concatenate(hots, axis=1)
    hot_t = jnp.concatenate(hots_t, axis=0)
    index = jnp.arange(seq, dtype=jnp.int32)
    live_patch = jnp.where(res_class.reshape(()) == 1, PATCH, SMALL_PATCH)
    valid = jnp.where(index < TEXT, index < text_len.reshape(()), index - TEXT < live_patch)
    column = jnp.arange(128, dtype=jnp.int32)
    mask = jnp.where((column[None, :] % 64 == 0) & ~valid[:, None], -1e30, 0.0).astype(BF)

    rows_long = jnp.pad(rows_in, ((0, lanes - seq), (0, 0)))
    q = ((mm(rows_long, query_weight) + query_bias) * 0.125).astype(BF)
    q_t = (
        (lax.dot_general(query_weight, rows_long, (((0,), (1,)), ((), ())), preferred_element_type=F32)
         + query_bias[:, None]) * 0.125
    ).astype(BF)
    k = mm(rows_in, key_weight).astype(BF)
    k_t = k.T
    v = (mm(rows_in, value_weight) + value_bias).astype(BF)
    v_t = v.T
    exps, ctx_t, inverse = attend(k, q_t, v_t, hot, mask, hot_t, line, width, height)
    final_low, d_mid, d_ctx_t, row_grads = row_pass(rows_in, ctx_t, cot, inverse, weights)
    d_q_t, d_k, d_v, g_width, g_height, g_line = attend_back(
        exps, ctx_t, v, k_t, q, d_ctx_t.T, d_ctx_t, hot, hot_t
    )
    d_q = d_q_t[:, :seq].T
    line_table_grad = gather_table(g_line, line_table)
    width_table_grad = gather_table(g_width, width_table)
    height_table_grad = gather_table(g_height, height_table)
    query_weight_grad = inner(rows_in, d_q)
    key_weight_grad = inner(rows_in, d_k)
    value_weight_grad = inner(rows_in, d_v)
    query_bias_grad = jnp.sum(d_q.astype(F32), axis=0)
    value_bias_grad = jnp.sum(d_v.astype(F32), axis=0)
    d_rows = (
        d_mid + against(d_q, query_weight) + against(d_k, key_weight) + against(d_v, value_weight)
    ).astype(BF)
    text_out = text_away(final_low[:TEXT], text_shape)
    patch_out = patch_away(final_low[TEXT:], patch_shape)
    text_grad = text_away(d_rows[:TEXT], text_shape)
    patch_grad = patch_away(d_rows[TEXT:], patch_shape)
    (
        output_weight_grad,
        output_bias_grad,
        norm_gain_grad,
        norm_shift_grad,
        up_weight_grad,
        up_bias_grad,
        down_weight_grad,
        down_bias_grad,
        final_gain_grad,
        final_shift_grad,
    ) = row_grads
    both = ("wide", "narrow")

    def total(grad):
        return lax.psum(grad.astype(BF), both).astype(F32)

    down_weight_grad, up_weight_grad, output_weight_grad = (
        total(down_weight_grad), total(up_weight_grad), total(output_weight_grad)
    )
    query_weight_grad, key_weight_grad, value_weight_grad = (
        total(query_weight_grad), total(key_weight_grad), total(value_weight_grad)
    )
    (
        query_bias_grad,
        value_bias_grad,
        output_bias_grad,
        norm_gain_grad,
        norm_shift_grad,
        up_bias_grad,
        down_bias_grad,
        final_gain_grad,
        final_shift_grad,
        line_table_grad,
        width_table_grad,
        height_table_grad,
    ) = lax.psum(
        (
            query_bias_grad,
            value_bias_grad,
            output_bias_grad,
            norm_gain_grad,
            norm_shift_grad,
            up_bias_grad,
            down_bias_grad,
            final_gain_grad,
            final_shift_grad,
            line_table_grad,
            width_table_grad,
            height_table_grad,
        ),
        both,
    )
    return (
        text_out,
        patch_out,
        text_grad,
        patch_grad,
        query_weight_grad,
        query_bias_grad,
        key_weight_grad,
        value_weight_grad,
        value_bias_grad,
        output_weight_grad,
        output_bias_grad,
        norm_gain_grad,
        norm_shift_grad,
        up_weight_grad,
        up_bias_grad,
        down_weight_grad,
        down_bias_grad,
        final_gain_grad,
        final_shift_grad,
        line_table_grad,
        width_table_grad,
        height_table_grad,
    )


def solution(mesh):
    text = P(None, "narrow", "wide", None)
    patch = P("wide", None, "narrow", None)
    page = P("wide", "narrow")
    spots = P("wide", "narrow", None)
    in_specs = (text, patch, page, page, spots, spots, spots) + (P(),) * 18 + (text, patch)
    out_specs = (text, patch, text, patch) + (P(),) * 18
    return jax.shard_map(body, mesh=mesh, in_specs=in_specs, out_specs=out_specs, check_vma=False)
```

```python
from functools import partial

import jax
import jax.numpy as jnp
from jax import lax
from jax.experimental import pallas as pl
from jax.experimental.pallas import tpu as pltpu
from jax.sharding import PartitionSpec as P

HEADS = 12
TEXT = 512
PATCH = 576
SMALL_PATCH = 196
BF = jnp.bfloat16
F32 = jnp.float32
VMEM_BYTES = 60 * 2**20


def mm(left, right):
    return lax.dot_general(left, right, (((1,), (0,)), ((), ())), preferred_element_type=F32)


def inner(left, right):
    return lax.dot_general(left, right, (((0,), (0,)), ((), ())), preferred_element_type=F32)


def against(left, right):
    return lax.dot_general(left, right, (((1,), (1,)), ((), ())), preferred_element_type=F32)


def layer_norm(rows, gain, shift):
    mean = jnp.mean(rows, axis=-1, keepdims=True)
    centred = rows - mean
    spread = jnp.mean(centred * centred, axis=-1, keepdims=True)
    return centred * lax.rsqrt(spread + 1e-05) * gain + shift


def attend_kernel(
    k_ref, qt_ref, vt_ref, hot_ref, mask_ref, hott_ref, line_ref, width_ref, height_ref,
    exp_ref, ctx_ref, inv_ref, keys, queries, values,
):
    seq = k_ref.shape[0]
    lanes = qt_ref.shape[1]

    @pl.when(pl.program_id(0) == 0)
    def _():
        keys[:, 0:320] = hot_ref[0:seq, :]
        keys[:, 320:640] = hot_ref[0:seq, :]
        values[64:80, :] = jnp.ones((16, seq), BF)

    lane = lax.broadcasted_iota(jnp.int32, (seq, 128), 1)
    for h in range(2):
        mine = (lane < 64) if h == 0 else (lane >= 64)
        own, other = (640, 704) if h == 0 else (704, 640)
        keys[:, 640:768] = jnp.where(
            mine, k_ref[...].astype(F32), mask_ref[...].astype(F32)
        ).astype(BF)
        queries[own : own + 64, :] = qt_ref[h * 64 : h * 64 + 64, :]
        queries[other : other + 64, :] = jnp.ones((64, lanes), BF)
        values[0:64, :] = vt_ref[h * 64 : h * 64 + 64, :]
        near = mm(line_ref[h], hott_ref[0:64, :]).astype(BF)
        queries[0:64, :] = near[0:64]
        queries[320:384, :] = near[64:128]
        near = mm(width_ref[h], hott_ref[64:192, :]).astype(BF)
        queries[64:192, :] = near[0:128]
        queries[384:512, :] = near[128:256]
        near = mm(height_ref[h], hott_ref[192:320, :]).astype(BF)
        queries[192:320, :] = near[0:128]
        queries[512:640, :] = near[128:256]
        scores = mm(keys[...], queries[...])
        peak = jnp.max(scores, axis=0, keepdims=True)
        weights = jnp.exp(scores - peak).astype(BF)
        exp_ref[h] = weights
        ctx = mm(values[...], weights)
        inverse = 1.0 / ctx[64:65]
        inv_ref[h] = inverse
        ctx_ref[h * 64 : h * 64 + 64, :] = (ctx[0:64] * inverse).astype(BF)


def attend(k, q_t, v_t, hot, mask, hot_t, line, width, height):
    seq = k.shape[0]
    dim, lanes = q_t.shape

    def whole(a):
        return pl.BlockSpec(a.shape, lambda p: (0,) * a.ndim)

    def pair(a):
        return pl.BlockSpec((2,) + a.shape[1:], lambda p: (p, 0, 0))

    return pl.pallas_call(
        attend_kernel,
        grid=(HEADS // 2,),
        in_specs=[
            pl.BlockSpec((seq, 128), lambda p: (0, p)),
            pl.BlockSpec((128, lanes), lambda p: (p, 0)),
            pl.BlockSpec((128, seq), lambda p: (p, 0)),
            whole(hot),
            whole(mask),
            whole(hot_t),
            pair(line),
            pair(width),
            pair(height),
        ],
        out_specs=[
            pl.BlockSpec((2, seq, lanes), lambda p: (p, 0, 0)),
            pl.BlockSpec((128, lanes), lambda p: (p, 0)),
            pl.BlockSpec((2, 1, lanes), lambda p: (p, 0, 0)),
        ],
        out_shape=[
            jax.ShapeDtypeStruct((HEADS, seq, lanes), BF),
            jax.ShapeDtypeStruct((dim, lanes), BF),
            jax.ShapeDtypeStruct((HEADS, 1, lanes), F32),
        ],
        scratch_shapes=[
            pltpu.VMEM((seq, 768), BF),
            pltpu.VMEM((768, lanes), BF),
            pltpu.VMEM((80, seq), BF),
        ],
        compiler_params=pltpu.CompilerParams(vmem_limit_bytes=VMEM_BYTES),
        cost_estimate=pl.CostEstimate(
            flops=HEADS * seq * lanes * 4096, bytes_accessed=HEADS * seq * lanes * 2,
            transcendentals=HEADS * seq * lanes,
        ),
    )(k, q_t, v_t, hot, mask, hot_t, line, width, height)


def attend_back_kernel(held, *refs):
    (
        exp_ref, ctx_ref, v_ref, kt_ref, q_ref, dc_ref, dct_ref, hot_ref, hott_ref,
        dqt_ref, dk_ref, dv_ref, gwidth_ref, gheight_ref, gline_ref, values, dctx, lefts, rights, ds,
    ) = refs[:9] + refs[9 + held :]
    seq = v_ref.shape[0]
    lanes = dct_ref.shape[1]

    @pl.when(pl.program_id(0) == 0)
    def _():
        for h in range(2):
            lefts[h, 64:192, :] = hott_ref[64:192, 0:seq]
            rights[h, :, 128:256] = hot_ref[:, 192:320]

    lane = lax.broadcasted_iota(jnp.int32, (seq, 128), 1)
    query_lane = lax.broadcasted_iota(jnp.int32, (lanes, 128), 1)
    row = lax.broadcasted_iota(jnp.int32, (64, lanes), 0)
    line_hot = jnp.concatenate([hot_ref[:, 0:64], hot_ref[:, 0:64]], axis=1).astype(F32)
    results = []
    for h in range(2):
        mine = (lane < 64) if h == 0 else (lane >= 64)
        query_mine = (query_lane < 64) if h == 0 else (query_lane >= 64)
        own, other = (0, 64) if h == 0 else (64, 0)
        part = slice(h * 64, h * 64 + 64)
        values[h] = jnp.where(mine, v_ref[...].astype(F32), 1.0).astype(BF)
        d_rows = dct_ref[part, :]
        delta = -jnp.sum(
            d_rows.astype(F32) * ctx_ref[part, :].astype(F32), axis=0, keepdims=True
        )
        high = delta.astype(BF).astype(F32)
        extra = jnp.where(row == 0, high, jnp.where(row == 1, delta - high, 0.0))
        dctx[h, own : own + 64, :] = d_rows
        dctx[h, other : other + 64, :] = extra.astype(BF)
        lefts[h, 0:64, :] = kt_ref[part, :]
        rights[h, :, 0:128] = jnp.where(query_mine, q_ref[...].astype(F32), line_hot).astype(BF)
        d_scores = mm(values[h], dctx[h])
        ds[h] = (exp_ref[h].astype(F32) * d_scores).astype(BF)
        by_query = mm(lefts[h], ds[h])
        dqt_ref[part, :] = (by_query[0:64] * 0.125).astype(BF)
        gwidth_ref[h] = mm(by_query[64:192].astype(BF), hot_ref[:, 64:192])
        by_key = mm(ds[h], rights[h])
        near = mm(hott_ref[0:64, 0:seq], by_key[:, 0:128].astype(BF))
        gline_ref[h] = near[:, 64:128] if h == 0 else near[:, 0:64]
        gheight_ref[h] = mm(hott_ref[192:320, 0:seq], by_key[:, 128:256].astype(BF))
        results.append((by_key[:, 0:128], mm(exp_ref[h], dc_ref[...])))
    dk_ref[...] = jnp.where(lane < 64, results[0][0], results[1][0]).astype(BF)
    dv_ref[...] = jnp.where(lane < 64, results[0][1], results[1][1]).astype(BF)


def attend_back(first, pairs, held, exps, ctx_t, v, k_t, q, d_ctx, d_ctx_t, hot, hot_t):
    seq, dim = v.shape
    lanes = d_ctx_t.shape[1]

    def whole(a):
        return pl.BlockSpec(a.shape, lambda p: (0,) * a.ndim)

    def columns(rows, start=first):
        return pl.BlockSpec((rows, 128), lambda p: (0, p + start))

    def rows(length, start=first):
        return pl.BlockSpec((128, length), lambda p: (p + start, 0))

    def pair(*shape, start=first):
        return pl.BlockSpec((2,) + shape, lambda p: (p + start, 0, 0))

    shape = jax.ShapeDtypeStruct
    return pl.pallas_call(
        partial(attend_back_kernel, len(held)),
        grid=(pairs,),
        in_specs=[
            pair(seq, lanes),
            rows(lanes),
            columns(seq),
            rows(seq),
            columns(lanes),
            columns(lanes),
            rows(lanes),
            whole(hot),
            whole(hot_t),
        ]
        + [pl.BlockSpec(memory_space=pl.ANY)] * len(held),
        out_specs=[
            rows(lanes, 0),
            columns(seq, 0),
            columns(seq, 0),
            pair(128, 128, start=0),
            pair(128, 128, start=0),
            pair(64, 64, start=0),
        ],
        out_shape=[
            shape((128 * pairs, lanes), BF),
            shape((seq, 128 * pairs), BF),
            shape((seq, 128 * pairs), BF),
            shape((2 * pairs, 128, 128), F32),
            shape((2 * pairs, 128, 128), F32),
            shape((2 * pairs, 64, 64), F32),
        ],
        scratch_shapes=[
            pltpu.VMEM((2, seq, 128), BF),
            pltpu.VMEM((2, 128, lanes), BF),
            pltpu.VMEM((2, 192, seq), BF),
            pltpu.VMEM((2, lanes, 256), BF),
            pltpu.VMEM((2, seq, lanes), BF),
        ],
        compiler_params=pltpu.CompilerParams(vmem_limit_bytes=VMEM_BYTES),
        cost_estimate=pl.CostEstimate(
            flops=2 * pairs * seq * lanes * 4096, bytes_accessed=2 * pairs * seq * lanes * 2,
            transcendentals=0,
        ),
    )(exps, ctx_t, v, k_t, q, d_ctx, d_ctx_t, hot, hot_t, *held)


def bucket_select(table):
    reach = (table.shape[0] - 1) // 2
    spots = jnp.arange(4 * reach, dtype=jnp.int32)
    bucket = jnp.clip(spots[None, :] - spots[:, None], -reach, reach) + reach
    return bucket[None] == jnp.arange(2 * reach + 1, dtype=jnp.int32)[:, None, None]


def spread_table(table):
    span = 2 * (table.shape[0] - 1)
    high = table.astype(BF)
    low = (table - high.astype(F32)).astype(BF)
    both = jnp.stack([high, low], axis=2).reshape(table.shape[0], -1)
    spread = lax.dot_general(
        both,
        bucket_select(table).astype(BF).reshape(table.shape[0], -1),
        (((0,), (0,)), ((), ())),
        preferred_element_type=F32,
    )
    return spread.astype(BF).reshape(HEADS, 2 * span, span)


def gather_table(grads, table):
    select = bucket_select(table).astype(F32).reshape(table.shape[0], -1)
    return lax.dot_general(
        select,
        grads.reshape(HEADS, -1),
        (((1,), (1,)), ((), ())),
        precision=lax.Precision.HIGHEST,
        preferred_element_type=F32,
    )


def row_pass(rows_in, ctx_t, cot, inverse, weights):
    (
        output_weight,
        output_bias,
        norm_gain,
        norm_shift,
        up_weight,
        up_bias,
        down_weight,
        down_bias,
        final_gain,
        final_shift,
    ) = weights
    seq = rows_in.shape[0]
    lanes = inverse.shape[2]
    attn = inner(ctx_t, output_weight)[:seq] + output_bias
    mid = rows_in.astype(F32) + attn
    normed, norm_back = jax.vjp(layer_norm, mid, norm_gain, norm_shift)
    normed_low = normed.astype(BF)
    pre = mm(normed_low, up_weight) + up_bias
    act, gelu_back = jax.vjp(partial(jax.nn.gelu, approximate=False), pre)
    act_low = act.astype(BF)
    branch = mm(act_low, down_weight) + down_bias
    final, final_back = jax.vjp(layer_norm, normed + branch, final_gain, final_shift)
    final_low = final.astype(BF)
    d_sum, final_gain_grad, final_shift_grad = final_back(cot)
    d_branch = d_sum.astype(BF)
    down_weight_grad = inner(act_low, d_branch)
    down_bias_grad = jnp.sum(d_branch.astype(F32), axis=0)
    d_act = against(d_branch, down_weight)
    (d_pre,) = gelu_back(d_act)
    d_pre_low = d_pre.astype(BF)
    up_weight_grad = inner(normed_low, d_pre_low)
    up_bias_grad = jnp.sum(d_pre_low.astype(F32), axis=0)
    d_normed = d_sum + against(d_pre_low, up_weight)
    d_mid, norm_gain_grad, norm_shift_grad = norm_back(d_normed)
    d_attn = d_mid.astype(BF)
    output_weight_grad = mm(ctx_t[:, :seq], d_attn)
    output_bias_grad = jnp.sum(d_attn.astype(F32), axis=0)
    d_attn_long = jnp.pad(d_attn, ((0, lanes - seq), (0, 0)))
    d_ctx_t = against(output_weight, d_attn_long).reshape(HEADS, -1, lanes) * inverse
    d_ctx_t = d_ctx_t.astype(BF).reshape(-1, lanes)
    grads = (
        output_weight_grad,
        output_bias_grad,
        norm_gain_grad,
        norm_shift_grad,
        up_weight_grad,
        up_bias_grad,
        down_weight_grad,
        down_bias_grad,
        final_gain_grad,
        final_shift_grad,
    )
    return (final_low, d_mid, d_ctx_t, grads)


def shift_pairs(size, step):
    return [(i, (i + step) % size) for i in range(size)]


def flip_pairs(size, step):
    return [(i, i ^ step) for i in range(size)]


def pick(array, index):
    return lax.dynamic_index_in_dim(array, index, 0, keepdims=False)


def swap_text(parts):
    return lax.all_to_all(parts, "wide", split_axis=0, concat_axis=0, tiled=True)


def patch_order(size):
    me = lax.axis_index("narrow")
    return [me ^ k for k in range(size)]


def swap_patch(parts):
    size = parts.shape[0]
    me = lax.axis_index("narrow")
    return [pick(parts, me)] + [
        lax.ppermute(pick(parts, me ^ k), "narrow", flip_pairs(size, k)) for k in range(1, size)
    ]


def flip_axis(array, axis, bit):
    return jnp.where(bit == 1, jnp.flip(array, axis), array)


def from_flipped(parts, me):
    size = parts.shape[0]
    bits = size.bit_length() - 1
    parts = parts.reshape((2,) * bits + parts.shape[1:])
    for b in range(bits):
        parts = flip_axis(parts, bits - 1 - b, (me >> b) & 1)
    return parts.reshape((size,) + parts.shape[bits:])


def patch_away(rows, size):
    me = lax.axis_index("narrow")
    parts = rows.reshape(size, -1, rows.shape[1])
    arrived = [parts[0]] + [
        lax.ppermute(parts[k], "narrow", flip_pairs(size, k)) for k in range(1, size)
    ]
    return from_flipped(jnp.stack(arrived), me)


def add(*terms):
    total = terms[0].astype(F32)
    for term in terms[1:]:
        total = total + term.astype(F32)
    return total.astype(BF)


def stages(wide, order):
    bits = list(range(1, wide.bit_length() - 1))
    return [0] + bits[:: 1 if order == 0 else -1] + [None]


def scatter_step(grad, wide, narrow, bit):
    columns = grad.shape[1]
    if bit is None:
        me = lax.axis_index("narrow")
        return add(*swap_patch(grad.reshape(narrow, -1, columns)))
    me = (lax.axis_index("wide") >> bit) & 1
    parts = grad.reshape(2, -1, columns)
    arrived = lax.ppermute(pick(parts, 1 - me), "wide", flip_pairs(wide, 1 << bit))
    return add(pick(parts, me), arrived)


def scatter_sum(grad, wide, narrow, order):
    steps = []
    for bit in stages(wide, order):
        grad = scatter_step(grad, wide, narrow, bit)
        steps.append(grad)
    return steps


def gather_all(part, wide, narrow, order):
    rows, columns = part.shape
    order = stages(wide, order)
    part = part[None]
    for bit in order[::-1]:
        if bit is None:
            parts = [part] + [
                lax.ppermute(part, "narrow", flip_pairs(narrow, k)) for k in range(1, narrow)
            ]
        else:
            parts = [part, lax.ppermute(part, "wide", flip_pairs(wide, 1 << bit))]
        part = jnp.concatenate(parts, axis=0)
    bits = []
    for bit in order:
        if bit is None:
            me = lax.axis_index("narrow")
            bits += [(me >> b) & 1 for b in range(narrow.bit_length() - 2, -1, -1)]
        else:
            bits.append((lax.axis_index("wide") >> bit) & 1)
    part = part.reshape((2,) * len(bits) + (rows, columns))
    for axis, bit in enumerate(bits):
        part = flip_axis(part, axis, bit)
    return part.reshape(-1, columns)


def pack(grads, columns, rows):
    lines = []
    for grad in grads:
        flat = grad.reshape(-1)
        lines.append(jnp.pad(flat, (0, -flat.shape[0] % columns)).reshape(-1, columns))
    lines = jnp.concatenate(lines, axis=0)
    return jnp.pad(lines, ((0, -lines.shape[0] % rows), (0, 0)))


def unpack(lines, grads):
    columns = lines.shape[1]
    at = 0
    out = []
    for grad in grads:
        count = -(-grad.size // columns)
        out.append(lines[at : at + count].reshape(-1)[: grad.size].reshape(grad.shape))
        at += count
    return out


def body(
    text_in,
    patch_in,
    res_class,
    text_len,
    pos_line,
    pos_x,
    pos_y,
    query_weight,
    query_bias,
    key_weight,
    value_weight,
    value_bias,
    output_weight,
    output_bias,
    norm_gain,
    norm_shift,
    up_weight,
    up_bias,
    down_weight,
    down_bias,
    final_gain,
    final_shift,
    line_table,
    width_table,
    height_table,
    cot_text,
    cot_patch,
):
    text_shape = text_in.shape
    patch_shape = patch_in.shape
    dim = text_shape[3]
    seq = TEXT + PATCH
    lanes = -(-seq // 128) * 128
    weights = (
        output_weight,
        output_bias,
        norm_gain,
        norm_shift,
        up_weight,
        up_bias,
        down_weight,
        down_bias,
        final_gain,
        final_shift,
    )
    wide = text_shape[0]
    narrow = patch_shape[1]
    rows_in = jnp.concatenate(
        [swap_text(text_in.reshape(wide, -1, dim)).reshape(-1, dim)]
        + swap_patch(patch_in.reshape(narrow, -1, dim)),
        axis=0,
    )
    cot = [swap_text(cot_text.reshape(wide, -1, dim)).reshape(-1, dim)] + swap_patch(
        cot_patch.reshape(narrow, -1, dim)
    )
    index = jnp.arange(seq, dtype=jnp.int32)
    live_patch = jnp.where(res_class.reshape(()) == 1, PATCH, SMALL_PATCH)
    valid = jnp.where(index < TEXT, index < text_len.reshape(()), index - TEXT < live_patch)
    facts = jnp.concatenate(
        [pos_line.reshape(1, -1), pos_x.reshape(1, -1), pos_y.reshape(1, -1), valid.astype(jnp.int32)[None]]
    )
    patch_facts = facts[:, TEXT:].reshape(4, narrow, -1)
    facts = jnp.concatenate(
        [facts[:, :TEXT]]
        + [
            lax.dynamic_index_in_dim(patch_facts, i, 1, keepdims=False)
            for i in patch_order(narrow)
        ],
        axis=1,
    )
    line_spots, x_spots, y_spots = facts[0], facts[1], facts[2]
    valid = facts[3] == 1

    line = spread_table(line_table)
    width = spread_table(width_table)
    height = spread_table(height_table)
    hots = []
    hots_t = []
    for spots, table in ((line_spots, line_table), (x_spots, width_table), (y_spots, height_table)):
        span = jnp.arange(2 * (table.shape[0] - 1), dtype=jnp.int32)
        long = jnp.pad(spots, (0, lanes - seq), constant_values=-1)
        hots.append((long[:, None] == span[None, :]).astype(BF))
        hots_t.append((long[None, :] == span[:, None]).astype(BF))
    hot = jnp.concatenate(hots, axis=1)
    hot_t = jnp.concatenate(hots_t, axis=0)
    column = jnp.arange(128, dtype=jnp.int32)
    mask = jnp.where((column[None, :] % 64 == 0) & ~valid[:, None], -1e30, 0.0).astype(BF)

    rows_long = jnp.pad(rows_in, ((0, lanes - seq), (0, 0)))
    q = ((mm(rows_long, query_weight) + query_bias) * 0.125).astype(BF)
    q_t = (
        (lax.dot_general(query_weight, rows_long, (((0,), (1,)), ((), ())), preferred_element_type=F32)
         + query_bias[:, None]) * 0.125
    ).astype(BF)
    k = mm(rows_in, key_weight).astype(BF)
    k_t = k.T
    v = (mm(rows_in, value_weight) + value_bias).astype(BF)
    v_t = v.T
    exps, ctx_t, inverse = attend(k, q_t, v_t, hot, mask, hot_t, line, width, height)
    ctx_t, cot = lax.optimization_barrier((ctx_t, cot))
    cot = jnp.concatenate(cot, axis=0).astype(F32)
    final_low, d_mid, d_ctx_t, row_grads = row_pass(rows_in, ctx_t, cot, inverse, weights)
    (
        output_weight_grad,
        output_bias_grad,
        norm_gain_grad,
        norm_shift_grad,
        up_weight_grad,
        up_bias_grad,
        down_weight_grad,
        down_bias_grad,
        final_gain_grad,
        final_shift_grad,
    ) = row_grads
    early = (
        output_bias_grad, norm_gain_grad, norm_shift_grad, up_bias_grad, down_bias_grad,
        final_gain_grad, final_shift_grad,
    )
    sums = lax.psum(
        (
            down_weight_grad.astype(BF),
            up_weight_grad.astype(BF),
            jnp.concatenate([output_weight_grad, pack(early, dim, 16)], axis=0).astype(BF),
        ),
        ("wide", "narrow"),
    )
    down_weight_grad, up_weight_grad, output_weight_grad = (a.astype(F32) for a in sums)
    (
        output_bias_grad,
        norm_gain_grad,
        norm_shift_grad,
        up_bias_grad,
        down_bias_grad,
        final_gain_grad,
        final_shift_grad,
    ) = unpack(output_weight_grad[dim:], early)
    output_weight_grad = output_weight_grad[:dim]
    def backward():
        text_out = swap_text(final_low[:TEXT].reshape(wide, -1, dim)).reshape(text_shape)
        patch_out = patch_away(final_low[TEXT:], narrow).reshape(patch_shape)
        pairs = HEADS // 4
        held = [[], [text_out, patch_out]]
        d_ctx = d_ctx_t.T
        backs = [
            attend_back(i * pairs, pairs, held[i], exps, ctx_t, v, k_t, q, d_ctx, d_ctx_t, hot, hot_t)
            for i in range(2)
        ]
        d_q = jnp.concatenate([b[0] for b in backs], axis=0)[:, :seq].T
        d_k = jnp.concatenate([b[1] for b in backs], axis=1)
        d_v = jnp.concatenate([b[2] for b in backs], axis=1)
        g_width = jnp.concatenate([b[3] for b in backs], axis=0)
        g_height = jnp.concatenate([b[4] for b in backs], axis=0)
        g_line = jnp.concatenate([b[5] for b in backs], axis=0)
        d_rows = (
            d_mid + against(d_q, query_weight) + against(d_k, key_weight) + against(d_v, value_weight)
        ).astype(BF)
        text_grad = swap_text(d_rows[:TEXT].reshape(wide, -1, dim)).reshape(text_shape)
        patch_grad = patch_away(d_rows[TEXT:], narrow).reshape(patch_shape)
        late = (
            jnp.sum(d_q.astype(F32), axis=0),
            jnp.sum(d_v.astype(F32), axis=0),
            gather_table(g_line, line_table),
            gather_table(g_width, width_table),
            gather_table(g_height, height_table),
        )
        tail = jnp.concatenate(
            [
                inner(rows_in, d_q),
                inner(rows_in, d_k),
                inner(rows_in, d_v),
                pack(late, dim, 8 * wide * narrow),
            ],
            axis=0,
        ).astype(BF)
        half = tail.shape[0] // 2
        tail = jnp.concatenate(
            [
                gather_all(
                    scatter_sum(tail[order * half : (order + 1) * half], wide, narrow, order)[-1],
                    wide,
                    narrow,
                    order,
                )
                for order in range(2)
            ],
            axis=0,
        ).astype(F32)
        return (text_out, patch_out, text_grad, patch_grad) + tuple(
            tail[i * dim : (i + 1) * dim] for i in range(3)
        ) + tuple(unpack(tail[3 * dim :], late))

    def never():
        return jax.tree.map(lambda a: jnp.zeros(a.shape, a.dtype), jax.eval_shape(backward))

    (
        text_out, patch_out, text_grad, patch_grad, query_weight_grad, key_weight_grad, value_weight_grad,
        query_bias_grad, value_bias_grad, line_table_grad, width_table_grad, height_table_grad,
    ) = lax.cond(text_len.reshape(()) >= 0, backward, never)
    return (
        text_out,
        patch_out,
        text_grad,
        patch_grad,
        query_weight_grad,
        query_bias_grad,
        key_weight_grad,
        value_weight_grad,
        value_bias_grad,
        output_weight_grad,
        output_bias_grad,
        norm_gain_grad,
        norm_shift_grad,
        up_weight_grad,
        up_bias_grad,
        down_weight_grad,
        down_bias_grad,
        final_gain_grad,
        final_shift_grad,
        line_table_grad,
        width_table_grad,
        height_table_grad,
    )


def solution(mesh):
    text = P(None, "narrow", "wide", None)
    patch = P("wide", None, "narrow", None)
    page = P("wide", "narrow")
    spots = P("wide", "narrow", None)
    in_specs = (text, patch, page, page, spots, spots, spots) + (P(),) * 18 + (text, patch)
    out_specs = (text, patch, text, patch) + (P(),) * 18
    return jax.shard_map(body, mesh=mesh, in_specs=in_specs, out_specs=out_specs, check_vma=False)
```

```python
from functools import partial

import jax
import jax.numpy as jnp
from jax import lax
from jax.experimental import pallas as pl
from jax.experimental.pallas import tpu as pltpu
from jax.sharding import PartitionSpec as P

HEADS = 12
TEXT = 512
PATCH = 576
SMALL_PATCH = 196
BF = jnp.bfloat16
F32 = jnp.float32
VMEM_BYTES = 60 * 2**20


def mm(left, right):
    return lax.dot_general(left, right, (((1,), (0,)), ((), ())), preferred_element_type=F32)


def inner(left, right):
    return lax.dot_general(left, right, (((0,), (0,)), ((), ())), preferred_element_type=F32)


def against(left, right):
    return lax.dot_general(left, right, (((1,), (1,)), ((), ())), preferred_element_type=F32)


def assemble(pieces, rows):
    at = 0
    for piece in pieces:
        rows[at : at + piece.shape[0], :] = piece[...]
        at += piece.shape[0]


def attend_kernel(count, *refs):
    pieces = refs[:count]
    (
        qw_ref, kw_ref, vw_ref, bias_ref, hot_ref, mask_ref, hott_ref, line_ref, width_ref,
        height_ref, exp_ref, ctxt_ref, ctx_ref, inv_ref, q_ref, kt_ref, v_ref, x_ref,
        keys, queries, values, rows,
    ) = refs[count:]
    seq = v_ref.shape[0]
    lanes = rows.shape[0]

    @pl.when(pl.program_id(0) == 0)
    def _():
        keys[:, 0:320] = hot_ref[0:seq, :]
        keys[:, 320:640] = hot_ref[0:seq, :]
        values[64:80, :] = jnp.ones((16, seq), BF)
        assemble(pieces, rows)
        rows[seq:lanes, :] = jnp.zeros((lanes - seq, rows.shape[1]), BF)
        x_ref[...] = rows[0:seq, :]

    both = mm(rows[...], jnp.concatenate([qw_ref[...], kw_ref[...]], axis=1))
    q = ((both[:, 0:128] + bias_ref[0]) * 0.125).astype(BF)
    k = both[:, 128:256].astype(BF)
    v = (mm(rows[...], vw_ref[...]) + bias_ref[1]).astype(BF)
    q_ref[...] = q
    v_ref[...] = v[0:seq]
    q_t = q.astype(F32).T.astype(BF)
    k = k.astype(F32)
    kt_ref[...] = k.T[:, 0:seq].astype(BF)
    v_t = v.astype(F32).T[:, 0:seq].astype(BF)
    lane = lax.broadcasted_iota(jnp.int32, (seq, 128), 1)
    contexts = []
    for h in range(2):
        mine = (lane < 64) if h == 0 else (lane >= 64)
        own, other = (640, 704) if h == 0 else (704, 640)
        keys[:, 640:768] = jnp.where(mine, k[0:seq], mask_ref[...].astype(F32)).astype(BF)
        queries[own : own + 64, :] = q_t[h * 64 : h * 64 + 64, :]
        queries[other : other + 64, :] = jnp.ones((64, lanes), BF)
        values[0:64, :] = v_t[h * 64 : h * 64 + 64, :]
        near = mm(line_ref[h], hott_ref[0:64, :]).astype(BF)
        queries[0:64, :] = near[0:64]
        queries[320:384, :] = near[64:128]
        near = mm(width_ref[h], hott_ref[64:192, :]).astype(BF)
        queries[64:192, :] = near[0:128]
        queries[384:512, :] = near[128:256]
        near = mm(height_ref[h], hott_ref[192:320, :]).astype(BF)
        queries[192:320, :] = near[0:128]
        queries[512:640, :] = near[128:256]
        scores = mm(keys[...], queries[...])
        peak = jnp.max(scores, axis=0, keepdims=True)
        weights = jnp.exp(scores - peak).astype(BF)
        exp_ref[h] = weights
        ctx = mm(values[...], weights)
        inverse = 1.0 / ctx[64:65]
        inv_ref[h] = inverse
        contexts.append(ctx[0:64] * inverse)
    ctx = jnp.concatenate(contexts, axis=0)
    ctxt_ref[...] = ctx.astype(BF)
    ctx_ref[...] = ctx.T[0:seq].astype(BF)


def attend(pieces, q_weight, k_weight, v_weight, bias, hot, mask, hot_t, line, width, height):
    seq = mask.shape[0]
    lanes, dim = hot.shape[0], q_weight.shape[0]

    def whole(a):
        return pl.BlockSpec(a.shape, lambda p: (0,) * a.ndim, pipeline_mode=pl.Buffered(1))

    def pair(a):
        return pl.BlockSpec((2,) + a.shape[1:], lambda p: (p, 0, 0))

    def columns(rows):
        return pl.BlockSpec((rows, 128), lambda p: (0, p))

    def rows(length):
        return pl.BlockSpec((128, length), lambda p: (p, 0))

    shape = jax.ShapeDtypeStruct
    return pl.pallas_call(
        partial(attend_kernel, len(pieces)),
        grid=(HEADS // 2,),
        in_specs=[whole(a) for a in pieces]
        + [
            columns(dim),
            columns(dim),
            columns(dim),
            pl.BlockSpec((2, 1, 128), lambda p: (0, 0, p)),
            whole(hot),
            whole(mask),
            whole(hot_t),
            pair(line),
            pair(width),
            pair(height),
        ],
        out_specs=[
            pl.BlockSpec((2, seq, lanes), lambda p: (p, 0, 0)),
            rows(lanes),
            columns(seq),
            pl.BlockSpec((2, 1, lanes), lambda p: (p, 0, 0)),
            columns(lanes),
            rows(seq),
            columns(seq),
            pl.BlockSpec((seq, dim), lambda p: (0, 0)),
        ],
        out_shape=[
            shape((HEADS, seq, lanes), BF),
            shape((dim, lanes), BF),
            shape((seq, dim), BF),
            shape((HEADS, 1, lanes), F32),
            shape((lanes, dim), BF),
            shape((dim, seq), BF),
            shape((seq, dim), BF),
            shape((seq, dim), BF),
        ],
        scratch_shapes=[
            pltpu.VMEM((seq, 768), BF),
            pltpu.VMEM((768, lanes), BF),
            pltpu.VMEM((80, seq), BF),
            pltpu.VMEM((lanes, dim), BF),
        ],
        compiler_params=pltpu.CompilerParams(vmem_limit_bytes=VMEM_BYTES),
        cost_estimate=pl.CostEstimate(
            flops=HEADS * seq * lanes * 4096, bytes_accessed=HEADS * seq * lanes * 2,
            transcendentals=HEADS * seq * lanes,
        ),
    )(*pieces, q_weight, k_weight, v_weight, bias, hot, mask, hot_t, line, width, height)


def attend_back_kernel(held, *refs):
    (
        exp_ref, ctxt_ref, inv_ref, v_ref, kt_ref, q_ref, dattn_ref, outw_ref, hot_ref, hott_ref,
        dqkv_ref, gwidth_ref, gheight_ref, gline_ref, values, dctx, lefts, rights, ds, dattn,
    ) = refs[:10] + refs[10 + held :]
    seq = v_ref.shape[0]
    lanes = q_ref.shape[0]

    @pl.when(pl.program_id(0) == 0)
    def _():
        for h in range(2):
            lefts[h, 64:192, :] = hott_ref[64:192, 0:seq]
            rights[h, :, 128:256] = hot_ref[:, 192:320]
        dattn[0:seq, :] = dattn_ref[...]
        dattn[seq:lanes, :] = jnp.zeros((lanes - seq, dattn.shape[1]), BF)

    lane = lax.broadcasted_iota(jnp.int32, (seq, 128), 1)
    query_lane = lax.broadcasted_iota(jnp.int32, (lanes, 128), 1)
    row = lax.broadcasted_iota(jnp.int32, (64, lanes), 0)
    line_hot = jnp.concatenate([hot_ref[:, 0:64], hot_ref[:, 0:64]], axis=1).astype(F32)
    d_rows_t = against(outw_ref[...], dattn[...])
    d_rows_t = [d_rows_t[h * 64 : h * 64 + 64] * inv_ref[h] for h in range(2)]
    d_rows = jnp.concatenate(d_rows_t, axis=0).T.astype(BF)
    results = []
    by_queries = []
    for h in range(2):
        mine = (lane < 64) if h == 0 else (lane >= 64)
        query_mine = (query_lane < 64) if h == 0 else (query_lane >= 64)
        own, other = (0, 64) if h == 0 else (64, 0)
        part = slice(h * 64, h * 64 + 64)
        values[h] = jnp.where(mine, v_ref[...].astype(F32), 1.0).astype(BF)
        delta = -jnp.sum(d_rows_t[h] * ctxt_ref[part, :].astype(F32), axis=0, keepdims=True)
        high = delta.astype(BF).astype(F32)
        extra = jnp.where(row == 0, high, jnp.where(row == 1, delta - high, 0.0))
        dctx[h, own : own + 64, :] = d_rows_t[h].astype(BF)
        dctx[h, other : other + 64, :] = extra.astype(BF)
        lefts[h, 0:64, :] = kt_ref[part, :]
        rights[h, :, 0:128] = jnp.where(query_mine, q_ref[...].astype(F32), line_hot).astype(BF)
        d_scores = mm(values[h], dctx[h])
        ds[h] = (exp_ref[h].astype(F32) * d_scores).astype(BF)
        by_query = mm(lefts[h], ds[h])
        by_queries.append(by_query[0:64] * 0.125)
        gwidth_ref[h] = mm(by_query[64:192].astype(BF), hot_ref[:, 64:192])
        by_key = mm(ds[h], rights[h])
        near = mm(hott_ref[0:64, 0:seq], by_key[:, 0:128].astype(BF))
        gline_ref[h] = near[:, 64:128] if h == 0 else near[:, 0:64]
        gheight_ref[h] = mm(hott_ref[192:320, 0:seq], by_key[:, 128:256].astype(BF))
        results.append((by_key[:, 0:128], mm(exp_ref[h], d_rows)))
    dqkv_ref[0] = jnp.concatenate(by_queries, axis=0).T[0:seq].astype(BF)
    dqkv_ref[1] = jnp.where(lane < 64, results[0][0], results[1][0]).astype(BF)
    dqkv_ref[2] = jnp.where(lane < 64, results[0][1], results[1][1]).astype(BF)


def attend_back(first, pairs, held, exps, ctx_t, inverse, v, k_t, q, d_attn, out_weight, hot, hot_t):
    seq, dim = v.shape
    lanes = q.shape[0]

    def whole(a):
        return pl.BlockSpec(a.shape, lambda p: (0,) * a.ndim, pipeline_mode=pl.Buffered(1))

    def columns(rows):
        return pl.BlockSpec((rows, 128), lambda p: (0, p + first))

    def rows(length):
        return pl.BlockSpec((128, length), lambda p: (p + first, 0))

    def pair(*shape, start=first):
        return pl.BlockSpec((2,) + shape, lambda p: (p + start, 0, 0))

    shape = jax.ShapeDtypeStruct
    return pl.pallas_call(
        partial(attend_back_kernel, len(held)),
        grid=(pairs,),
        in_specs=[
            pair(seq, lanes),
            rows(lanes),
            pair(1, lanes),
            columns(seq),
            rows(seq),
            columns(lanes),
            whole(d_attn),
            rows(dim),
            whole(hot),
            whole(hot_t),
        ]
        + [pl.BlockSpec(memory_space=pl.ANY)] * len(held),
        out_specs=[
            pl.BlockSpec((3, seq, 128), lambda p: (0, 0, p)),
            pair(128, 128, start=0),
            pair(128, 128, start=0),
            pair(64, 64, start=0),
        ],
        out_shape=[
            shape((3, seq, 128 * pairs), BF),
            shape((2 * pairs, 128, 128), F32),
            shape((2 * pairs, 128, 128), F32),
            shape((2 * pairs, 64, 64), F32),
        ],
        scratch_shapes=[
            pltpu.VMEM((2, seq, 128), BF),
            pltpu.VMEM((2, 128, lanes), BF),
            pltpu.VMEM((2, 192, seq), BF),
            pltpu.VMEM((2, lanes, 256), BF),
            pltpu.VMEM((2, seq, lanes), BF),
            pltpu.VMEM((lanes, dim), BF),
        ],
        compiler_params=pltpu.CompilerParams(vmem_limit_bytes=VMEM_BYTES),
        cost_estimate=pl.CostEstimate(
            flops=2 * pairs * seq * lanes * 4096, bytes_accessed=4 * pairs * seq * lanes,
            transcendentals=0,
        ),
    )(exps, ctx_t, inverse, v, k_t, q, d_attn, out_weight, hot, hot_t, *held)


def gelu_pair(x):
    bell = jnp.exp(x * x * -0.5)
    t = 1.0 / (1.0 + 0.23164189 * jnp.abs(x))
    poly = t * (0.127414796 + t * (-0.142248368 + t * (0.7107068705 + t * (-0.7265760135 + t * 0.5307027145))))
    upper = poly * bell
    phi = jnp.where(x < 0, upper, 1.0 - upper)
    return x * phi, phi + x * bell * 0.3989422804014327

def normalise(rows):
    mean = jnp.mean(rows, axis=-1, keepdims=True)
    centred = rows - mean
    scale = lax.rsqrt(jnp.mean(centred * centred, axis=-1, keepdims=True) + 1e-05)
    return centred * scale, scale

def normalise_back(hat, scale, d_hat):
    return scale * (d_hat - jnp.mean(d_hat, axis=-1, keepdims=True) - hat * jnp.mean(d_hat * hat, axis=-1, keepdims=True))

def rows_kernel(count, *refs):
    pieces = refs[:count]
    (
        x_ref, ctx_ref, out_w, up_w, down_w, bias_ref, up_b, final_ref, dmid_ref, dattn_ref,
        normed_ref, act_ref, dbranch_ref, dpre_ref, sums_ref, upsum_ref, slope, cots,
    ) = refs[count:]
    step = pl.program_id(0)
    block = x_ref.shape[0]

    @pl.when(pl.program_id(0)==0)
    def _():
        sums_ref[...] = jnp.zeros_like(sums_ref)
        upsum_ref[...] = jnp.zeros_like(upsum_ref)
        assemble(pieces, cots)

    ff = up_w.shape[1]
    attn = mm(ctx_ref[...], out_w[...]) + bias_ref[0:1]
    hat, scale = normalise(x_ref[...].astype(F32) + attn)
    normed = hat * bias_ref[1:2] + bias_ref[2:3]
    low = normed.astype(BF)
    normed_ref[...] = low
    branch = bias_ref[3:4]
    for f in range(0, ff, 768):
        part = slice(f, f+768)
        act, grad = gelu_pair(mm(low, up_w[:, part]) + up_b[:, part])
        slope[:, part] = grad
        act = act.astype(BF)
        act_ref[:, part] = act
        branch = branch + mm(act, down_w[part, :])
    final_hat, final_scale = normalise(normed + branch)
    final_ref[...] = (final_hat * bias_ref[4:5] + bias_ref[5:6]).astype(BF)
    cot = cots[pl.ds(pl.multiple_of(step * block, 16), block), :].astype(F32)
    d_sum = normalise_back(final_hat, final_scale, cot * bias_ref[4:5])
    d_branch = d_sum.astype(BF)
    dbranch_ref[...] = d_branch
    total = lambda a: jnp.sum(a, axis=0, keepdims=True)
    d_normed = d_sum
    for f in range(0, ff, 768):
        part = slice(f, f+768)
        d_pre = (against(d_branch, down_w[part, :]) * slope[:, part]).astype(BF)
        dpre_ref[:, part] = d_pre
        upsum_ref[:, part] += total(d_pre.astype(F32))
        d_normed = d_normed + against(d_pre, up_w[:, part])
    d_mid = normalise_back(hat, scale, d_normed * bias_ref[1:2])
    dmid_ref[...] = d_mid
    d_attn = d_mid.astype(BF)
    dattn_ref[...] = d_attn
    sums_ref[...] += jnp.concatenate([total(d_attn.astype(F32)), total(d_normed*hat), total(d_normed), total(d_branch.astype(F32)), total(cot*final_hat), total(cot), jnp.zeros((2,cot.shape[1]),F32)], axis=0)

def rows_pass(pieces, x, ctx, out_w, up_w, down_w, bias, up_b):
    seq, dim = ctx.shape
    ff = up_w.shape[1]
    block = seq // 4
    row = lambda w: pl.BlockSpec((block, w), lambda i: (i,0))
    whole = lambda a: pl.BlockSpec(a.shape, lambda i: (0,)*a.ndim, pipeline_mode=pl.Buffered(1))
    sd = jax.ShapeDtypeStruct
    return pl.pallas_call(partial(rows_kernel, len(pieces)), grid=(seq//block,),
        in_specs=[whole(a) for a in pieces] + [row(dim),row(dim),whole(out_w),whole(up_w),whole(down_w),whole(bias),whole(up_b)],
        out_specs=[row(dim),row(dim),row(dim),row(dim),row(ff),row(dim),row(ff),pl.BlockSpec((8,dim),lambda i:(0,0)),pl.BlockSpec((1,ff),lambda i:(0,0))],
        out_shape=[sd((seq,dim),BF),sd((seq,dim),F32),sd((seq,dim),BF),sd((seq,dim),BF),sd((seq,ff),BF),sd((seq,dim),BF),sd((seq,ff),BF),sd((8,dim),F32),sd((1,ff),F32)],
        scratch_shapes=[pltpu.VMEM((block, ff), F32), pltpu.VMEM((seq, dim), BF)],
        compiler_params=pltpu.CompilerParams(vmem_limit_bytes=VMEM_BYTES),
        cost_estimate=pl.CostEstimate(
            flops=34 * seq * dim * dim, bytes_accessed=64 * seq * dim, transcendentals=seq * ff
        ),
    )(*pieces,x,ctx,out_w,up_w,down_w,bias,up_b)


def down_kernel(act_ref, dbranch_ref, ctxt_ref, dattn_ref, down_ref, out_ref):
    step = pl.program_id(0)
    last = pl.num_programs(0) - 1
    seq = act_ref.shape[0]

    @pl.when(step < last)
    def _():
        down_ref[...] = inner(act_ref[...], dbranch_ref[...]).astype(BF)

    @pl.when(step == last)
    def _():
        out_ref[...] = mm(ctxt_ref[:, 0:seq], dattn_ref[...]).astype(BF)


def down_sums(room, act, d_branch, ctx_t, d_attn):
    seq, ff = act.shape
    dim = d_branch.shape[1]
    steps = ff // dim

    def whole(a):
        return pl.BlockSpec(a.shape, lambda p: (0,) * a.ndim, pipeline_mode=pl.Buffered(1))

    shape = jax.ShapeDtypeStruct
    return pl.pallas_call(
        down_kernel,
        grid=(steps + 1,),
        in_specs=[
            pl.BlockSpec((seq, dim), lambda p: (0, jnp.minimum(p, steps - 1))),
            whole(d_branch),
            whole(ctx_t),
            whole(d_attn),
        ],
        out_specs=[
            pl.BlockSpec((dim, dim), lambda p: (jnp.minimum(p, steps - 1), 0)),
            pl.BlockSpec((dim, dim), lambda p: (0, 0)),
        ],
        out_shape=[shape((ff, dim), BF), shape((dim + room, dim), BF)],
        compiler_params=pltpu.CompilerParams(vmem_limit_bytes=VMEM_BYTES),
        cost_estimate=pl.CostEstimate(
            flops=10 * seq * dim * dim, bytes_accessed=32 * seq * dim, transcendentals=0
        ),
    )(act, d_branch, ctx_t, d_attn)


def up_kernel(normed_ref, dpre_ref, grad_ref, normed_t):
    @pl.when(pl.program_id(0) == 0)
    def _():
        normed_t[...] = normed_ref[...].astype(F32).T.astype(BF)

    grad_ref[...] = mm(normed_t[...], dpre_ref[...]).astype(BF)


def up_sums(normed, d_pre):
    seq, dim = normed.shape
    ff = d_pre.shape[1]
    return pl.pallas_call(
        up_kernel,
        grid=(ff // dim,),
        in_specs=[
            pl.BlockSpec((seq, dim), lambda p: (0, 0), pipeline_mode=pl.Buffered(1)),
            pl.BlockSpec((seq, dim), lambda p: (0, p)),
        ],
        out_specs=pl.BlockSpec((dim, dim), lambda p: (0, p)),
        out_shape=jax.ShapeDtypeStruct((dim, ff), BF),
        scratch_shapes=[pltpu.VMEM((dim, seq), BF)],
        compiler_params=pltpu.CompilerParams(vmem_limit_bytes=VMEM_BYTES),
        cost_estimate=pl.CostEstimate(
            flops=8 * seq * dim * dim, bytes_accessed=24 * seq * dim, transcendentals=0
        ),
    )(normed, d_pre)


def last_kernel(count, held, *refs):
    parts = refs[:count]
    x_ref, weight_ref, dmid_ref = refs[count : count + 3]
    grad_ref, drows_ref, sums_ref, x_t, total = refs[count + 3 + held :]
    step = pl.program_id(0)
    d_qkv = jnp.concatenate([part[0] for part in parts], axis=1)

    @pl.when(step == 0)
    def _():
        x_t[...] = x_ref[...].astype(F32).T.astype(BF)
        total[...] = dmid_ref[...]

    grad_ref[...] = mm(x_t[...], d_qkv).astype(BF)
    total[...] += against(d_qkv, weight_ref[0])
    sums_ref[0] = jnp.broadcast_to(
        jnp.sum(d_qkv.astype(F32), axis=0, keepdims=True), sums_ref.shape[1:]
    )

    @pl.when(step == 2)
    def _():
        drows_ref[...] = total[...].astype(BF)


def last_products(rows, held, x, d_qkv, weights, d_mid):
    seq, dim = d_mid.shape

    def whole(a):
        return pl.BlockSpec(a.shape, lambda p: (0,) * a.ndim, pipeline_mode=pl.Buffered(1))

    shape = jax.ShapeDtypeStruct
    return pl.pallas_call(
        partial(last_kernel, len(d_qkv), len(held)),
        grid=(3,),
        in_specs=[pl.BlockSpec((1,) + a.shape[1:], lambda p: (p, 0, 0)) for a in d_qkv]
        + [
            whole(x),
            pl.BlockSpec((1, dim, dim), lambda p: (p, 0, 0)),
            whole(d_mid),
        ]
        + [pl.BlockSpec(memory_space=pl.ANY)] * len(held),
        out_specs=[
            pl.BlockSpec((dim, dim), lambda p: (p, 0)),
            pl.BlockSpec((seq, dim), lambda p: (0, 0)),
            pl.BlockSpec((1, 8, dim), lambda p: (p, 0, 0)),
        ],
        out_shape=[shape((rows, dim), BF), shape((seq, dim), BF), shape((3, 8, dim), F32)],
        scratch_shapes=[pltpu.VMEM((dim, seq), BF), pltpu.VMEM((seq, dim), F32)],
        compiler_params=pltpu.CompilerParams(vmem_limit_bytes=VMEM_BYTES),
        cost_estimate=pl.CostEstimate(
            flops=12 * seq * dim * dim, bytes_accessed=32 * seq * dim, transcendentals=0
        ),
    )(*d_qkv, x, weights, d_mid, *held)


def bucket_select(table):
    reach = (table.shape[0] - 1) // 2
    spots = jnp.arange(4 * reach, dtype=jnp.int32)
    bucket = jnp.clip(spots[None, :] - spots[:, None], -reach, reach) + reach
    return bucket[None] == jnp.arange(2 * reach + 1, dtype=jnp.int32)[:, None, None]


def spread_table(table):
    span = 2 * (table.shape[0] - 1)
    high = table.astype(BF)
    low = (table - high.astype(F32)).astype(BF)
    both = jnp.stack([high, low], axis=2).reshape(table.shape[0], -1)
    spread = lax.dot_general(
        both,
        bucket_select(table).astype(BF).reshape(table.shape[0], -1),
        (((0,), (0,)), ((), ())),
        preferred_element_type=F32,
    )
    return spread.astype(BF).reshape(HEADS, 2 * span, span)


def gather_table(parts, table):
    select = bucket_select(table).astype(F32).reshape(table.shape[0], -1)
    return jnp.concatenate(
        [
            lax.dot_general(
                select,
                grads.reshape(grads.shape[0], -1),
                (((1,), (1,)), ((), ())),
                precision=lax.Precision.HIGHEST,
                preferred_element_type=F32,
            )
            for grads in parts
        ],
        axis=1,
    )


def shift_pairs(size, step):
    return [(i, (i + step) % size) for i in range(size)]


def flip_pairs(size, step):
    return [(i, i ^ step) for i in range(size)]


def pick(array, index):
    return lax.dynamic_index_in_dim(array, index, 0, keepdims=False)


def swap_text(parts):
    return lax.all_to_all(parts, "wide", split_axis=0, concat_axis=0, tiled=True)


def patch_order(size):
    me = lax.axis_index("narrow")
    return [me ^ k for k in range(size)]


def swap_patch(parts):
    size = parts.shape[0]
    me = lax.axis_index("narrow")
    return [pick(parts, me)] + [
        lax.ppermute(pick(parts, me ^ k), "narrow", flip_pairs(size, k)) for k in range(1, size)
    ]


def flip_axis(array, axis, bit):
    return jnp.where(bit == 1, jnp.flip(array, axis), array)


def from_flipped(parts, me):
    size = parts.shape[0]
    bits = size.bit_length() - 1
    parts = parts.reshape((2,) * bits + parts.shape[1:])
    for b in range(bits):
        parts = flip_axis(parts, bits - 1 - b, (me >> b) & 1)
    return parts.reshape((size,) + parts.shape[bits:])


def patch_away(rows, size):
    me = lax.axis_index("narrow")
    parts = rows.reshape(size, -1, rows.shape[1])
    arrived = [parts[0]] + [
        lax.ppermute(parts[k], "narrow", flip_pairs(size, k)) for k in range(1, size)
    ]
    return from_flipped(jnp.stack(arrived), me)


def add(*terms):
    total = terms[0].astype(F32)
    for term in terms[1:]:
        total = total + term.astype(F32)
    return total.astype(BF)


def wide_orders(wide, ways):
    bits = list(range(1, wide.bit_length() - 1))
    return [bits, bits[::-1]][:ways]


def wide_bit(bit):
    return (lax.axis_index("wide") >> bit) & 1


def add_kernel(me_ref, own_ref, arrived_ref, *refs):
    refs[-1][...] = (own_ref[0].astype(F32) + arrived_ref[...].astype(F32)).astype(BF)


def add_own(parts, me, arrived, held):
    rows, columns = arrived.shape
    steps = 2 if rows % 32 == 0 else 1
    block = rows // steps
    return pl.pallas_call(
        add_kernel,
        grid_spec=pltpu.PrefetchScalarGridSpec(
            num_scalar_prefetch=1,
            grid=(steps,),
            in_specs=[
                pl.BlockSpec((1, block, columns), lambda i, me_ref: (me_ref[0], i, 0)),
                pl.BlockSpec((block, columns), lambda i, me_ref: (i, 0)),
            ]
            + [pl.BlockSpec(memory_space=pl.ANY)] * len(held),
            out_specs=pl.BlockSpec((block, columns), lambda i, me_ref: (i, 0)),
        ),
        out_shape=jax.ShapeDtypeStruct((rows, columns), BF),
        compiler_params=pltpu.CompilerParams(vmem_limit_bytes=VMEM_BYTES),
        cost_estimate=pl.CostEstimate(flops=0, bytes_accessed=6 * rows * columns, transcendentals=0),
    )(me.reshape(1), parts, arrived, *held)


def wide_step(grad, wide, bit, held=()):
    parts = grad.reshape(2, -1, grad.shape[1])
    me = wide_bit(bit)
    arrived = lax.ppermute(pick(parts, 1 - me), "wide", flip_pairs(wide, 1 << bit))
    return add_own(parts, me, arrived, held) if held else add(pick(parts, me), arrived)


def cut(grad, ways):
    part = grad.shape[0] // ways
    return [grad[i * part : (i + 1) * part] for i in range(ways)]


def wide_steps(shares, wide, i, held=()):
    orders = wide_orders(wide, len(shares))
    return [
        wide_step(a, wide, order[i], held if n == 0 else ())
        for n, (a, order) in enumerate(zip(shares, orders))
    ]


def narrow_step(shares, narrow):
    me = lax.axis_index("narrow")
    parts = [a.reshape(narrow, -1, a.shape[1]) for a in shares]

    def picked(index):
        return jnp.stack([pick(a, index) for a in parts])

    arrived = [
        lax.ppermute(picked(me ^ k), "narrow", flip_pairs(narrow, k)) for k in range(1, narrow)
    ]
    return add(picked(me), *arrived)


def gather_narrow(part, narrow):
    parts = [part] + [
        lax.ppermute(part, "narrow", flip_pairs(narrow, k)) for k in range(1, narrow)
    ]
    return [jnp.stack([p[n] for p in parts]) for n in range(part.shape[0])]


def gather_wide(shares, wide, i):
    return [
        jnp.concatenate([a, lax.ppermute(a, "wide", flip_pairs(wide, 1 << order[i]))], axis=0)
        for a, order in zip(shares, wide_orders(wide, len(shares)))
    ]


def gather_core(shares, wide):
    return shares + [lax.ppermute(a, "wide", flip_pairs(wide, 1)) for a in shares]


def convert_kernel(up_ref, down_ref, out_ref, after_ref, up_out, down_out, out_out):
    step = pl.program_id(0)
    parts = (pl.num_programs(0) - 1) // 2

    @pl.when(step < parts)
    def _():
        up_out[...] = up_ref[...].astype(F32)

    @pl.when((step >= parts) & (step < 2 * parts))
    def _():
        down_out[...] = down_ref[...].astype(F32)

    @pl.when(step == 2 * parts)
    def _():
        out_out[...] = out_ref[...].astype(F32)


def convert(up_total, down_total, out_total, after):
    dim, ff = up_total.shape
    parts = ff // dim

    def block(index):
        return pl.BlockSpec((dim, dim), index)

    up_block = block(lambda p: (0, jnp.minimum(p, parts - 1)))
    down_block = block(lambda p: (jnp.clip(p - parts, 0, parts - 1), 0))
    out_block = block(lambda p: (0, 0))
    shape = jax.ShapeDtypeStruct
    return pl.pallas_call(
        convert_kernel,
        grid=(2 * parts + 1,),
        in_specs=[up_block, down_block, out_block, pl.BlockSpec(memory_space=pl.ANY)],
        out_specs=[up_block, down_block, out_block],
        out_shape=[shape((dim, ff), F32), shape((ff, dim), F32), shape((dim, dim), F32)],
        compiler_params=pltpu.CompilerParams(vmem_limit_bytes=VMEM_BYTES),
        cost_estimate=pl.CostEstimate(flops=0, bytes_accessed=13 * dim * ff, transcendentals=0),
    )(up_total, down_total, out_total, after)


def finish_kernel(places, ways, cuts, index_ref, *refs):
    pieces, outs = refs[: 2 * ways], refs[2 * ways :]
    rows = pieces[0].shape[1]
    for core in range(2):
        for way in range(ways):
            for place in range(places):
                at = ((core * ways + way) * places + place) * rows
                if at >= cuts[-1][1]:
                    continue
                here = index_ref[way, place]
                same = pieces[way][here].astype(F32)
                other = pieces[ways + way][here].astype(F32)
                block = jnp.where(index_ref[2, 0] == core, same, other)
                for (start, stop), out in zip(cuts, outs):
                    low, high = max(at, start), min(at + rows, stop)
                    if low < high:
                        out[low - start : high - start, :] = block[low - at : high - at]


def finish(pieces, wide, narrow, lengths):
    places, _, columns = pieces[0].shape
    ways = len(pieces) // 2
    index = []
    for order in wide_orders(wide, 2):
        me = jnp.int32(0)
        for bit in order:
            me = me * 2 + wide_bit(bit)
        me = me * narrow + lax.axis_index("narrow")
        index.append(jnp.arange(places, dtype=jnp.int32) ^ me)
    index.append(jnp.full((places,), wide_bit(0), jnp.int32))
    cuts = []
    for length in lengths:
        start = cuts[-1][1] if cuts else 0
        cuts.append((start, start + length))
    return pl.pallas_call(
        partial(finish_kernel, places, ways, cuts),
        in_specs=[pl.BlockSpec(memory_space=pltpu.SMEM)]
        + [pl.BlockSpec(memory_space=pltpu.VMEM)] * len(pieces),
        out_specs=[pl.BlockSpec(memory_space=pltpu.VMEM)] * len(lengths),
        out_shape=[jax.ShapeDtypeStruct((length, columns), F32) for length in lengths],
        compiler_params=pltpu.CompilerParams(vmem_limit_bytes=VMEM_BYTES),
        cost_estimate=pl.CostEstimate(
            flops=0, bytes_accessed=8 * sum(lengths) * columns, transcendentals=0
        ),
    )(jnp.stack(index), *pieces)


def room_for(rows, wide, narrow):
    return 16 + -(rows + 16) % (8 * wide * narrow)


def pack(grads, columns, rows):
    lines = []
    for grad in grads:
        flat = grad.reshape(-1)
        lines.append(jnp.pad(flat, (0, -flat.shape[0] % columns)).reshape(-1, columns))
    lines = jnp.concatenate(lines, axis=0)
    return jnp.pad(lines, ((0, -lines.shape[0] % rows), (0, 0)))


def unpack(lines, grads):
    columns = lines.shape[1]
    at = 0
    out = []
    for grad in grads:
        count = -(-grad.size // columns)
        out.append(lines[at : at + count].reshape(-1)[: grad.size].reshape(grad.shape))
        at += count
    return out


def body(
    text_in,
    patch_in,
    res_class,
    text_len,
    pos_line,
    pos_x,
    pos_y,
    query_weight,
    query_bias,
    key_weight,
    value_weight,
    value_bias,
    output_weight,
    output_bias,
    norm_gain,
    norm_shift,
    up_weight,
    up_bias,
    down_weight,
    down_bias,
    final_gain,
    final_shift,
    line_table,
    width_table,
    height_table,
    cot_text,
    cot_patch,
):
    text_shape = text_in.shape
    patch_shape = patch_in.shape
    dim = text_shape[3]
    seq = TEXT + PATCH
    lanes = -(-seq // 128) * 128
    wide = text_shape[0]
    narrow = patch_shape[1]
    pieces = [swap_text(text_in.reshape(wide, -1, dim)).reshape(-1, dim)]
    pieces += swap_patch(patch_in.reshape(narrow, -1, dim))
    cot_text, cot_patch, pieces = lax.optimization_barrier((cot_text, cot_patch, pieces))
    cots = [swap_text(cot_text.reshape(wide, -1, dim)).reshape(-1, dim)]
    cots += swap_patch(cot_patch.reshape(narrow, -1, dim))
    index = jnp.arange(seq, dtype=jnp.int32)
    live_patch = jnp.where(res_class.reshape(()) == 1, PATCH, SMALL_PATCH)
    valid = jnp.where(index < TEXT, index < text_len.reshape(()), index - TEXT < live_patch)
    facts = jnp.concatenate(
        [pos_line.reshape(1, -1), pos_x.reshape(1, -1), pos_y.reshape(1, -1), valid.astype(jnp.int32)[None]]
    )
    patch_facts = facts[:, TEXT:].reshape(4, narrow, -1)
    facts = jnp.concatenate(
        [facts[:, :TEXT]]
        + [
            lax.dynamic_index_in_dim(patch_facts, i, 1, keepdims=False)
            for i in patch_order(narrow)
        ],
        axis=1,
    )
    line_spots, x_spots, y_spots = facts[0], facts[1], facts[2]
    valid = facts[3] == 1

    line = spread_table(line_table)
    width = spread_table(width_table)
    height = spread_table(height_table)
    hots = []
    hots_t = []
    for spots, table in ((line_spots, line_table), (x_spots, width_table), (y_spots, height_table)):
        span = jnp.arange(2 * (table.shape[0] - 1), dtype=jnp.int32)
        long = jnp.pad(spots, (0, lanes - seq), constant_values=-1)
        hots.append((long[:, None] == span[None, :]).astype(BF))
        hots_t.append((long[None, :] == span[:, None]).astype(BF))
    hot = jnp.concatenate(hots, axis=1)
    hot_t = jnp.concatenate(hots_t, axis=0)
    column = jnp.arange(128, dtype=jnp.int32)
    mask = jnp.where((column[None, :] % 64 == 0) & ~valid[:, None], -1e30, 0.0).astype(BF)

    exps, ctx_t, ctx, inverse, q, k_t, v, rows_in = attend(
        pieces,
        query_weight,
        key_weight,
        value_weight,
        jnp.stack([query_bias, value_bias])[:, None],
        hot,
        mask,
        hot_t,
        line,
        width,
        height,
    )
    vectors = jnp.stack(
        [output_bias, norm_gain, norm_shift, down_bias, final_gain, final_shift] + [final_shift] * 2
    )
    final_low, d_mid, d_attn, normed, act, d_branch, d_pre, sums, up_sum = rows_pass(
        cots, rows_in, ctx, output_weight, up_weight, down_weight, vectors, up_bias[None]
    )
    early = (sums[0], sums[1], sums[2], up_sum, sums[3], sums[4], sums[5])
    small = pack(early, dim, 16).astype(BF)
    down_low, out_low = down_sums(small.shape[0], act, d_branch, ctx_t, d_attn)
    out_low = lax.dynamic_update_slice(out_low, small, (dim, 0))
    up_low = up_sums(normed, d_pre)
    down_total, up_total, out_total = lax.psum((down_low, up_low, out_low), ("wide", "narrow"))
    qkv_weight = jnp.stack([query_weight, key_weight, value_weight])

    def backward():
        text_out = swap_text(final_low[:TEXT].reshape(wide, -1, dim)).reshape(text_shape)
        patch_out = patch_away(final_low[TEXT:], narrow).reshape(patch_shape)
        levels = wide.bit_length() - 2
        d_qkv, g_width, g_height, g_line = attend_back(
            0, HEADS // 2, [], exps, ctx_t, inverse, v, k_t, q, d_attn, output_weight, hot, hot_t
        )
        late_room = room_for(3 * dim, wide, narrow)
        tail, d_rows, qkv_sums = last_products(
            3 * dim + late_room, [text_out, patch_out], rows_in, [d_qkv], qkv_weight, d_mid
        )
        text_grad = swap_text(d_rows[:TEXT].reshape(wide, -1, dim)).reshape(text_shape)
        patch_grad = patch_away(d_rows[TEXT:], narrow).reshape(patch_shape)
        late = (
            qkv_sums[0, 0],
            qkv_sums[2, 0],
            gather_table([g_line], line_table),
            gather_table([g_width], width_table),
            gather_table([g_height], height_table),
        )
        small = pack(late, dim, late_room).astype(BF)
        tail = lax.dynamic_update_slice(tail, small, (3 * dim, 0))
        halves = cut(wide_step(tail, wide, 0), 2)
        for i in range(levels):
            moved = [text_grad, patch_grad] if i == levels - 1 else []
            halves = wide_steps(halves, wide, i, moved)
        halves = gather_narrow(narrow_step(halves, narrow), narrow)
        for i in range(levels - 1, -1, -1):
            halves = gather_wide(halves, wide, i)
        *large, late_small = finish(gather_core(halves, wide), wide, narrow, (dim,) * 3 + (16,))
        return (
            text_out, patch_out, text_grad, patch_grad, *large, *unpack(late_small, late),
        )

    def never():
        return jax.tree.map(lambda a: jnp.zeros(a.shape, a.dtype), jax.eval_shape(backward))

    (
        text_out, patch_out, text_grad, patch_grad, query_weight_grad, key_weight_grad,
        value_weight_grad, query_bias_grad, value_bias_grad, line_table_grad, width_table_grad,
        height_table_grad,
    ) = lax.cond(text_len.reshape(()) >= 0, backward, never)
    up_weight_grad, down_weight_grad, output_weight_grad = convert(
        up_total, down_total, out_total, value_weight_grad
    )
    (
        output_bias_grad,
        norm_gain_grad,
        norm_shift_grad,
        up_bias_grad,
        down_bias_grad,
        final_gain_grad,
        final_shift_grad,
    ) = unpack(out_total[dim:].astype(F32), early)
    up_bias_grad = up_bias_grad.reshape(-1)
    return (
        text_out,
        patch_out,
        text_grad,
        patch_grad,
        query_weight_grad,
        query_bias_grad,
        key_weight_grad,
        value_weight_grad,
        value_bias_grad,
        output_weight_grad,
        output_bias_grad,
        norm_gain_grad,
        norm_shift_grad,
        up_weight_grad,
        up_bias_grad,
        down_weight_grad,
        down_bias_grad,
        final_gain_grad,
        final_shift_grad,
        line_table_grad,
        width_table_grad,
        height_table_grad,
    )


def solution(mesh):
    text = P(None, "narrow", "wide", None)
    patch = P("wide", None, "narrow", None)
    page = P("wide", "narrow")
    spots = P("wide", "narrow", None)
    in_specs = (text, patch, page, page, spots, spots, spots) + (P(),) * 18 + (text, patch)
    out_specs = (text, patch, text, patch) + (P(),) * 18
    return jax.shard_map(body, mesh=mesh, in_specs=in_specs, out_specs=out_specs, check_vma=False)
```

```python
from functools import partial

import jax
import jax.numpy as jnp
from jax import lax
from jax.experimental import pallas as pl
from jax.experimental.pallas import tpu as pltpu
from jax.sharding import PartitionSpec as P

HEADS = 12
TEXT = 512
PATCH = 576
SMALL_PATCH = 196
BF = jnp.bfloat16
F32 = jnp.float32
VMEM_BYTES = 60 * 2**20


def mm(left, right):
    return lax.dot_general(left, right, (((1,), (0,)), ((), ())), preferred_element_type=F32)


def inner(left, right):
    return lax.dot_general(left, right, (((0,), (0,)), ((), ())), preferred_element_type=F32)


def against(left, right):
    return lax.dot_general(left, right, (((1,), (1,)), ((), ())), preferred_element_type=F32)


def assemble(pieces, rows):
    at = 0
    for piece in pieces:
        rows[at : at + piece.shape[0], :] = piece[...]
        at += piece.shape[0]


def attend_kernel(count, *refs):
    pieces = refs[:count]
    (
        qw_ref, kw_ref, vw_ref, bias_ref, hot_ref, mask_ref, hott_ref, line_ref, width_ref,
        height_ref, exp_ref, ctxt_ref, ctx_ref, inv_ref, q_ref, kt_ref, v_ref, x_ref,
        keys, queries, values, rows,
    ) = refs[count:]
    seq = v_ref.shape[0]
    lanes = rows.shape[0]

    @pl.when(pl.program_id(0) == 0)
    def _():
        keys[:, 0:320] = hot_ref[0:seq, :]
        values[64:80, :] = jnp.ones((16, seq), BF)
        assemble(pieces, rows)
        rows[seq:lanes, :] = jnp.zeros((lanes - seq, rows.shape[1]), BF)
        x_ref[...] = rows[0:seq, :]

    both = mm(rows[...], jnp.concatenate([qw_ref[...], kw_ref[...]], axis=1))
    q = ((both[:, 0:128] + bias_ref[0]) * 0.125).astype(BF)
    k = both[:, 128:256].astype(BF)
    v = (mm(rows[...], vw_ref[...]) + bias_ref[1]).astype(BF)
    q_ref[...] = q
    v_ref[...] = v[0:seq]
    q_t = q.astype(F32).T.astype(BF)
    k = k.astype(F32)
    kt_ref[...] = k.T[:, 0:seq].astype(BF)
    v_t = v.astype(F32).T[:, 0:seq].astype(BF)
    lane = lax.broadcasted_iota(jnp.int32, (seq, 128), 1)
    contexts = []
    for h in range(2):
        mine = (lane < 64) if h == 0 else (lane >= 64)
        own, other = (320, 384) if h == 0 else (384, 320)
        keys[:, 320:448] = jnp.where(mine, k[0:seq], mask_ref[...].astype(F32)).astype(BF)
        queries[own : own + 64, :] = q_t[h * 64 : h * 64 + 64, :]
        queries[other : other + 64, :] = jnp.ones((64, lanes), BF)
        values[0:64, :] = v_t[h * 64 : h * 64 + 64, :]
        queries[0:64, :] = mm(line_ref[h], hott_ref[0:64, :]).astype(BF)
        queries[64:192, :] = mm(width_ref[h], hott_ref[64:192, :]).astype(BF)
        queries[192:320, :] = mm(height_ref[h], hott_ref[192:320, :]).astype(BF)
        scores = mm(keys[...], queries[...])
        peak = jnp.max(scores, axis=0, keepdims=True)
        weights = jnp.exp(scores - peak).astype(BF)
        exp_ref[h] = weights
        ctx = mm(values[...], weights)
        inverse = 1.0 / ctx[64:65]
        inv_ref[h] = inverse
        contexts.append(ctx[0:64] * inverse)
    ctx = jnp.concatenate(contexts, axis=0)
    ctxt_ref[...] = ctx.astype(BF)
    ctx_ref[...] = ctx.T[0:seq].astype(BF)


def attend(pieces, q_weight, k_weight, v_weight, bias, hot, mask, hot_t, line, width, height):
    seq = mask.shape[0]
    lanes, dim = hot.shape[0], q_weight.shape[0]

    def whole(a):
        return pl.BlockSpec(a.shape, lambda p: (0,) * a.ndim, pipeline_mode=pl.Buffered(1))

    def pair(a):
        return pl.BlockSpec((2,) + a.shape[1:], lambda p: (p, 0, 0))

    def columns(rows):
        return pl.BlockSpec((rows, 128), lambda p: (0, p))

    def rows(length):
        return pl.BlockSpec((128, length), lambda p: (p, 0))

    shape = jax.ShapeDtypeStruct
    return pl.pallas_call(
        partial(attend_kernel, len(pieces)),
        grid=(HEADS // 2,),
        in_specs=[whole(a) for a in pieces]
        + [
            columns(dim),
            columns(dim),
            columns(dim),
            pl.BlockSpec((2, 1, 128), lambda p: (0, 0, p)),
            whole(hot),
            whole(mask),
            whole(hot_t),
            pair(line),
            pair(width),
            pair(height),
        ],
        out_specs=[
            pl.BlockSpec((2, seq, lanes), lambda p: (p, 0, 0)),
            rows(lanes),
            columns(seq),
            pl.BlockSpec((2, 1, lanes), lambda p: (p, 0, 0)),
            columns(lanes),
            rows(seq),
            columns(seq),
            pl.BlockSpec((seq, dim), lambda p: (0, 0)),
        ],
        out_shape=[
            shape((HEADS, seq, lanes), BF),
            shape((dim, lanes), BF),
            shape((seq, dim), BF),
            shape((HEADS, 1, lanes), F32),
            shape((lanes, dim), BF),
            shape((dim, seq), BF),
            shape((seq, dim), BF),
            shape((seq, dim), BF),
        ],
        scratch_shapes=[
            pltpu.VMEM((seq, 448), BF),
            pltpu.VMEM((448, lanes), BF),
            pltpu.VMEM((80, seq), BF),
            pltpu.VMEM((lanes, dim), BF),
        ],
        compiler_params=pltpu.CompilerParams(vmem_limit_bytes=VMEM_BYTES),
        cost_estimate=pl.CostEstimate(
            flops=HEADS * seq * lanes * 4096, bytes_accessed=HEADS * seq * lanes * 2,
            transcendentals=HEADS * seq * lanes,
        ),
    )(*pieces, q_weight, k_weight, v_weight, bias, hot, mask, hot_t, line, width, height)


def attend_back_kernel(held, *refs):
    (
        exp_ref, ctxt_ref, inv_ref, v_ref, kt_ref, q_ref, dattn_ref, outw_ref, hot_ref, hott_ref,
        dqkv_ref, gwidth_ref, gheight_ref, gline_ref, values, dctx, lefts, rights, ds, dattn,
    ) = refs[:10] + refs[10 + held :]
    seq = v_ref.shape[0]
    lanes = q_ref.shape[0]

    @pl.when(pl.program_id(0) == 0)
    def _():
        for h in range(2):
            lefts[h, 64:192, :] = hott_ref[64:192, 0:seq]
            rights[h, :, 128:256] = hot_ref[:, 192:320]
        dattn[0:seq, :] = dattn_ref[...]
        dattn[seq:lanes, :] = jnp.zeros((lanes - seq, dattn.shape[1]), BF)

    lane = lax.broadcasted_iota(jnp.int32, (seq, 128), 1)
    query_lane = lax.broadcasted_iota(jnp.int32, (lanes, 128), 1)
    row = lax.broadcasted_iota(jnp.int32, (64, lanes), 0)
    line_hot = jnp.concatenate([hot_ref[:, 0:64], hot_ref[:, 0:64]], axis=1).astype(F32)
    d_rows_t = against(outw_ref[...], dattn[...])
    d_rows_t = [d_rows_t[h * 64 : h * 64 + 64] * inv_ref[h] for h in range(2)]
    d_rows = jnp.concatenate(d_rows_t, axis=0).T.astype(BF)
    results = []
    by_queries = []
    for h in range(2):
        mine = (lane < 64) if h == 0 else (lane >= 64)
        query_mine = (query_lane < 64) if h == 0 else (query_lane >= 64)
        own, other = (0, 64) if h == 0 else (64, 0)
        part = slice(h * 64, h * 64 + 64)
        values[h] = jnp.where(mine, v_ref[...].astype(F32), 1.0).astype(BF)
        delta = -jnp.sum(d_rows_t[h] * ctxt_ref[part, :].astype(F32), axis=0, keepdims=True)
        high = delta.astype(BF).astype(F32)
        extra = jnp.where(row == 0, high, jnp.where(row == 1, delta - high, 0.0))
        dctx[h, own : own + 64, :] = d_rows_t[h].astype(BF)
        dctx[h, other : other + 64, :] = extra.astype(BF)
        lefts[h, 0:64, :] = kt_ref[part, :]
        rights[h, :, 0:128] = jnp.where(query_mine, q_ref[...].astype(F32), line_hot).astype(BF)
        d_scores = mm(values[h], dctx[h])
        ds[h] = (exp_ref[h].astype(F32) * d_scores).astype(BF)
        by_query = mm(lefts[h], ds[h])
        by_queries.append(by_query[0:64] * 0.125)
        gwidth_ref[h] = mm(by_query[64:192].astype(BF), hot_ref[:, 64:192])
        by_key = mm(ds[h], rights[h])
        near = mm(hott_ref[0:64, 0:seq], by_key[:, 0:128].astype(BF))
        gline_ref[h] = near[:, 64:128] if h == 0 else near[:, 0:64]
        gheight_ref[h] = mm(hott_ref[192:320, 0:seq], by_key[:, 128:256].astype(BF))
        results.append((by_key[:, 0:128], mm(exp_ref[h], d_rows)))
    dqkv_ref[0] = jnp.concatenate(by_queries, axis=0).T[0:seq].astype(BF)
    dqkv_ref[1] = jnp.where(lane < 64, results[0][0], results[1][0]).astype(BF)
    dqkv_ref[2] = jnp.where(lane < 64, results[0][1], results[1][1]).astype(BF)


def attend_back(first, pairs, held, exps, ctx_t, inverse, v, k_t, q, d_attn, out_weight, hot, hot_t):
    seq, dim = v.shape
    lanes = q.shape[0]

    def whole(a):
        return pl.BlockSpec(a.shape, lambda p: (0,) * a.ndim, pipeline_mode=pl.Buffered(1))

    def columns(rows):
        return pl.BlockSpec((rows, 128), lambda p: (0, p + first))

    def rows(length):
        return pl.BlockSpec((128, length), lambda p: (p + first, 0))

    def pair(*shape, start=first):
        return pl.BlockSpec((2,) + shape, lambda p: (p + start, 0, 0))

    shape = jax.ShapeDtypeStruct
    return pl.pallas_call(
        partial(attend_back_kernel, len(held)),
        grid=(pairs,),
        in_specs=[
            pair(seq, lanes),
            rows(lanes),
            pair(1, lanes),
            columns(seq),
            rows(seq),
            columns(lanes),
            whole(d_attn),
            rows(dim),
            whole(hot),
            whole(hot_t),
        ]
        + [pl.BlockSpec(memory_space=pl.ANY)] * len(held),
        out_specs=[
            pl.BlockSpec((3, seq, 128), lambda p: (0, 0, p)),
            pair(128, 128, start=0),
            pair(128, 128, start=0),
            pair(64, 64, start=0),
        ],
        out_shape=[
            shape((3, seq, 128 * pairs), BF),
            shape((2 * pairs, 128, 128), F32),
            shape((2 * pairs, 128, 128), F32),
            shape((2 * pairs, 64, 64), F32),
        ],
        scratch_shapes=[
            pltpu.VMEM((2, seq, 128), BF),
            pltpu.VMEM((2, 128, lanes), BF),
            pltpu.VMEM((2, 192, seq), BF),
            pltpu.VMEM((2, lanes, 256), BF),
            pltpu.VMEM((2, seq, lanes), BF),
            pltpu.VMEM((lanes, dim), BF),
        ],
        compiler_params=pltpu.CompilerParams(vmem_limit_bytes=VMEM_BYTES),
        cost_estimate=pl.CostEstimate(
            flops=2 * pairs * seq * lanes * 4096, bytes_accessed=4 * pairs * seq * lanes,
            transcendentals=0,
        ),
    )(exps, ctx_t, inverse, v, k_t, q, d_attn, out_weight, hot, hot_t, *held)


def gelu_pair(x):
    bell = jnp.exp(x * x * -0.5)
    t = 1.0 / (1.0 + 0.23164189 * jnp.abs(x))
    poly = t * (0.127414796 + t * (-0.142248368 + t * (0.7107068705 + t * (-0.7265760135 + t * 0.5307027145))))
    upper = poly * bell
    phi = jnp.where(x < 0, upper, 1.0 - upper)
    return x * phi, phi + x * bell * 0.3989422804014327

def normalise(rows):
    mean = jnp.mean(rows, axis=-1, keepdims=True)
    centred = rows - mean
    scale = lax.rsqrt(jnp.mean(centred * centred, axis=-1, keepdims=True) + 1e-05)
    return centred * scale, scale

def normalise_back(hat, scale, d_hat):
    return scale * (d_hat - jnp.mean(d_hat, axis=-1, keepdims=True) - hat * jnp.mean(d_hat * hat, axis=-1, keepdims=True))

def total(rows):
    return jnp.sum(rows, axis=0, keepdims=True)


def rows_kernel(count, blocks, *refs):
    pieces = refs[:count]
    (
        x_ref, ctx_ref, ctxt_ref, out_w, up_w, down_w, bias_ref, up_b,
        final_ref, dmid_ref, dattn_ref, up_ref, down_ref, out_ref, sums_ref, upsum_ref,
        slope, cots, lows, acts, d_branches, d_pres, lows_t, d_attns,
    ) = refs[count:]
    step = pl.program_id(0)
    block = x_ref.shape[0]
    seq, dim = cots.shape
    parts = acts.shape[0]

    @pl.when(step == 0)
    def _():
        sums_ref[...] = jnp.zeros_like(sums_ref)
        upsum_ref[...] = jnp.zeros_like(upsum_ref)
        assemble(pieces, cots)

    @pl.when(step < blocks)
    def _():
        here = pl.ds(pl.multiple_of(step * block, 16), block)
        attn = mm(ctx_ref[...], out_w[...]) + bias_ref[0:1]
        hat, scale = normalise(x_ref[...].astype(F32) + attn)
        normed = hat * bias_ref[1:2] + bias_ref[2:3]
        low = normed.astype(BF)
        lows[here, :] = low
        branch = bias_ref[3:4]
        for n in range(parts):
            part = slice(n * dim, (n + 1) * dim)
            act, grad = gelu_pair(mm(low, up_w[:, part]) + up_b[:, part])
            slope[:, part] = grad
            act = act.astype(BF)
            acts[n, here, :] = act
            branch = branch + mm(act, down_w[part, :])
        final_hat, final_scale = normalise(normed + branch)
        final_ref[...] = (final_hat * bias_ref[4:5] + bias_ref[5:6]).astype(BF)
        cot = cots[here, :].astype(F32)
        d_sum = normalise_back(final_hat, final_scale, cot * bias_ref[4:5])
        d_branch = d_sum.astype(BF)
        d_branches[here, :] = d_branch
        d_normed = d_sum
        for n in range(parts):
            part = slice(n * dim, (n + 1) * dim)
            d_pre = (against(d_branch, down_w[part, :]) * slope[:, part]).astype(BF)
            d_pres[n, here, :] = d_pre
            upsum_ref[:, part] += total(d_pre.astype(F32))
            d_normed = d_normed + against(d_pre, up_w[:, part])
        d_mid = normalise_back(hat, scale, d_normed * bias_ref[1:2])
        dmid_ref[...] = d_mid
        d_attn = d_mid.astype(BF)
        dattn_ref[...] = d_attn
        d_attns[here, :] = d_attn
        sums_ref[...] += jnp.concatenate(
            [
                total(d_attn.astype(F32)),
                total(d_normed * hat),
                total(d_normed),
                total(d_branch.astype(F32)),
                total(cot * final_hat),
                total(cot),
                jnp.zeros((2, dim), F32),
            ],
            axis=0,
        )

    @pl.when(step == blocks)
    def _():
        lows_t[...] = lows[...].astype(F32).T.astype(BF)

    @pl.when((step >= blocks) & (step < blocks + parts))
    def _():
        n = step - blocks
        down_ref[...] = inner(acts[n], d_branches[...]).astype(BF)
        up_ref[...] = mm(lows_t[...], d_pres[n]).astype(BF)

    @pl.when(step == blocks + parts)
    def _():
        out_ref[...] = mm(ctxt_ref[:, 0:seq], d_attns[...]).astype(BF)


def rows_pass(room, pieces, x, ctx, ctx_t, out_w, up_w, down_w, bias, up_b):
    seq, dim = ctx.shape
    ff = up_w.shape[1]
    blocks = 4
    block = seq // blocks
    parts = ff // dim

    def row(width):
        return pl.BlockSpec((block, width), lambda p: (jnp.minimum(p, blocks - 1), 0))

    def whole(a):
        return pl.BlockSpec(a.shape, lambda p: (0,) * a.ndim, pipeline_mode=pl.Buffered(1))

    def part(p):
        return jnp.clip(p - blocks, 0, parts - 1)

    shape = jax.ShapeDtypeStruct
    return pl.pallas_call(
        partial(rows_kernel, len(pieces), blocks),
        grid=(blocks + parts + 1,),
        in_specs=[whole(a) for a in pieces]
        + [row(dim), row(dim)]
        + [whole(a) for a in (ctx_t, out_w, up_w, down_w, bias, up_b)],
        out_specs=[
            row(dim),
            row(dim),
            row(dim),
            pl.BlockSpec((dim, dim), lambda p: (0, part(p))),
            pl.BlockSpec((dim, dim), lambda p: (part(p), 0)),
            pl.BlockSpec((dim, dim), lambda p: (0, 0)),
            pl.BlockSpec((8, dim), lambda p: (0, 0)),
            pl.BlockSpec((1, ff), lambda p: (0, 0)),
        ],
        out_shape=[
            shape((seq, dim), BF),
            shape((seq, dim), F32),
            shape((seq, dim), BF),
            shape((dim, ff), BF),
            shape((ff, dim), BF),
            shape((dim + room, dim), BF),
            shape((8, dim), F32),
            shape((1, ff), F32),
        ],
        scratch_shapes=[
            pltpu.VMEM((block, ff), F32),
            pltpu.VMEM((seq, dim), BF),
            pltpu.VMEM((seq, dim), BF),
            pltpu.VMEM((parts, seq, dim), BF),
            pltpu.VMEM((seq, dim), BF),
            pltpu.VMEM((parts, seq, dim), BF),
            pltpu.VMEM((dim, seq), BF),
            pltpu.VMEM((seq, dim), BF),
        ],
        compiler_params=pltpu.CompilerParams(vmem_limit_bytes=VMEM_BYTES),
        cost_estimate=pl.CostEstimate(
            flops=56 * seq * dim * dim, bytes_accessed=64 * seq * dim, transcendentals=seq * ff
        ),
    )(*pieces, x, ctx, ctx_t, out_w, up_w, down_w, bias, up_b)


def last_kernel(count, held, *refs):
    parts = refs[:count]
    x_ref, weight_ref, dmid_ref = refs[count : count + 3]
    grad_ref, drows_ref, sums_ref, x_t, total = refs[count + 3 + held :]
    step = pl.program_id(0)
    d_qkv = jnp.concatenate([part[0] for part in parts], axis=1)

    @pl.when(step == 0)
    def _():
        x_t[...] = x_ref[...].astype(F32).T.astype(BF)
        total[...] = dmid_ref[...]

    grad_ref[...] = mm(x_t[...], d_qkv).astype(BF)
    total[...] += against(d_qkv, weight_ref[0])
    sums_ref[0] = jnp.broadcast_to(
        jnp.sum(d_qkv.astype(F32), axis=0, keepdims=True), sums_ref.shape[1:]
    )

    @pl.when(step == 2)
    def _():
        drows_ref[...] = total[...].astype(BF)


def last_products(rows, held, x, d_qkv, weights, d_mid):
    seq, dim = d_mid.shape

    def whole(a):
        return pl.BlockSpec(a.shape, lambda p: (0,) * a.ndim, pipeline_mode=pl.Buffered(1))

    shape = jax.ShapeDtypeStruct
    return pl.pallas_call(
        partial(last_kernel, len(d_qkv), len(held)),
        grid=(3,),
        in_specs=[pl.BlockSpec((1,) + a.shape[1:], lambda p: (p, 0, 0)) for a in d_qkv]
        + [
            whole(x),
            pl.BlockSpec((1, dim, dim), lambda p: (p, 0, 0)),
            whole(d_mid),
        ]
        + [pl.BlockSpec(memory_space=pl.ANY)] * len(held),
        out_specs=[
            pl.BlockSpec((dim, dim), lambda p: (p, 0)),
            pl.BlockSpec((seq, dim), lambda p: (0, 0)),
            pl.BlockSpec((1, 8, dim), lambda p: (p, 0, 0)),
        ],
        out_shape=[shape((rows, dim), BF), shape((seq, dim), BF), shape((3, 8, dim), F32)],
        scratch_shapes=[pltpu.VMEM((dim, seq), BF), pltpu.VMEM((seq, dim), F32)],
        compiler_params=pltpu.CompilerParams(vmem_limit_bytes=VMEM_BYTES),
        cost_estimate=pl.CostEstimate(
            flops=12 * seq * dim * dim, bytes_accessed=32 * seq * dim, transcendentals=0
        ),
    )(*d_qkv, x, weights, d_mid, *held)


def bucket_select(table):
    reach = (table.shape[0] - 1) // 2
    spots = jnp.arange(4 * reach, dtype=jnp.int32)
    bucket = jnp.clip(spots[None, :] - spots[:, None], -reach, reach) + reach
    return bucket[None] == jnp.arange(2 * reach + 1, dtype=jnp.int32)[:, None, None]


def spread_table(table):
    span = 2 * (table.shape[0] - 1)
    spread = lax.dot_general(
        table.astype(BF),
        bucket_select(table).astype(BF).reshape(table.shape[0], -1),
        (((0,), (0,)), ((), ())),
        preferred_element_type=F32,
    )
    return spread.astype(BF).reshape(HEADS, span, span)


def gather_table(parts, table):
    select = bucket_select(table).astype(F32).reshape(table.shape[0], -1)
    return jnp.concatenate(
        [
            lax.dot_general(
                select,
                grads.reshape(grads.shape[0], -1),
                (((1,), (1,)), ((), ())),
                precision=lax.Precision.HIGHEST,
                preferred_element_type=F32,
            )
            for grads in parts
        ],
        axis=1,
    )


def shift_pairs(size, step):
    return [(i, (i + step) % size) for i in range(size)]


def flip_pairs(size, step):
    return [(i, i ^ step) for i in range(size)]


def pick(array, index):
    return lax.dynamic_index_in_dim(array, index, 0, keepdims=False)


def swap_text(parts):
    return lax.all_to_all(parts, "wide", split_axis=0, concat_axis=0, tiled=True)


def patch_order(size):
    me = lax.axis_index("narrow")
    return [me ^ k for k in range(size)]


def swap_patch(parts):
    size = parts.shape[0]
    me = lax.axis_index("narrow")
    return [pick(parts, me)] + [
        lax.ppermute(pick(parts, me ^ k), "narrow", flip_pairs(size, k)) for k in range(1, size)
    ]


def flip_axis(array, axis, bit):
    return jnp.where(bit == 1, jnp.flip(array, axis), array)


def from_flipped(parts, me):
    size = parts.shape[0]
    bits = size.bit_length() - 1
    parts = parts.reshape((2,) * bits + parts.shape[1:])
    for b in range(bits):
        parts = flip_axis(parts, bits - 1 - b, (me >> b) & 1)
    return parts.reshape((size,) + parts.shape[bits:])


def patch_away(rows, size):
    me = lax.axis_index("narrow")
    parts = rows.reshape(size, -1, rows.shape[1])
    arrived = [parts[0]] + [
        lax.ppermute(parts[k], "narrow", flip_pairs(size, k)) for k in range(1, size)
    ]
    return from_flipped(jnp.stack(arrived), me)


def add(*terms):
    total = terms[0].astype(F32)
    for term in terms[1:]:
        total = total + term.astype(F32)
    return total.astype(BF)


def wide_orders(wide, ways):
    bits = list(range(1, wide.bit_length() - 1))
    return [bits, bits[::-1]][:ways]


def wide_bit(bit):
    return (lax.axis_index("wide") >> bit) & 1


def add_kernel(me_ref, own_ref, arrived_ref, *refs):
    refs[-1][...] = (own_ref[0].astype(F32) + arrived_ref[...].astype(F32)).astype(BF)


def add_own(parts, me, arrived, held):
    rows, columns = arrived.shape
    steps = 2 if rows % 32 == 0 else 1
    block = rows // steps
    return pl.pallas_call(
        add_kernel,
        grid_spec=pltpu.PrefetchScalarGridSpec(
            num_scalar_prefetch=1,
            grid=(steps,),
            in_specs=[
                pl.BlockSpec((1, block, columns), lambda i, me_ref: (me_ref[0], i, 0)),
                pl.BlockSpec((block, columns), lambda i, me_ref: (i, 0)),
            ]
            + [pl.BlockSpec(memory_space=pl.ANY)] * len(held),
            out_specs=pl.BlockSpec((block, columns), lambda i, me_ref: (i, 0)),
        ),
        out_shape=jax.ShapeDtypeStruct((rows, columns), BF),
        compiler_params=pltpu.CompilerParams(vmem_limit_bytes=VMEM_BYTES),
        cost_estimate=pl.CostEstimate(flops=0, bytes_accessed=6 * rows * columns, transcendentals=0),
    )(me.reshape(1), parts, arrived, *held)


def wide_step(grad, wide, bit, held=()):
    parts = grad.reshape(2, -1, grad.shape[1])
    me = wide_bit(bit)
    arrived = lax.ppermute(pick(parts, 1 - me), "wide", flip_pairs(wide, 1 << bit))
    return add_own(parts, me, arrived, held) if held else add(pick(parts, me), arrived)


def cut(grad, ways):
    part = grad.shape[0] // ways
    return [grad[i * part : (i + 1) * part] for i in range(ways)]


def wide_steps(shares, wide, i, held=()):
    orders = wide_orders(wide, len(shares))
    return [
        wide_step(a, wide, order[i], held if n == 0 else ())
        for n, (a, order) in enumerate(zip(shares, orders))
    ]


def narrow_step(shares, narrow):
    me = lax.axis_index("narrow")
    parts = [a.reshape(narrow, -1, a.shape[1]) for a in shares]

    def picked(index):
        return jnp.stack([pick(a, index) for a in parts])

    arrived = [
        lax.ppermute(picked(me ^ k), "narrow", flip_pairs(narrow, k)) for k in range(1, narrow)
    ]
    return add(picked(me), *arrived)


def gather_narrow(part, narrow):
    parts = [part] + [
        lax.ppermute(part, "narrow", flip_pairs(narrow, k)) for k in range(1, narrow)
    ]
    return [jnp.stack([p[n] for p in parts]) for n in range(part.shape[0])]


def gather_wide(shares, wide, i):
    return [
        jnp.concatenate([a, lax.ppermute(a, "wide", flip_pairs(wide, 1 << order[i]))], axis=0)
        for a, order in zip(shares, wide_orders(wide, len(shares)))
    ]


def gather_core(shares, wide):
    return shares + [lax.ppermute(a, "wide", flip_pairs(wide, 1)) for a in shares]


def convert_kernel(up_ref, down_ref, out_ref, after_ref, up_out, down_out, out_out):
    step = pl.program_id(0)
    parts = (pl.num_programs(0) - 1) // 2

    @pl.when(step < parts)
    def _():
        up_out[...] = up_ref[...].astype(F32)

    @pl.when((step >= parts) & (step < 2 * parts))
    def _():
        down_out[...] = down_ref[...].astype(F32)

    @pl.when(step == 2 * parts)
    def _():
        out_out[...] = out_ref[...].astype(F32)


def convert(up_total, down_total, out_total, after):
    dim, ff = up_total.shape
    parts = ff // dim

    def block(index):
        return pl.BlockSpec((dim, dim), index)

    up_block = block(lambda p: (0, jnp.minimum(p, parts - 1)))
    down_block = block(lambda p: (jnp.clip(p - parts, 0, parts - 1), 0))
    out_block = block(lambda p: (0, 0))
    shape = jax.ShapeDtypeStruct
    return pl.pallas_call(
        convert_kernel,
        grid=(2 * parts + 1,),
        in_specs=[up_block, down_block, out_block, pl.BlockSpec(memory_space=pl.ANY)],
        out_specs=[up_block, down_block, out_block],
        out_shape=[shape((dim, ff), F32), shape((ff, dim), F32), shape((dim, dim), F32)],
        compiler_params=pltpu.CompilerParams(vmem_limit_bytes=VMEM_BYTES),
        cost_estimate=pl.CostEstimate(flops=0, bytes_accessed=13 * dim * ff, transcendentals=0),
    )(up_total, down_total, out_total, after)


def finish_kernel(places, ways, cuts, index_ref, *refs):
    pieces, outs = refs[: 2 * ways], refs[2 * ways :]
    rows = pieces[0].shape[1]
    for core in range(2):
        for way in range(ways):
            for place in range(places):
                at = ((core * ways + way) * places + place) * rows
                if at >= cuts[-1][1]:
                    continue
                here = index_ref[way, place]
                same = pieces[way][here].astype(F32)
                other = pieces[ways + way][here].astype(F32)
                block = jnp.where(index_ref[2, 0] == core, same, other)
                for (start, stop), out in zip(cuts, outs):
                    low, high = max(at, start), min(at + rows, stop)
                    if low < high:
                        out[low - start : high - start, :] = block[low - at : high - at]


def finish(pieces, wide, narrow, lengths):
    places, _, columns = pieces[0].shape
    ways = len(pieces) // 2
    index = []
    for order in wide_orders(wide, 2):
        me = jnp.int32(0)
        for bit in order:
            me = me * 2 + wide_bit(bit)
        me = me * narrow + lax.axis_index("narrow")
        index.append(jnp.arange(places, dtype=jnp.int32) ^ me)
    index.append(jnp.full((places,), wide_bit(0), jnp.int32))
    cuts = []
    for length in lengths:
        start = cuts[-1][1] if cuts else 0
        cuts.append((start, start + length))
    return pl.pallas_call(
        partial(finish_kernel, places, ways, cuts),
        in_specs=[pl.BlockSpec(memory_space=pltpu.SMEM)]
        + [pl.BlockSpec(memory_space=pltpu.VMEM)] * len(pieces),
        out_specs=[pl.BlockSpec(memory_space=pltpu.VMEM)] * len(lengths),
        out_shape=[jax.ShapeDtypeStruct((length, columns), F32) for length in lengths],
        compiler_params=pltpu.CompilerParams(vmem_limit_bytes=VMEM_BYTES),
        cost_estimate=pl.CostEstimate(
            flops=0, bytes_accessed=8 * sum(lengths) * columns, transcendentals=0
        ),
    )(jnp.stack(index), *pieces)


def room_for(rows, wide, narrow):
    return 16 + -(rows + 16) % (8 * wide * narrow)


def pack(grads, columns, rows):
    lines = []
    for grad in grads:
        flat = grad.reshape(-1)
        lines.append(jnp.pad(flat, (0, -flat.shape[0] % columns)).reshape(-1, columns))
    lines = jnp.concatenate(lines, axis=0)
    return jnp.pad(lines, ((0, -lines.shape[0] % rows), (0, 0)))


def unpack(lines, grads):
    columns = lines.shape[1]
    at = 0
    out = []
    for grad in grads:
        count = -(-grad.size // columns)
        out.append(lines[at : at + count].reshape(-1)[: grad.size].reshape(grad.shape))
        at += count
    return out


def body(
    text_in,
    patch_in,
    res_class,
    text_len,
    pos_line,
    pos_x,
    pos_y,
    query_weight,
    query_bias,
    key_weight,
    value_weight,
    value_bias,
    output_weight,
    output_bias,
    norm_gain,
    norm_shift,
    up_weight,
    up_bias,
    down_weight,
    down_bias,
    final_gain,
    final_shift,
    line_table,
    width_table,
    height_table,
    cot_text,
    cot_patch,
):
    text_shape = text_in.shape
    patch_shape = patch_in.shape
    dim = text_shape[3]
    seq = TEXT + PATCH
    lanes = -(-seq // 128) * 128
    wide = text_shape[0]
    narrow = patch_shape[1]
    pieces = [swap_text(text_in.reshape(wide, -1, dim)).reshape(-1, dim)]
    pieces += swap_patch(patch_in.reshape(narrow, -1, dim))
    cot_text, pieces[0] = lax.optimization_barrier((cot_text, pieces[0]))
    cot_patch, pieces = lax.optimization_barrier((cot_patch, pieces))
    cots = [swap_text(cot_text.reshape(wide, -1, dim)).reshape(-1, dim)]
    cots += swap_patch(cot_patch.reshape(narrow, -1, dim))
    index = jnp.arange(seq, dtype=jnp.int32)
    live_patch = jnp.where(res_class.reshape(()) == 1, PATCH, SMALL_PATCH)
    valid = jnp.where(index < TEXT, index < text_len.reshape(()), index - TEXT < live_patch)
    facts = jnp.concatenate(
        [pos_line.reshape(1, -1), pos_x.reshape(1, -1), pos_y.reshape(1, -1), valid.astype(jnp.int32)[None]]
    )
    patch_facts = facts[:, TEXT:].reshape(4, narrow, -1)
    facts = jnp.concatenate(
        [facts[:, :TEXT]]
        + [
            lax.dynamic_index_in_dim(patch_facts, i, 1, keepdims=False)
            for i in patch_order(narrow)
        ],
        axis=1,
    )
    line_spots, x_spots, y_spots = facts[0], facts[1], facts[2]
    valid = facts[3] == 1

    line = spread_table(line_table)
    width = spread_table(width_table)
    height = spread_table(height_table)
    hots = []
    hots_t = []
    for spots, table in ((line_spots, line_table), (x_spots, width_table), (y_spots, height_table)):
        span = jnp.arange(2 * (table.shape[0] - 1), dtype=jnp.int32)
        long = jnp.pad(spots, (0, lanes - seq), constant_values=-1)
        hots.append((long[:, None] == span[None, :]).astype(BF))
        hots_t.append((long[None, :] == span[:, None]).astype(BF))
    hot = jnp.concatenate(hots, axis=1)
    hot_t = jnp.concatenate(hots_t, axis=0)
    column = jnp.arange(128, dtype=jnp.int32)
    mask = jnp.where((column[None, :] % 64 == 0) & ~valid[:, None], -1e30, 0.0).astype(BF)

    exps, ctx_t, ctx, inverse, q, k_t, v, rows_in = attend(
        pieces,
        query_weight,
        key_weight,
        value_weight,
        jnp.stack([query_bias, value_bias])[:, None],
        hot,
        mask,
        hot_t,
        line,
        width,
        height,
    )
    vectors = jnp.stack(
        [output_bias, norm_gain, norm_shift, down_bias, final_gain, final_shift] + [final_shift] * 2
    )
    room = 16
    final_low, d_mid, d_attn, up_low, down_low, out_low, sums, up_sum = rows_pass(
        room, cots, rows_in, ctx, ctx_t, output_weight, up_weight, down_weight, vectors, up_bias[None]
    )
    early = (sums[0], sums[1], sums[2], up_sum, sums[3], sums[4], sums[5])
    out_low = lax.dynamic_update_slice(out_low, pack(early, dim, room).astype(BF), (dim, 0))
    down_total, up_total, out_total = lax.psum((down_low, up_low, out_low), ("wide", "narrow"))
    qkv_weight = jnp.stack([query_weight, key_weight, value_weight])

    def backward():
        text_out = swap_text(final_low[:TEXT].reshape(wide, -1, dim)).reshape(text_shape)
        patch_out = patch_away(final_low[TEXT:], narrow).reshape(patch_shape)
        levels = wide.bit_length() - 2
        d_qkv, g_width, g_height, g_line = attend_back(
            0, HEADS // 2, [], exps, ctx_t, inverse, v, k_t, q, d_attn, output_weight, hot, hot_t
        )
        late_room = room_for(3 * dim, wide, narrow)
        tail, d_rows, qkv_sums = last_products(
            3 * dim + late_room, [text_out, patch_out], rows_in, [d_qkv], qkv_weight, d_mid
        )
        text_grad = swap_text(d_rows[:TEXT].reshape(wide, -1, dim)).reshape(text_shape)
        patch_grad = patch_away(d_rows[TEXT:], narrow).reshape(patch_shape)
        late = (
            qkv_sums[0, 0],
            qkv_sums[2, 0],
            gather_table([g_line], line_table),
            gather_table([g_width], width_table),
            gather_table([g_height], height_table),
        )
        small = pack(late, dim, late_room).astype(BF)
        tail = lax.dynamic_update_slice(tail, small, (3 * dim, 0))
        halves = cut(wide_step(tail, wide, 0), 2)
        for i in range(levels):
            moved = [text_grad, patch_grad] if i == levels - 1 else []
            halves = wide_steps(halves, wide, i, moved)
        halves = gather_narrow(narrow_step(halves, narrow), narrow)
        for i in range(levels - 1, -1, -1):
            halves = gather_wide(halves, wide, i)
        *large, late_small = finish(gather_core(halves, wide), wide, narrow, (dim,) * 3 + (16,))
        return (
            text_out, patch_out, text_grad, patch_grad, *large, *unpack(late_small, late),
        )

    def never():
        return jax.tree.map(lambda a: jnp.zeros(a.shape, a.dtype), jax.eval_shape(backward))

    (
        text_out, patch_out, text_grad, patch_grad, query_weight_grad, key_weight_grad,
        value_weight_grad, query_bias_grad, value_bias_grad, line_table_grad, width_table_grad,
        height_table_grad,
    ) = lax.cond(text_len.reshape(()) >= 0, backward, never)
    up_weight_grad, down_weight_grad, output_weight_grad = convert(
        up_total, down_total, out_total, value_weight_grad
    )
    (
        output_bias_grad,
        norm_gain_grad,
        norm_shift_grad,
        up_bias_grad,
        down_bias_grad,
        final_gain_grad,
        final_shift_grad,
    ) = unpack(out_total[dim:].astype(F32), early)
    up_bias_grad = up_bias_grad.reshape(-1)
    return (
        text_out,
        patch_out,
        text_grad,
        patch_grad,
        query_weight_grad,
        query_bias_grad,
        key_weight_grad,
        value_weight_grad,
        value_bias_grad,
        output_weight_grad,
        output_bias_grad,
        norm_gain_grad,
        norm_shift_grad,
        up_weight_grad,
        up_bias_grad,
        down_weight_grad,
        down_bias_grad,
        final_gain_grad,
        final_shift_grad,
        line_table_grad,
        width_table_grad,
        height_table_grad,
    )


def solution(mesh):
    text = P(None, "narrow", "wide", None)
    patch = P("wide", None, "narrow", None)
    page = P("wide", "narrow")
    spots = P("wide", "narrow", None)
    in_specs = (text, patch, page, page, spots, spots, spots) + (P(),) * 18 + (text, patch)
    out_specs = (text, patch, text, patch) + (P(),) * 18
    return jax.shard_map(body, mesh=mesh, in_specs=in_specs, out_specs=out_specs, check_vma=False)
```

```python
from functools import partial

import jax
import jax.numpy as jnp
from jax import lax
from jax.experimental import pallas as pl
from jax.experimental.pallas import tpu as pltpu
from jax.sharding import PartitionSpec as P

HEADS = 12
TEXT = 512
PATCH = 576
SMALL_PATCH = 196
BF = jnp.bfloat16
F32 = jnp.float32
VMEM_BYTES = 60 * 2**20


def mm(left, right):
    return lax.dot_general(left, right, (((1,), (0,)), ((), ())), preferred_element_type=F32)


def inner(left, right):
    return lax.dot_general(left, right, (((0,), (0,)), ((), ())), preferred_element_type=F32)


def against(left, right):
    return lax.dot_general(left, right, (((1,), (1,)), ((), ())), preferred_element_type=F32)


def assemble(pieces, rows):
    at = 0
    for piece in pieces:
        rows[at : at + piece.shape[0], :] = piece[...]
        at += piece.shape[0]


def attend_kernel(count, *refs):
    pieces = refs[:count]
    (
        qw_ref, kw_ref, vw_ref, bias_ref, hot_ref, mask_ref, hott_ref, line_ref, width_ref,
        height_ref, exp_ref, ctxt_ref, ctx_ref, inv_ref, q_ref, kt_ref, v_ref, x_ref,
        keys, queries, values, rows,
    ) = refs[count:]
    seq = v_ref.shape[0]
    lanes = rows.shape[0]

    @pl.when(pl.program_id(0) == 0)
    def _():
        keys[:, 0:320] = hot_ref[0:seq, :]
        values[64:80, :] = jnp.ones((16, seq), BF)
        assemble(pieces, rows)
        rows[seq:lanes, :] = jnp.zeros((lanes - seq, rows.shape[1]), BF)
        x_ref[...] = rows[0:seq, :]

    both = mm(rows[...], jnp.concatenate([qw_ref[...], kw_ref[...]], axis=1))
    q = ((both[:, 0:128] + bias_ref[0]) * 0.125).astype(BF)
    k = both[:, 128:256].astype(BF)
    v = (mm(rows[...], vw_ref[...]) + bias_ref[1]).astype(BF)
    q_ref[...] = q
    v_ref[...] = v[0:seq]
    q_t = q.astype(F32).T.astype(BF)
    k = k.astype(F32)
    kt_ref[...] = k.T[:, 0:seq].astype(BF)
    v_t = v.astype(F32).T[:, 0:seq].astype(BF)
    lane = lax.broadcasted_iota(jnp.int32, (seq, 128), 1)
    contexts = []
    for h in range(2):
        mine = (lane < 64) if h == 0 else (lane >= 64)
        own, other = (320, 384) if h == 0 else (384, 320)
        keys[:, 320:448] = jnp.where(mine, k[0:seq], mask_ref[...].astype(F32)).astype(BF)
        queries[own : own + 64, :] = q_t[h * 64 : h * 64 + 64, :]
        queries[other : other + 64, :] = jnp.ones((64, lanes), BF)
        values[0:64, :] = v_t[h * 64 : h * 64 + 64, :]
        queries[0:64, :] = mm(line_ref[h], hott_ref[0:64, :]).astype(BF)
        queries[64:192, :] = mm(width_ref[h], hott_ref[64:192, :]).astype(BF)
        queries[192:320, :] = mm(height_ref[h], hott_ref[192:320, :]).astype(BF)
        scores = mm(keys[...], queries[...])
        peak = jnp.max(scores, axis=0, keepdims=True)
        weights = jnp.exp(scores - peak).astype(BF)
        exp_ref[h] = weights
        ctx = mm(values[...], weights)
        inverse = 1.0 / ctx[64:65]
        inv_ref[h] = inverse
        contexts.append(ctx[0:64] * inverse)
    ctx = jnp.concatenate(contexts, axis=0)
    ctxt_ref[...] = ctx.astype(BF)
    ctx_ref[...] = ctx.T[0:seq].astype(BF)


def attend(pieces, q_weight, k_weight, v_weight, bias, hot, mask, hot_t, line, width, height):
    seq = mask.shape[0]
    lanes, dim = hot.shape[0], q_weight.shape[0]

    def whole(a):
        return pl.BlockSpec(a.shape, lambda p: (0,) * a.ndim, pipeline_mode=pl.Buffered(1))

    def pair(a):
        return pl.BlockSpec((2,) + a.shape[1:], lambda p: (p, 0, 0))

    def columns(rows):
        return pl.BlockSpec((rows, 128), lambda p: (0, p))

    def rows(length):
        return pl.BlockSpec((128, length), lambda p: (p, 0))

    shape = jax.ShapeDtypeStruct
    return pl.pallas_call(
        partial(attend_kernel, len(pieces)),
        grid=(HEADS // 2,),
        in_specs=[whole(a) for a in pieces]
        + [
            columns(dim),
            columns(dim),
            columns(dim),
            pl.BlockSpec((2, 1, 128), lambda p: (0, 0, p)),
            whole(hot),
            whole(mask),
            whole(hot_t),
            pair(line),
            pair(width),
            pair(height),
        ],
        out_specs=[
            pl.BlockSpec((2, seq, lanes), lambda p: (p, 0, 0)),
            rows(lanes),
            columns(seq),
            pl.BlockSpec((2, 1, lanes), lambda p: (p, 0, 0)),
            columns(lanes),
            rows(seq),
            columns(seq),
            pl.BlockSpec((seq, dim), lambda p: (0, 0)),
        ],
        out_shape=[
            shape((HEADS, seq, lanes), BF),
            shape((dim, lanes), BF),
            shape((seq, dim), BF),
            shape((HEADS, 1, lanes), F32),
            shape((lanes, dim), BF),
            shape((dim, seq), BF),
            shape((seq, dim), BF),
            shape((seq, dim), BF),
        ],
        scratch_shapes=[
            pltpu.VMEM((seq, 448), BF),
            pltpu.VMEM((448, lanes), BF),
            pltpu.VMEM((80, seq), BF),
            pltpu.VMEM((lanes, dim), BF),
        ],
        compiler_params=pltpu.CompilerParams(vmem_limit_bytes=VMEM_BYTES),
        cost_estimate=pl.CostEstimate(
            flops=HEADS * seq * lanes * 4096, bytes_accessed=HEADS * seq * lanes * 2,
            transcendentals=HEADS * seq * lanes,
        ),
    )(*pieces, q_weight, k_weight, v_weight, bias, hot, mask, hot_t, line, width, height)


def by_distance(sums, turn):
    if sums.shape[0] == sums.shape[1]:
        sums = jnp.concatenate([sums, jnp.zeros_like(sums)], axis=1)
    sums = pltpu.roll(sums, turn, 1, stride=1, stride_axis=0)
    sums = jnp.sum(sums, axis=0, keepdims=True)
    if sums.shape[1] < 256:
        sums = jnp.concatenate([sums, jnp.zeros_like(sums)], axis=1)
    return sums


def attend_back_kernel(held, *refs):
    (
        exp_ref, ctxt_ref, inv_ref, v_ref, kt_ref, q_ref, dattn_ref, outw_ref, hot_ref, hott_ref,
        dqkv_ref, spread_ref, values, dctx, lefts, rights, ds, dattn,
    ) = refs[:10] + refs[10 + held :]
    seq = v_ref.shape[0]
    lanes = q_ref.shape[0]

    @pl.when(pl.program_id(0) == 0)
    def _():
        for h in range(2):
            lefts[h, 64:192, :] = hott_ref[64:192, 0:seq]
            rights[h, :, 128:256] = hot_ref[:, 192:320]
        dattn[0:seq, :] = dattn_ref[...]
        dattn[seq:lanes, :] = jnp.zeros((lanes - seq, dattn.shape[1]), BF)

    lane = lax.broadcasted_iota(jnp.int32, (seq, 128), 1)
    query_lane = lax.broadcasted_iota(jnp.int32, (lanes, 128), 1)
    row = lax.broadcasted_iota(jnp.int32, (64, lanes), 0)
    line_hot = jnp.concatenate([hot_ref[:, 0:64], hot_ref[:, 0:64]], axis=1).astype(F32)
    d_rows_t = against(outw_ref[...], dattn[...])
    d_rows_t = [d_rows_t[h * 64 : h * 64 + 64] * inv_ref[h] for h in range(2)]
    d_rows = jnp.concatenate(d_rows_t, axis=0).T.astype(BF)
    results = []
    by_queries = []
    for h in range(2):
        mine = (lane < 64) if h == 0 else (lane >= 64)
        query_mine = (query_lane < 64) if h == 0 else (query_lane >= 64)
        own, other = (0, 64) if h == 0 else (64, 0)
        part = slice(h * 64, h * 64 + 64)
        values[h] = jnp.where(mine, v_ref[...].astype(F32), 1.0).astype(BF)
        delta = -jnp.sum(d_rows_t[h] * ctxt_ref[part, :].astype(F32), axis=0, keepdims=True)
        high = delta.astype(BF).astype(F32)
        extra = jnp.where(row == 0, high, jnp.where(row == 1, delta - high, 0.0))
        dctx[h, own : own + 64, :] = d_rows_t[h].astype(BF)
        dctx[h, other : other + 64, :] = extra.astype(BF)
        lefts[h, 0:64, :] = kt_ref[part, :]
        rights[h, :, 0:128] = jnp.where(query_mine, q_ref[...].astype(F32), line_hot).astype(BF)
        d_scores = mm(values[h], dctx[h])
        ds[h] = (exp_ref[h].astype(F32) * d_scores).astype(BF)
        by_query = mm(lefts[h], ds[h])
        by_queries.append(by_query[0:64] * 0.125)
        by_key = mm(ds[h], rights[h])
        width = mm(by_query[64:192].astype(BF), hot_ref[:, 64:192])
        height = mm(hott_ref[192:320, 0:seq], by_key[:, 128:256].astype(BF))
        near = mm(hott_ref[0:64, 0:seq], by_key[:, 0:128].astype(BF))
        spread_ref[h, 0:1, :] = by_distance(width, 0)
        spread_ref[h, 1:2, :] = by_distance(height, 0)
        line_lane = lax.broadcasted_iota(jnp.int32, near.shape, 1)
        near = jnp.where((line_lane >= 64) if h == 0 else (line_lane < 64), near, 0.0)
        spread_ref[h, 2:3, :] = by_distance(near, 64 if h == 0 else 0)
        results.append((by_key[:, 0:128], mm(exp_ref[h], d_rows)))
    dqkv_ref[0] = jnp.concatenate(by_queries, axis=0).T[0:seq].astype(BF)
    dqkv_ref[1] = jnp.where(lane < 64, results[0][0], results[1][0]).astype(BF)
    dqkv_ref[2] = jnp.where(lane < 64, results[0][1], results[1][1]).astype(BF)


def attend_back(first, pairs, held, exps, ctx_t, inverse, v, k_t, q, d_attn, out_weight, hot, hot_t):
    seq, dim = v.shape
    lanes = q.shape[0]

    def whole(a):
        return pl.BlockSpec(a.shape, lambda p: (0,) * a.ndim, pipeline_mode=pl.Buffered(1))

    def columns(rows):
        return pl.BlockSpec((rows, 128), lambda p: (0, p + first))

    def rows(length):
        return pl.BlockSpec((128, length), lambda p: (p + first, 0))

    def pair(*shape, start=first):
        return pl.BlockSpec((2,) + shape, lambda p: (p + start, 0, 0))

    shape = jax.ShapeDtypeStruct
    return pl.pallas_call(
        partial(attend_back_kernel, len(held)),
        grid=(pairs,),
        in_specs=[
            pair(seq, lanes),
            rows(lanes),
            pair(1, lanes),
            columns(seq),
            rows(seq),
            columns(lanes),
            whole(d_attn),
            rows(dim),
            whole(hot),
            whole(hot_t),
        ]
        + [pl.BlockSpec(memory_space=pl.ANY)] * len(held),
        out_specs=[
            pl.BlockSpec((3, seq, 128), lambda p: (0, 0, p)),
            pair(3, 256, start=0),
        ],
        out_shape=[
            shape((3, seq, 128 * pairs), BF),
            shape((2 * pairs, 3, 256), F32),
        ],
        scratch_shapes=[
            pltpu.VMEM((2, seq, 128), BF),
            pltpu.VMEM((2, 128, lanes), BF),
            pltpu.VMEM((2, 192, seq), BF),
            pltpu.VMEM((2, lanes, 256), BF),
            pltpu.VMEM((2, seq, lanes), BF),
            pltpu.VMEM((lanes, dim), BF),
        ],
        compiler_params=pltpu.CompilerParams(vmem_limit_bytes=VMEM_BYTES),
        cost_estimate=pl.CostEstimate(
            flops=2 * pairs * seq * lanes * 4096, bytes_accessed=4 * pairs * seq * lanes,
            transcendentals=0,
        ),
    )(exps, ctx_t, inverse, v, k_t, q, d_attn, out_weight, hot, hot_t, *held)


def gelu_pair(x):
    bell = jnp.exp(x * x * -0.5)
    t = 1.0 / (1.0 + 0.23164189 * jnp.abs(x))
    poly = t * (0.127414796 + t * (-0.142248368 + t * (0.7107068705 + t * (-0.7265760135 + t * 0.5307027145))))
    upper = poly * bell
    phi = jnp.where(x < 0, upper, 1.0 - upper)
    return x * phi, phi + x * bell * 0.3989422804014327

def normalise(rows):
    mean = jnp.mean(rows, axis=-1, keepdims=True)
    centred = rows - mean
    scale = lax.rsqrt(jnp.mean(centred * centred, axis=-1, keepdims=True) + 1e-05)
    return centred * scale, scale

def normalise_back(hat, scale, d_hat):
    return scale * (d_hat - jnp.mean(d_hat, axis=-1, keepdims=True) - hat * jnp.mean(d_hat * hat, axis=-1, keepdims=True))

def total(rows):
    return jnp.sum(rows, axis=0, keepdims=True)


def rows_kernel(count, blocks, *refs):
    pieces = refs[:count]
    (
        x_ref, ctx_ref, ctxt_ref, out_w, up_w, down_w, bias_ref, up_b,
        final_ref, dmid_ref, dattn_ref, up_ref, down_ref, out_ref, sums_ref, upsum_ref,
        slope, cots, lows, acts, d_branches, d_pres, lows_t, d_attns,
    ) = refs[count:]
    step = pl.program_id(0)
    block = x_ref.shape[0]
    seq, dim = cots.shape
    parts = acts.shape[0]

    @pl.when(step == 0)
    def _():
        sums_ref[...] = jnp.zeros_like(sums_ref)
        upsum_ref[...] = jnp.zeros_like(upsum_ref)
        assemble(pieces, cots)

    @pl.when(step < blocks)
    def _():
        here = pl.ds(pl.multiple_of(step * block, 16), block)
        attn = mm(ctx_ref[...], out_w[...]) + bias_ref[0:1]
        hat, scale = normalise(x_ref[...].astype(F32) + attn)
        normed = hat * bias_ref[1:2] + bias_ref[2:3]
        low = normed.astype(BF)
        lows[here, :] = low
        branch = bias_ref[3:4]
        for n in range(parts):
            part = slice(n * dim, (n + 1) * dim)
            act, grad = gelu_pair(mm(low, up_w[:, part]) + up_b[:, part])
            slope[:, part] = grad
            act = act.astype(BF)
            acts[n, here, :] = act
            branch = branch + mm(act, down_w[part, :])
        final_hat, final_scale = normalise(normed + branch)
        final_ref[...] = (final_hat * bias_ref[4:5] + bias_ref[5:6]).astype(BF)
        cot = cots[here, :].astype(F32)
        d_sum = normalise_back(final_hat, final_scale, cot * bias_ref[4:5])
        d_branch = d_sum.astype(BF)
        d_branches[here, :] = d_branch
        d_normed = d_sum
        for n in range(parts):
            part = slice(n * dim, (n + 1) * dim)
            d_pre = (against(d_branch, down_w[part, :]) * slope[:, part]).astype(BF)
            d_pres[n, here, :] = d_pre
            upsum_ref[:, part] += total(d_pre.astype(F32))
            d_normed = d_normed + against(d_pre, up_w[:, part])
        d_mid = normalise_back(hat, scale, d_normed * bias_ref[1:2])
        dmid_ref[...] = d_mid
        d_attn = d_mid.astype(BF)
        dattn_ref[...] = d_attn
        d_attns[here, :] = d_attn
        sums_ref[...] += jnp.concatenate(
            [
                total(d_attn.astype(F32)),
                total(d_normed * hat),
                total(d_normed),
                total(d_branch.astype(F32)),
                total(cot * final_hat),
                total(cot),
                jnp.zeros((2, dim), F32),
            ],
            axis=0,
        )

    @pl.when(step == blocks)
    def _():
        lows_t[...] = lows[...].astype(F32).T.astype(BF)

    @pl.when((step >= blocks) & (step < blocks + parts))
    def _():
        n = step - blocks
        down_ref[...] = inner(acts[n], d_branches[...]).astype(BF)
        up_ref[...] = mm(lows_t[...], d_pres[n]).astype(BF)

    @pl.when(step == blocks + parts)
    def _():
        out_ref[...] = mm(ctxt_ref[:, 0:seq], d_attns[...]).astype(BF)


def rows_pass(pieces, x, ctx, ctx_t, out_w, up_w, down_w, bias, up_b):
    seq, dim = ctx.shape
    ff = up_w.shape[1]
    blocks = 4
    block = seq // blocks
    parts = ff // dim

    def row(width):
        return pl.BlockSpec((block, width), lambda p: (jnp.minimum(p, blocks - 1), 0))

    def whole(a):
        return pl.BlockSpec(a.shape, lambda p: (0,) * a.ndim, pipeline_mode=pl.Buffered(1))

    def part(p):
        return jnp.clip(p - blocks, 0, parts - 1)

    shape = jax.ShapeDtypeStruct
    return pl.pallas_call(
        partial(rows_kernel, len(pieces), blocks),
        grid=(blocks + parts + 1,),
        in_specs=[whole(a) for a in pieces]
        + [row(dim), row(dim)]
        + [whole(a) for a in (ctx_t, out_w, up_w, down_w, bias, up_b)],
        out_specs=[
            row(dim),
            row(dim),
            row(dim),
            pl.BlockSpec((dim, dim), lambda p: (0, part(p))),
            pl.BlockSpec((dim, dim), lambda p: (part(p), 0)),
            pl.BlockSpec((dim, dim), lambda p: (0, 0)),
            pl.BlockSpec((8, dim), lambda p: (0, 0)),
            pl.BlockSpec((1, ff), lambda p: (0, 0)),
        ],
        out_shape=[
            shape((seq, dim), BF),
            shape((seq, dim), F32),
            shape((seq, dim), BF),
            shape((dim, ff), BF),
            shape((ff, dim), BF),
            shape((dim, dim), BF),
            shape((8, dim), F32),
            shape((1, ff), F32),
        ],
        scratch_shapes=[
            pltpu.VMEM((block, ff), F32),
            pltpu.VMEM((seq, dim), BF),
            pltpu.VMEM((seq, dim), BF),
            pltpu.VMEM((parts, seq, dim), BF),
            pltpu.VMEM((seq, dim), BF),
            pltpu.VMEM((parts, seq, dim), BF),
            pltpu.VMEM((dim, seq), BF),
            pltpu.VMEM((seq, dim), BF),
        ],
        compiler_params=pltpu.CompilerParams(vmem_limit_bytes=VMEM_BYTES),
        cost_estimate=pl.CostEstimate(
            flops=56 * seq * dim * dim, bytes_accessed=64 * seq * dim, transcendentals=seq * ff
        ),
    )(*pieces, x, ctx, ctx_t, out_w, up_w, down_w, bias, up_b)


def qkv_kernel(held, x_ref, dqkv_ref, out_ref, *refs):
    grad_ref, sums_ref, x_t = refs[held:]
    step = pl.program_id(0)

    @pl.when(step == 0)
    def _():
        x_t[...] = x_ref[...].astype(F32).T.astype(BF)

    @pl.when(step < 3)
    def _():
        grad_ref[...] = mm(x_t[...], dqkv_ref[0]).astype(BF)
        sums_ref[0] = jnp.broadcast_to(total(dqkv_ref[0].astype(F32)), sums_ref.shape[1:])

    @pl.when(step == 3)
    def _():
        grad_ref[...] = out_ref[...]


def qkv_sums(room, held, x, d_qkv, out_low):
    _, seq, dim = d_qkv.shape

    def whole(a):
        return pl.BlockSpec(a.shape, lambda p: (0,) * a.ndim, pipeline_mode=pl.Buffered(1))

    shape = jax.ShapeDtypeStruct
    return pl.pallas_call(
        partial(qkv_kernel, len(held)),
        grid=(4,),
        in_specs=[
            whole(x),
            pl.BlockSpec((1, seq, dim), lambda p: (jnp.minimum(p, 2), 0, 0)),
            whole(out_low),
        ]
        + [pl.BlockSpec(memory_space=pl.ANY)] * len(held),
        out_specs=[
            pl.BlockSpec((dim, dim), lambda p: (p, 0)),
            pl.BlockSpec((1, 8, dim), lambda p: (jnp.minimum(p, 2), 0, 0)),
        ],
        out_shape=[shape((4 * dim + room, dim), BF), shape((3, 8, dim), F32)],
        scratch_shapes=[pltpu.VMEM((dim, seq), BF)],
        compiler_params=pltpu.CompilerParams(vmem_limit_bytes=VMEM_BYTES),
        cost_estimate=pl.CostEstimate(
            flops=8 * seq * dim * dim, bytes_accessed=24 * seq * dim, transcendentals=0
        ),
    )(x, d_qkv, out_low, *held)


def rows_grad_kernel(dqkv_ref, weight_ref, dmid_ref, drows_ref, sum_ref):
    step = pl.program_id(0)

    @pl.when(step == 0)
    def _():
        sum_ref[...] = dmid_ref[...]

    sum_ref[...] += against(dqkv_ref[0], weight_ref[0])

    @pl.when(step == 2)
    def _():
        drows_ref[...] = sum_ref[...].astype(BF)


def rows_grad(d_qkv, weights, d_mid):
    _, seq, dim = d_qkv.shape
    return pl.pallas_call(
        rows_grad_kernel,
        grid=(3,),
        in_specs=[
            pl.BlockSpec((1, seq, dim), lambda p: (p, 0, 0)),
            pl.BlockSpec((1, dim, dim), lambda p: (p, 0, 0)),
            pl.BlockSpec((seq, dim), lambda p: (0, 0), pipeline_mode=pl.Buffered(1)),
        ],
        out_specs=pl.BlockSpec((seq, dim), lambda p: (0, 0)),
        out_shape=jax.ShapeDtypeStruct((seq, dim), BF),
        scratch_shapes=[pltpu.VMEM((seq, dim), F32)],
        compiler_params=pltpu.CompilerParams(vmem_limit_bytes=VMEM_BYTES),
        cost_estimate=pl.CostEstimate(
            flops=6 * seq * dim * dim, bytes_accessed=16 * seq * dim, transcendentals=0
        ),
    )(d_qkv, weights, d_mid)


def bucket_select(table):
    reach = (table.shape[0] - 1) // 2
    spots = jnp.arange(4 * reach, dtype=jnp.int32)
    bucket = jnp.clip(spots[None, :] - spots[:, None], -reach, reach) + reach
    return bucket[None] == jnp.arange(2 * reach + 1, dtype=jnp.int32)[:, None, None]


def spread_table(table):
    span = 2 * (table.shape[0] - 1)
    spread = lax.dot_general(
        table.astype(BF),
        bucket_select(table).astype(BF).reshape(table.shape[0], -1),
        (((0,), (0,)), ((), ())),
        preferred_element_type=F32,
    )
    return spread.astype(BF).reshape(HEADS, span, span)


def gather_table(spread, table):
    reach = (table.shape[0] - 1) // 2
    distance = jnp.arange(spread.shape[1], dtype=jnp.int32) - (4 * reach - 1)
    bucket = jnp.clip(distance, -reach, reach) + reach
    select = bucket[None, :] == jnp.arange(table.shape[0], dtype=jnp.int32)[:, None]
    return lax.dot_general(
        select.astype(F32),
        spread,
        (((1,), (1,)), ((), ())),
        precision=lax.Precision.HIGHEST,
        preferred_element_type=F32,
    )


def shift_pairs(size, step):
    return [(i, (i + step) % size) for i in range(size)]


def flip_pairs(size, step):
    return [(i, i ^ step) for i in range(size)]


def pick(array, index):
    return lax.dynamic_index_in_dim(array, index, 0, keepdims=False)


def swap_text(parts):
    return lax.all_to_all(parts, "wide", split_axis=0, concat_axis=0, tiled=True)


def patch_order(size):
    me = lax.axis_index("narrow")
    return [me ^ k for k in range(size)]


def swap_patch(parts):
    size = parts.shape[0]
    me = lax.axis_index("narrow")
    return [pick(parts, me)] + [
        lax.ppermute(pick(parts, me ^ k), "narrow", flip_pairs(size, k)) for k in range(1, size)
    ]


def flip_axis(array, axis, bit):
    return jnp.where(bit == 1, jnp.flip(array, axis), array)


def from_flipped(parts, me):
    size = parts.shape[0]
    bits = size.bit_length() - 1
    parts = parts.reshape((2,) * bits + parts.shape[1:])
    for b in range(bits):
        parts = flip_axis(parts, bits - 1 - b, (me >> b) & 1)
    return parts.reshape((size,) + parts.shape[bits:])


def patch_away(rows, size):
    parts = rows.reshape(size, -1, rows.shape[1])
    return [parts[0]] + [
        lax.ppermute(parts[k], "narrow", flip_pairs(size, k)) for k in range(1, size)
    ]


def patch_set(pieces, shape):
    return from_flipped(jnp.stack(pieces), lax.axis_index("narrow")).reshape(shape)


def add(*terms):
    total = terms[0].astype(F32)
    for term in terms[1:]:
        total = total + term.astype(F32)
    return total.astype(BF)


def wide_orders(wide, ways):
    bits = list(range(1, wide.bit_length() - 1))
    return [bits, bits[::-1]][:ways]


def wide_bit(bit):
    return (lax.axis_index("wide") >> bit) & 1


def add_kernel(me_ref, own_ref, arrived_ref, *refs):
    refs[-1][...] = (own_ref[0].astype(F32) + arrived_ref[...].astype(F32)).astype(BF)


def add_own(parts, me, arrived, held):
    rows, columns = arrived.shape
    steps = 2 if rows % 32 == 0 else 1
    block = rows // steps
    return pl.pallas_call(
        add_kernel,
        grid_spec=pltpu.PrefetchScalarGridSpec(
            num_scalar_prefetch=1,
            grid=(steps,),
            in_specs=[
                pl.BlockSpec((1, block, columns), lambda i, me_ref: (me_ref[0], i, 0)),
                pl.BlockSpec((block, columns), lambda i, me_ref: (i, 0)),
            ]
            + [pl.BlockSpec(memory_space=pl.ANY)] * len(held),
            out_specs=pl.BlockSpec((block, columns), lambda i, me_ref: (i, 0)),
        ),
        out_shape=jax.ShapeDtypeStruct((rows, columns), BF),
        compiler_params=pltpu.CompilerParams(vmem_limit_bytes=VMEM_BYTES),
        cost_estimate=pl.CostEstimate(flops=0, bytes_accessed=6 * rows * columns, transcendentals=0),
    )(me.reshape(1), parts, arrived, *held)


def wide_step(grad, wide, bit, held=()):
    parts = grad.reshape(2, -1, grad.shape[1])
    me = wide_bit(bit)
    arrived = lax.ppermute(pick(parts, 1 - me), "wide", flip_pairs(wide, 1 << bit))
    return add_own(parts, me, arrived, held) if held else add(pick(parts, me), arrived)


def cut(grad, parts):
    first = -(-grad.shape[0] // (16 * parts)) * 8 * parts
    return [grad[:first], grad[first:]]


def wide_steps(shares, wide, i, held=()):
    orders = wide_orders(wide, len(shares))
    return [
        wide_step(a, wide, order[i], held if n == 0 else ())
        for n, (a, order) in enumerate(zip(shares, orders))
    ]


def narrow_step(shares, narrow):
    me = lax.axis_index("narrow")
    parts = [a.reshape(narrow, -1, a.shape[1]) for a in shares]

    def picked(index):
        return jnp.concatenate([pick(a, index) for a in parts], axis=0)

    arrived = [
        lax.ppermute(picked(me ^ k), "narrow", flip_pairs(narrow, k)) for k in range(1, narrow)
    ]
    return add(picked(me), *arrived)


def gather_narrow(part, narrow, lengths):
    parts = [part] + [
        lax.ppermute(part, "narrow", flip_pairs(narrow, k)) for k in range(1, narrow)
    ]
    parts = jnp.stack(parts)
    return [parts[:, : lengths[0]], parts[:, lengths[0] :]]


def gather_wide(shares, wide, i):
    return [
        jnp.concatenate([a, lax.ppermute(a, "wide", flip_pairs(wide, 1 << order[i]))], axis=0)
        for a, order in zip(shares, wide_orders(wide, len(shares)))
    ]


def gather_core(shares, wide):
    return shares + [lax.ppermute(a, "wide", flip_pairs(wide, 1)) for a in shares]


def convert_kernel(up_ref, down_ref, after_ref, up_out, down_out):
    step = pl.program_id(0)
    parts = pl.num_programs(0) // 2

    @pl.when(step < parts)
    def _():
        up_out[...] = up_ref[...].astype(F32)

    @pl.when(step >= parts)
    def _():
        down_out[...] = down_ref[...].astype(F32)


def convert(up_total, down_total, after):
    dim, ff = up_total.shape
    parts = ff // dim

    def block(index):
        return pl.BlockSpec((dim, dim), index)

    up_block = block(lambda p: (0, jnp.minimum(p, parts - 1)))
    down_block = block(lambda p: (jnp.maximum(p - parts, 0), 0))
    shape = jax.ShapeDtypeStruct
    return pl.pallas_call(
        convert_kernel,
        grid=(2 * parts,),
        in_specs=[up_block, down_block, pl.BlockSpec(memory_space=pl.ANY)],
        out_specs=[up_block, down_block],
        out_shape=[shape((dim, ff), F32), shape((ff, dim), F32)],
        compiler_params=pltpu.CompilerParams(vmem_limit_bytes=VMEM_BYTES),
        cost_estimate=pl.CostEstimate(flops=0, bytes_accessed=12 * dim * ff, transcendentals=0),
    )(up_total, down_total, after)


def finish_kernel(places, ways, cuts, index_ref, *refs):
    pieces, outs = refs[: 2 * ways], refs[2 * ways :]
    at = 0
    for core in range(2):
        for way in range(ways):
            rows = pieces[way].shape[1]
            for place in range(places):
                here = index_ref[way, place]
                for (start, stop), out in zip(cuts, outs):
                    low, high = max(at, start), min(at + rows, stop)
                    if low < high:
                        same = pieces[way][here].astype(F32)
                        other = pieces[ways + way][here].astype(F32)
                        block = jnp.where(index_ref[2, 0] == core, same, other)
                        out[low - start : high - start, :] = block[low - at : high - at]
                at += rows


def finish(pieces, wide, narrow, lengths):
    places, _, columns = pieces[0].shape
    ways = len(pieces) // 2
    index = []
    for order in wide_orders(wide, 2):
        me = jnp.int32(0)
        for bit in order:
            me = me * 2 + wide_bit(bit)
        me = me * narrow + lax.axis_index("narrow")
        index.append(jnp.arange(places, dtype=jnp.int32) ^ me)
    index.append(jnp.full((places,), wide_bit(0), jnp.int32))
    cuts = []
    for length in lengths:
        start = cuts[-1][1] if cuts else 0
        cuts.append((start, start + length))
    return pl.pallas_call(
        partial(finish_kernel, places, ways, cuts),
        in_specs=[pl.BlockSpec(memory_space=pltpu.SMEM)]
        + [pl.BlockSpec(memory_space=pltpu.VMEM)] * len(pieces),
        out_specs=[pl.BlockSpec(memory_space=pltpu.VMEM)] * len(lengths),
        out_shape=[jax.ShapeDtypeStruct((length, columns), F32) for length in lengths],
        compiler_params=pltpu.CompilerParams(vmem_limit_bytes=VMEM_BYTES),
        cost_estimate=pl.CostEstimate(
            flops=0, bytes_accessed=8 * sum(lengths) * columns, transcendentals=0
        ),
    )(jnp.stack(index), *pieces)


def room_for(rows, wide, narrow):
    return 32 + -(rows + 32) % (8 * wide * narrow)


def pack(grads, columns, rows):
    lines = []
    for grad in grads:
        flat = grad.reshape(-1)
        lines.append(jnp.pad(flat, (0, -flat.shape[0] % columns)).reshape(-1, columns))
    lines = jnp.concatenate(lines, axis=0)
    return jnp.pad(lines, ((0, -lines.shape[0] % rows), (0, 0)))


def unpack(lines, grads):
    columns = lines.shape[1]
    at = 0
    out = []
    for grad in grads:
        count = -(-grad.size // columns)
        out.append(lines[at : at + count].reshape(-1)[: grad.size].reshape(grad.shape))
        at += count
    return out


def body(
    text_in,
    patch_in,
    res_class,
    text_len,
    pos_line,
    pos_x,
    pos_y,
    query_weight,
    query_bias,
    key_weight,
    value_weight,
    value_bias,
    output_weight,
    output_bias,
    norm_gain,
    norm_shift,
    up_weight,
    up_bias,
    down_weight,
    down_bias,
    final_gain,
    final_shift,
    line_table,
    width_table,
    height_table,
    cot_text,
    cot_patch,
):
    text_shape = text_in.shape
    patch_shape = patch_in.shape
    dim = text_shape[3]
    seq = TEXT + PATCH
    lanes = -(-seq // 128) * 128
    wide = text_shape[0]
    narrow = patch_shape[1]
    pieces = [swap_text(text_in.reshape(wide, -1, dim)).reshape(-1, dim)]
    pieces += swap_patch(patch_in.reshape(narrow, -1, dim))
    cot_text, pieces[0] = lax.optimization_barrier((cot_text, pieces[0]))
    cot_patch, pieces = lax.optimization_barrier((cot_patch, pieces))
    cots = [swap_text(cot_text.reshape(wide, -1, dim)).reshape(-1, dim)]
    cots += swap_patch(cot_patch.reshape(narrow, -1, dim))
    index = jnp.arange(seq, dtype=jnp.int32)
    live_patch = jnp.where(res_class.reshape(()) == 1, PATCH, SMALL_PATCH)
    valid = jnp.where(index < TEXT, index < text_len.reshape(()), index - TEXT < live_patch)
    facts = jnp.concatenate(
        [pos_line.reshape(1, -1), pos_x.reshape(1, -1), pos_y.reshape(1, -1), valid.astype(jnp.int32)[None]]
    )
    patch_facts = facts[:, TEXT:].reshape(4, narrow, -1)
    facts = jnp.concatenate(
        [facts[:, :TEXT]]
        + [
            lax.dynamic_index_in_dim(patch_facts, i, 1, keepdims=False)
            for i in patch_order(narrow)
        ],
        axis=1,
    )
    line_spots, x_spots, y_spots = facts[0], facts[1], facts[2]
    valid = facts[3] == 1

    line = spread_table(line_table)
    width = spread_table(width_table)
    height = spread_table(height_table)
    hots = []
    hots_t = []
    hots_back = []
    for spots, table in ((line_spots, line_table), (x_spots, width_table), (y_spots, height_table)):
        span = jnp.arange(2 * (table.shape[0] - 1), dtype=jnp.int32)
        long = jnp.pad(spots, (0, lanes - seq), constant_values=-1)
        hots.append((long[:, None] == span[None, :]).astype(BF))
        hots_t.append((long[None, :] == span[:, None]).astype(BF))
        hots_back.append((long[None, :] == span[::-1, None]).astype(BF))
    hot = jnp.concatenate(hots, axis=1)
    hot_t = jnp.concatenate(hots_t, axis=0)
    hot_back = jnp.concatenate(hots_back, axis=0)
    column = jnp.arange(128, dtype=jnp.int32)
    mask = jnp.where((column[None, :] % 64 == 0) & ~valid[:, None], -1e30, 0.0).astype(BF)

    exps, ctx_t, ctx, inverse, q, k_t, v, rows_in = attend(
        pieces,
        query_weight,
        key_weight,
        value_weight,
        jnp.stack([query_bias, value_bias])[:, None],
        hot,
        mask,
        hot_t,
        line,
        width,
        height,
    )
    vectors = jnp.stack(
        [output_bias, norm_gain, norm_shift, down_bias, final_gain, final_shift] + [final_shift] * 2
    )
    final_low, d_mid, d_attn, up_low, down_low, out_low, sums, up_sum = rows_pass(
        cots, rows_in, ctx, ctx_t, output_weight, up_weight, down_weight, vectors, up_bias[None]
    )
    early = (sums[0], sums[1], sums[2], up_sum, sums[3], sums[4], sums[5])
    down_total, up_total = lax.psum((down_low, up_low), ("wide", "narrow"))
    qkv_weight = jnp.stack([query_weight, key_weight, value_weight])

    def backward():
        text_out = swap_text(final_low[:TEXT].reshape(wide, -1, dim)).reshape(text_shape)
        out_pieces = patch_away(final_low[TEXT:], narrow)
        levels = wide.bit_length() - 2
        d_qkv, spread = attend_back(
            0, HEADS // 2, [], exps, ctx_t, inverse, v, k_t, q, d_attn, output_weight, hot, hot_back
        )
        room = room_for(4 * dim, wide, narrow)
        tail, d_sums = qkv_sums(room, [text_out, *out_pieces[1:]], rows_in, d_qkv, out_low)
        d_rows = rows_grad(d_qkv, qkv_weight, d_mid)
        text_grad = swap_text(d_rows[:TEXT].reshape(wide, -1, dim)).reshape(text_shape)
        grad_pieces = patch_away(d_rows[TEXT:], narrow)
        late = (
            d_sums[0, 0],
            d_sums[2, 0],
            gather_table(spread[:, 2], line_table),
            gather_table(spread[:, 0], width_table),
            gather_table(spread[:, 1], height_table),
        )
        small = pack(early + late, dim, room).astype(BF)
        tail = lax.dynamic_update_slice(tail, small, (4 * dim, 0))
        halves = cut(wide_step(tail, wide, 0), wide * narrow // 2)
        for i in range(levels):
            moved = [text_grad, *grad_pieces[1:]] if i == levels - 1 else []
            halves = wide_steps(halves, wide, i, moved)
        lengths = [a.shape[0] // narrow for a in halves]
        halves = gather_narrow(narrow_step(halves, narrow), narrow, lengths)
        for i in range(levels - 1, -1, -1):
            halves = gather_wide(halves, wide, i)
        *large, small = finish(gather_core(halves, wide), wide, narrow, (dim,) * 4 + (32,))
        return (
            text_out, patch_set(out_pieces, patch_shape), text_grad,
            patch_set(grad_pieces, patch_shape), *large, *unpack(small, early + late),
        )

    def never():
        return jax.tree.map(lambda a: jnp.zeros(a.shape, a.dtype), jax.eval_shape(backward))

    (
        text_out, patch_out, text_grad, patch_grad, query_weight_grad, key_weight_grad,
        value_weight_grad, output_weight_grad, output_bias_grad, norm_gain_grad, norm_shift_grad,
        up_bias_grad, down_bias_grad, final_gain_grad, final_shift_grad, query_bias_grad,
        value_bias_grad, line_table_grad, width_table_grad, height_table_grad,
    ) = lax.cond(text_len.reshape(()) >= 0, backward, never)
    up_weight_grad, down_weight_grad = convert(up_total, down_total, value_weight_grad)
    up_bias_grad = up_bias_grad.reshape(-1)
    return (
        text_out,
        patch_out,
        text_grad,
        patch_grad,
        query_weight_grad,
        query_bias_grad,
        key_weight_grad,
        value_weight_grad,
        value_bias_grad,
        output_weight_grad,
        output_bias_grad,
        norm_gain_grad,
        norm_shift_grad,
        up_weight_grad,
        up_bias_grad,
        down_weight_grad,
        down_bias_grad,
        final_gain_grad,
        final_shift_grad,
        line_table_grad,
        width_table_grad,
        height_table_grad,
    )


def solution(mesh):
    text = P(None, "narrow", "wide", None)
    patch = P("wide", None, "narrow", None)
    page = P("wide", "narrow")
    spots = P("wide", "narrow", None)
    in_specs = (text, patch, page, page, spots, spots, spots) + (P(),) * 18 + (text, patch)
    out_specs = (text, patch, text, patch) + (P(),) * 18
    return jax.shard_map(body, mesh=mesh, in_specs=in_specs, out_specs=out_specs, check_vma=False)
```

```python
from functools import partial

import jax
import jax.numpy as jnp
from jax import lax
from jax.experimental import pallas as pl
from jax.experimental.pallas import tpu as pltpu
from jax.sharding import PartitionSpec as P

HEADS = 12
TEXT = 512
PATCH = 576
SMALL_PATCH = 196
BF = jnp.bfloat16
F32 = jnp.float32
VMEM_BYTES = 60 * 2**20


def mm(left, right):
    return lax.dot_general(left, right, (((1,), (0,)), ((), ())), preferred_element_type=F32)


def inner(left, right):
    return lax.dot_general(left, right, (((0,), (0,)), ((), ())), preferred_element_type=F32)


def against(left, right):
    return lax.dot_general(left, right, (((1,), (1,)), ((), ())), preferred_element_type=F32)


def assemble(pieces, rows):
    at = 0
    for piece in pieces:
        rows[at : at + piece.shape[0], :] = piece[...]
        at += piece.shape[0]


def attend_kernel(count, *refs):
    pieces = refs[:count]
    (
        qw_ref, kw_ref, vw_ref, bias_ref, hot_ref, mask_ref, hott_ref, line_ref, width_ref,
        height_ref, exp_ref, ctxt_ref, ctx_ref, inv_ref, q_ref, kt_ref, v_ref, x_ref,
        keys, queries, values, rows,
    ) = refs[count:]
    seq = v_ref.shape[0]
    lanes = rows.shape[0]

    @pl.when(pl.program_id(0) == 0)
    def _():
        keys[:, 0:320] = hot_ref[0:seq, :]
        values[64:80, :] = jnp.ones((16, seq), BF)
        assemble(pieces, rows)
        rows[seq:lanes, :] = jnp.zeros((lanes - seq, rows.shape[1]), BF)
        x_ref[...] = rows[0:seq, :]

    both = mm(rows[...], jnp.concatenate([qw_ref[...], kw_ref[...]], axis=1))
    q = ((both[:, 0:128] + bias_ref[0]) * 0.125).astype(BF)
    k = both[:, 128:256].astype(BF)
    v = (mm(rows[...], vw_ref[...]) + bias_ref[1]).astype(BF)
    q_ref[...] = q
    v_ref[...] = v[0:seq]
    q_t = q.astype(F32).T.astype(BF)
    k = k.astype(F32)
    kt_ref[...] = k.T[:, 0:seq].astype(BF)
    v_t = v.astype(F32).T[:, 0:seq].astype(BF)
    lane = lax.broadcasted_iota(jnp.int32, (seq, 128), 1)
    contexts = []
    for h in range(2):
        mine = (lane < 64) if h == 0 else (lane >= 64)
        own, other = (320, 384) if h == 0 else (384, 320)
        keys[:, 320:448] = jnp.where(mine, k[0:seq], mask_ref[...].astype(F32)).astype(BF)
        queries[own : own + 64, :] = q_t[h * 64 : h * 64 + 64, :]
        queries[other : other + 64, :] = jnp.ones((64, lanes), BF)
        values[0:64, :] = v_t[h * 64 : h * 64 + 64, :]
        queries[0:64, :] = mm(line_ref[h], hott_ref[0:64, :]).astype(BF)
        queries[64:192, :] = mm(width_ref[h], hott_ref[64:192, :]).astype(BF)
        queries[192:320, :] = mm(height_ref[h], hott_ref[192:320, :]).astype(BF)
        scores = mm(keys[...], queries[...])
        peak = jnp.max(scores, axis=0, keepdims=True)
        weights = jnp.exp(scores - peak).astype(BF)
        exp_ref[h] = weights
        ctx = mm(values[...], weights)
        inverse = 1.0 / ctx[64:65]
        inv_ref[h] = inverse
        contexts.append(ctx[0:64] * inverse)
    ctx = jnp.concatenate(contexts, axis=0)
    ctxt_ref[...] = ctx.astype(BF)
    ctx_ref[...] = ctx.T[0:seq].astype(BF)


def attend(pieces, q_weight, k_weight, v_weight, bias, hot, mask, hot_t, line, width, height):
    seq = mask.shape[0]
    lanes, dim = hot.shape[0], q_weight.shape[0]

    def whole(a):
        return pl.BlockSpec(a.shape, lambda p: (0,) * a.ndim, pipeline_mode=pl.Buffered(1))

    def pair(a):
        return pl.BlockSpec((2,) + a.shape[1:], lambda p: (p, 0, 0))

    def columns(rows):
        return pl.BlockSpec((rows, 128), lambda p: (0, p))

    def rows(length):
        return pl.BlockSpec((128, length), lambda p: (p, 0))

    shape = jax.ShapeDtypeStruct
    return pl.pallas_call(
        partial(attend_kernel, len(pieces)),
        grid=(HEADS // 2,),
        in_specs=[whole(a) for a in pieces]
        + [
            columns(dim),
            columns(dim),
            columns(dim),
            pl.BlockSpec((2, 1, 128), lambda p: (0, 0, p)),
            whole(hot),
            whole(mask),
            whole(hot_t),
            pair(line),
            pair(width),
            pair(height),
        ],
        out_specs=[
            pl.BlockSpec((2, seq, lanes), lambda p: (p, 0, 0)),
            rows(lanes),
            columns(seq),
            pl.BlockSpec((2, 1, lanes), lambda p: (p, 0, 0)),
            columns(lanes),
            rows(seq),
            columns(seq),
            pl.BlockSpec((seq, dim), lambda p: (0, 0)),
        ],
        out_shape=[
            shape((HEADS, seq, lanes), BF),
            shape((dim, lanes), BF),
            shape((seq, dim), BF),
            shape((HEADS, 1, lanes), F32),
            shape((lanes, dim), BF),
            shape((dim, seq), BF),
            shape((seq, dim), BF),
            shape((seq, dim), BF),
        ],
        scratch_shapes=[
            pltpu.VMEM((seq, 448), BF),
            pltpu.VMEM((448, lanes), BF),
            pltpu.VMEM((80, seq), BF),
            pltpu.VMEM((lanes, dim), BF),
        ],
        compiler_params=pltpu.CompilerParams(vmem_limit_bytes=VMEM_BYTES),
        cost_estimate=pl.CostEstimate(
            flops=HEADS * seq * lanes * 4096, bytes_accessed=HEADS * seq * lanes * 2,
            transcendentals=HEADS * seq * lanes,
        ),
    )(*pieces, q_weight, k_weight, v_weight, bias, hot, mask, hot_t, line, width, height)


def by_distance(sums, turn):
    if sums.shape[0] == sums.shape[1]:
        sums = jnp.concatenate([sums, jnp.zeros_like(sums)], axis=1)
    sums = pltpu.roll(sums, turn, 1, stride=1, stride_axis=0)
    sums = jnp.sum(sums, axis=0, keepdims=True)
    if sums.shape[1] < 256:
        sums = jnp.concatenate([sums, jnp.zeros_like(sums)], axis=1)
    return sums


def attend_back_kernel(held, *refs):
    (
        exp_ref, ctxt_ref, inv_ref, v_ref, kt_ref, q_ref, dattn_ref, outw_ref, hot_ref, hott_ref,
        dqkv_ref, spread_ref, values, dctx, lefts, rights, ds, dattn,
    ) = refs[:10] + refs[10 + held :]
    seq = v_ref.shape[0]
    lanes = q_ref.shape[0]

    @pl.when(pl.program_id(0) == 0)
    def _():
        for h in range(2):
            lefts[h, 64:192, :] = hott_ref[64:192, 0:seq]
            rights[h, :, 128:256] = hot_ref[:, 192:320]
        dattn[0:seq, :] = dattn_ref[...]
        dattn[seq:lanes, :] = jnp.zeros((lanes - seq, dattn.shape[1]), BF)

    lane = lax.broadcasted_iota(jnp.int32, (seq, 128), 1)
    query_lane = lax.broadcasted_iota(jnp.int32, (lanes, 128), 1)
    row = lax.broadcasted_iota(jnp.int32, (64, lanes), 0)
    line_hot = jnp.concatenate([hot_ref[:, 0:64], hot_ref[:, 0:64]], axis=1).astype(F32)
    d_rows_t = against(outw_ref[...], dattn[...])
    d_rows_t = [d_rows_t[h * 64 : h * 64 + 64] * inv_ref[h] for h in range(2)]
    d_rows = jnp.concatenate(d_rows_t, axis=0).T.astype(BF)
    results = []
    by_queries = []
    for h in range(2):
        mine = (lane < 64) if h == 0 else (lane >= 64)
        query_mine = (query_lane < 64) if h == 0 else (query_lane >= 64)
        own, other = (0, 64) if h == 0 else (64, 0)
        part = slice(h * 64, h * 64 + 64)
        values[h] = jnp.where(mine, v_ref[...].astype(F32), 1.0).astype(BF)
        delta = -jnp.sum(d_rows_t[h] * ctxt_ref[part, :].astype(F32), axis=0, keepdims=True)
        high = delta.astype(BF).astype(F32)
        extra = jnp.where(row == 0, high, jnp.where(row == 1, delta - high, 0.0))
        dctx[h, own : own + 64, :] = d_rows_t[h].astype(BF)
        dctx[h, other : other + 64, :] = extra.astype(BF)
        lefts[h, 0:64, :] = kt_ref[part, :]
        rights[h, :, 0:128] = jnp.where(query_mine, q_ref[...].astype(F32), line_hot).astype(BF)
        d_scores = mm(values[h], dctx[h])
        ds[h] = (exp_ref[h].astype(F32) * d_scores).astype(BF)
        by_query = mm(lefts[h], ds[h])
        by_queries.append(by_query[0:64] * 0.125)
        by_key = mm(ds[h], rights[h])
        width = mm(by_query[64:192].astype(BF), hot_ref[:, 64:192])
        height = mm(hott_ref[192:320, 0:seq], by_key[:, 128:256].astype(BF))
        near = mm(hott_ref[0:64, 0:seq], by_key[:, 0:128].astype(BF))
        spread_ref[h, 0:1, :] = by_distance(width, 0)
        spread_ref[h, 1:2, :] = by_distance(height, 0)
        line_lane = lax.broadcasted_iota(jnp.int32, near.shape, 1)
        near = jnp.where((line_lane >= 64) if h == 0 else (line_lane < 64), near, 0.0)
        spread_ref[h, 2:3, :] = by_distance(near, 64 if h == 0 else 0)
        results.append((by_key[:, 0:128], mm(exp_ref[h], d_rows)))
    dqkv_ref[0] = jnp.concatenate(by_queries, axis=0).T[0:seq].astype(BF)
    dqkv_ref[1] = jnp.where(lane < 64, results[0][0], results[1][0]).astype(BF)
    dqkv_ref[2] = jnp.where(lane < 64, results[0][1], results[1][1]).astype(BF)


def attend_back(first, pairs, held, exps, ctx_t, inverse, v, k_t, q, d_attn, out_weight, hot, hot_t):
    seq, dim = v.shape
    lanes = q.shape[0]

    def whole(a):
        return pl.BlockSpec(a.shape, lambda p: (0,) * a.ndim, pipeline_mode=pl.Buffered(1))

    def columns(rows):
        return pl.BlockSpec((rows, 128), lambda p: (0, p + first))

    def rows(length):
        return pl.BlockSpec((128, length), lambda p: (p + first, 0))

    def pair(*shape, start=first):
        return pl.BlockSpec((2,) + shape, lambda p: (p + start, 0, 0))

    shape = jax.ShapeDtypeStruct
    return pl.pallas_call(
        partial(attend_back_kernel, len(held)),
        grid=(pairs,),
        in_specs=[
            pair(seq, lanes),
            rows(lanes),
            pair(1, lanes),
            columns(seq),
            rows(seq),
            columns(lanes),
            whole(d_attn),
            rows(dim),
            whole(hot),
            whole(hot_t),
        ]
        + [pl.BlockSpec(memory_space=pl.ANY)] * len(held),
        out_specs=[
            pl.BlockSpec((3, seq, 128), lambda p: (0, 0, p)),
            pair(3, 256, start=0),
        ],
        out_shape=[
            shape((3, seq, 128 * pairs), BF),
            shape((2 * pairs, 3, 256), F32),
        ],
        scratch_shapes=[
            pltpu.VMEM((2, seq, 128), BF),
            pltpu.VMEM((2, 128, lanes), BF),
            pltpu.VMEM((2, 192, seq), BF),
            pltpu.VMEM((2, lanes, 256), BF),
            pltpu.VMEM((2, seq, lanes), BF),
            pltpu.VMEM((lanes, dim), BF),
        ],
        compiler_params=pltpu.CompilerParams(vmem_limit_bytes=VMEM_BYTES),
        cost_estimate=pl.CostEstimate(
            flops=2 * pairs * seq * lanes * 4096, bytes_accessed=4 * pairs * seq * lanes,
            transcendentals=0,
        ),
    )(exps, ctx_t, inverse, v, k_t, q, d_attn, out_weight, hot, hot_t, *held)


def gelu_pair(x):
    bell = jnp.exp(x * x * -0.5)
    t = 1.0 / (1.0 + 0.23164189 * jnp.abs(x))
    poly = t * (0.127414796 + t * (-0.142248368 + t * (0.7107068705 + t * (-0.7265760135 + t * 0.5307027145))))
    upper = poly * bell
    phi = jnp.where(x < 0, upper, 1.0 - upper)
    return x * phi, phi + x * bell * 0.3989422804014327

def normalise(rows):
    mean = jnp.mean(rows, axis=-1, keepdims=True)
    centred = rows - mean
    scale = lax.rsqrt(jnp.mean(centred * centred, axis=-1, keepdims=True) + 1e-05)
    return centred * scale, scale

def normalise_back(hat, scale, d_hat):
    return scale * (d_hat - jnp.mean(d_hat, axis=-1, keepdims=True) - hat * jnp.mean(d_hat * hat, axis=-1, keepdims=True))

def total(rows):
    return jnp.sum(rows, axis=0, keepdims=True)


def rows_kernel(count, blocks, *refs):
    pieces = refs[:count]
    (
        x_ref, ctx_ref, ctxt_ref, out_w, up_w, down_w, bias_ref, up_b,
        final_ref, dmid_ref, dattn_ref, up_ref, down_ref, out_ref, sums_ref, upsum_ref,
        slope, cots, lows, acts, d_branches, d_pres, lows_t, d_attns,
    ) = refs[count:]
    step = pl.program_id(0)
    block = x_ref.shape[0]
    seq, dim = cots.shape
    parts = acts.shape[0]

    @pl.when(step == 0)
    def _():
        sums_ref[...] = jnp.zeros_like(sums_ref)
        upsum_ref[...] = jnp.zeros_like(upsum_ref)
        assemble(pieces, cots)

    @pl.when(step < blocks)
    def _():
        here = pl.ds(pl.multiple_of(step * block, 16), block)
        attn = mm(ctx_ref[...], out_w[...]) + bias_ref[0:1]
        hat, scale = normalise(x_ref[...].astype(F32) + attn)
        normed = hat * bias_ref[1:2] + bias_ref[2:3]
        low = normed.astype(BF)
        lows[here, :] = low
        branch = bias_ref[3:4]
        for n in range(parts):
            part = slice(n * dim, (n + 1) * dim)
            act, grad = gelu_pair(mm(low, up_w[:, part]) + up_b[:, part])
            slope[:, part] = grad
            act = act.astype(BF)
            acts[n, here, :] = act
            branch = branch + mm(act, down_w[part, :])
        final_hat, final_scale = normalise(normed + branch)
        final_ref[...] = (final_hat * bias_ref[4:5] + bias_ref[5:6]).astype(BF)
        cot = cots[here, :].astype(F32)
        d_sum = normalise_back(final_hat, final_scale, cot * bias_ref[4:5])
        d_branch = d_sum.astype(BF)
        d_branches[here, :] = d_branch
        d_normed = d_sum
        for n in range(parts):
            part = slice(n * dim, (n + 1) * dim)
            d_pre = (against(d_branch, down_w[part, :]) * slope[:, part]).astype(BF)
            d_pres[n, here, :] = d_pre
            upsum_ref[:, part] += total(d_pre.astype(F32))
            d_normed = d_normed + against(d_pre, up_w[:, part])
        d_mid = normalise_back(hat, scale, d_normed * bias_ref[1:2])
        dmid_ref[...] = d_mid
        d_attn = d_mid.astype(BF)
        dattn_ref[...] = d_attn
        d_attns[here, :] = d_attn
        sums_ref[...] += jnp.concatenate(
            [
                total(d_attn.astype(F32)),
                total(d_normed * hat),
                total(d_normed),
                total(d_branch.astype(F32)),
                total(cot * final_hat),
                total(cot),
                jnp.zeros((2, dim), F32),
            ],
            axis=0,
        )

    @pl.when(step == blocks)
    def _():
        lows_t[...] = lows[...].astype(F32).T.astype(BF)

    @pl.when((step >= blocks) & (step < blocks + parts))
    def _():
        n = step - blocks
        down_ref[...] = inner(acts[n], d_branches[...]).astype(BF)
        up_ref[...] = mm(lows_t[...], d_pres[n]).astype(BF)

    @pl.when(step == blocks + parts)
    def _():
        out_ref[...] = mm(ctxt_ref[:, 0:seq], d_attns[...]).astype(BF)


def rows_pass(pieces, x, ctx, ctx_t, out_w, up_w, down_w, bias, up_b):
    seq, dim = ctx.shape
    ff = up_w.shape[1]
    blocks = 4
    block = seq // blocks
    parts = ff // dim

    def row(width):
        return pl.BlockSpec((block, width), lambda p: (jnp.minimum(p, blocks - 1), 0))

    def whole(a):
        return pl.BlockSpec(a.shape, lambda p: (0,) * a.ndim, pipeline_mode=pl.Buffered(1))

    def part(p):
        return jnp.clip(p - blocks, 0, parts - 1)

    shape = jax.ShapeDtypeStruct
    return pl.pallas_call(
        partial(rows_kernel, len(pieces), blocks),
        grid=(blocks + parts + 1,),
        in_specs=[whole(a) for a in pieces]
        + [row(dim), row(dim)]
        + [whole(a) for a in (ctx_t, out_w, up_w, down_w, bias, up_b)],
        out_specs=[
            row(dim),
            row(dim),
            row(dim),
            pl.BlockSpec((dim, dim), lambda p: (0, part(p))),
            pl.BlockSpec((dim, dim), lambda p: (part(p), 0)),
            pl.BlockSpec((dim, dim), lambda p: (0, 0)),
            pl.BlockSpec((8, dim), lambda p: (0, 0)),
            pl.BlockSpec((1, ff), lambda p: (0, 0)),
        ],
        out_shape=[
            shape((seq, dim), BF),
            shape((seq, dim), F32),
            shape((seq, dim), BF),
            shape((dim, ff), BF),
            shape((ff, dim), BF),
            shape((dim, dim), BF),
            shape((8, dim), F32),
            shape((1, ff), F32),
        ],
        scratch_shapes=[
            pltpu.VMEM((block, ff), F32),
            pltpu.VMEM((seq, dim), BF),
            pltpu.VMEM((seq, dim), BF),
            pltpu.VMEM((parts, seq, dim), BF),
            pltpu.VMEM((seq, dim), BF),
            pltpu.VMEM((parts, seq, dim), BF),
            pltpu.VMEM((dim, seq), BF),
            pltpu.VMEM((seq, dim), BF),
        ],
        compiler_params=pltpu.CompilerParams(vmem_limit_bytes=VMEM_BYTES),
        cost_estimate=pl.CostEstimate(
            flops=56 * seq * dim * dim, bytes_accessed=64 * seq * dim, transcendentals=seq * ff
        ),
    )(*pieces, x, ctx, ctx_t, out_w, up_w, down_w, bias, up_b)


def qkv_kernel(held, x_ref, dqkv_ref, out_ref, *refs):
    grad_ref, sums_ref, x_t = refs[held:]
    step = pl.program_id(0)

    @pl.when(step == 0)
    def _():
        x_t[...] = x_ref[...].astype(F32).T.astype(BF)

    @pl.when(step < 3)
    def _():
        grad_ref[...] = mm(x_t[...], dqkv_ref[0]).astype(BF)
        sums_ref[0] = jnp.broadcast_to(total(dqkv_ref[0].astype(F32)), sums_ref.shape[1:])

    @pl.when(step == 3)
    def _():
        grad_ref[...] = out_ref[...]


def qkv_sums(room, held, x, d_qkv, out_low):
    _, seq, dim = d_qkv.shape

    def whole(a):
        return pl.BlockSpec(a.shape, lambda p: (0,) * a.ndim, pipeline_mode=pl.Buffered(1))

    shape = jax.ShapeDtypeStruct
    return pl.pallas_call(
        partial(qkv_kernel, len(held)),
        grid=(4,),
        in_specs=[
            whole(x),
            pl.BlockSpec((1, seq, dim), lambda p: (jnp.minimum(p, 2), 0, 0)),
            whole(out_low),
        ]
        + [pl.BlockSpec(memory_space=pl.ANY)] * len(held),
        out_specs=[
            pl.BlockSpec((dim, dim), lambda p: (p, 0)),
            pl.BlockSpec((1, 8, dim), lambda p: (jnp.minimum(p, 2), 0, 0)),
        ],
        out_shape=[shape((4 * dim + room, dim), BF), shape((3, 8, dim), F32)],
        scratch_shapes=[pltpu.VMEM((dim, seq), BF)],
        compiler_params=pltpu.CompilerParams(vmem_limit_bytes=VMEM_BYTES),
        cost_estimate=pl.CostEstimate(
            flops=8 * seq * dim * dim, bytes_accessed=24 * seq * dim, transcendentals=0
        ),
    )(x, d_qkv, out_low, *held)


def rows_grad_kernel(dqkv_ref, weight_ref, dmid_ref, drows_ref, sum_ref):
    step = pl.program_id(0)

    @pl.when(step == 0)
    def _():
        sum_ref[...] = dmid_ref[...]

    sum_ref[...] += against(dqkv_ref[0], weight_ref[0])

    @pl.when(step == 2)
    def _():
        drows_ref[...] = sum_ref[...].astype(BF)


def rows_grad(d_qkv, weights, d_mid):
    _, seq, dim = d_qkv.shape
    return pl.pallas_call(
        rows_grad_kernel,
        grid=(3,),
        in_specs=[
            pl.BlockSpec((1, seq, dim), lambda p: (p, 0, 0)),
            pl.BlockSpec((1, dim, dim), lambda p: (p, 0, 0)),
            pl.BlockSpec((seq, dim), lambda p: (0, 0), pipeline_mode=pl.Buffered(1)),
        ],
        out_specs=pl.BlockSpec((seq, dim), lambda p: (0, 0)),
        out_shape=jax.ShapeDtypeStruct((seq, dim), BF),
        scratch_shapes=[pltpu.VMEM((seq, dim), F32)],
        compiler_params=pltpu.CompilerParams(vmem_limit_bytes=VMEM_BYTES),
        cost_estimate=pl.CostEstimate(
            flops=6 * seq * dim * dim, bytes_accessed=16 * seq * dim, transcendentals=0
        ),
    )(d_qkv, weights, d_mid)


def bucket_select(table):
    reach = (table.shape[0] - 1) // 2
    spots = jnp.arange(4 * reach, dtype=jnp.int32)
    bucket = jnp.clip(spots[None, :] - spots[:, None], -reach, reach) + reach
    return bucket[None] == jnp.arange(2 * reach + 1, dtype=jnp.int32)[:, None, None]


def spread_table(table):
    span = 2 * (table.shape[0] - 1)
    spread = lax.dot_general(
        table.astype(BF),
        bucket_select(table).astype(BF).reshape(table.shape[0], -1),
        (((0,), (0,)), ((), ())),
        preferred_element_type=F32,
    )
    return spread.astype(BF).reshape(HEADS, span, span)


def gather_table(spread, table):
    reach = (table.shape[0] - 1) // 2
    distance = jnp.arange(spread.shape[1], dtype=jnp.int32) - (4 * reach - 1)
    bucket = jnp.clip(distance, -reach, reach) + reach
    select = bucket[None, :] == jnp.arange(table.shape[0], dtype=jnp.int32)[:, None]
    return lax.dot_general(
        select.astype(F32),
        spread,
        (((1,), (1,)), ((), ())),
        precision=lax.Precision.HIGHEST,
        preferred_element_type=F32,
    )


def shift_pairs(size, step):
    return [(i, (i + step) % size) for i in range(size)]


def flip_pairs(size, step):
    return [(i, i ^ step) for i in range(size)]


def pick(array, index):
    return lax.dynamic_index_in_dim(array, index, 0, keepdims=False)


def swap_text(parts):
    return lax.all_to_all(parts, "wide", split_axis=0, concat_axis=0, tiled=True)


def patch_order(size):
    me = lax.axis_index("narrow")
    return [me ^ k for k in range(size)]


def swap_patch(parts):
    size = parts.shape[0]
    me = lax.axis_index("narrow")
    return [pick(parts, me)] + [
        lax.ppermute(pick(parts, me ^ k), "narrow", flip_pairs(size, k)) for k in range(1, size)
    ]


def flip_axis(array, axis, bit):
    return jnp.where(bit == 1, jnp.flip(array, axis), array)


def from_flipped(parts, me):
    size = parts.shape[0]
    bits = size.bit_length() - 1
    parts = parts.reshape((2,) * bits + parts.shape[1:])
    for b in range(bits):
        parts = flip_axis(parts, bits - 1 - b, (me >> b) & 1)
    return parts.reshape((size,) + parts.shape[bits:])


def patch_away(rows, size):
    parts = rows.reshape(size, -1, rows.shape[1])
    return [parts[0]] + [
        lax.ppermute(parts[k], "narrow", flip_pairs(size, k)) for k in range(1, size)
    ]


def patch_set(pieces, shape):
    return from_flipped(jnp.stack(pieces), lax.axis_index("narrow")).reshape(shape)


def add(*terms):
    total = terms[0].astype(F32)
    for term in terms[1:]:
        total = total + term.astype(F32)
    return total.astype(BF)


def wide_orders(wide, ways):
    bits = list(range(1, wide.bit_length() - 1))
    return [bits, bits[::-1]][:ways]


def wide_bit(bit):
    return (lax.axis_index("wide") >> bit) & 1


def add_kernel(me_ref, own_ref, arrived_ref, *refs):
    refs[-1][...] = (own_ref[0].astype(F32) + arrived_ref[...].astype(F32)).astype(BF)


def add_own(parts, me, arrived, held):
    rows, columns = arrived.shape
    steps = 2 if rows % 32 == 0 else 1
    block = rows // steps
    return pl.pallas_call(
        add_kernel,
        grid_spec=pltpu.PrefetchScalarGridSpec(
            num_scalar_prefetch=1,
            grid=(steps,),
            in_specs=[
                pl.BlockSpec((1, block, columns), lambda i, me_ref: (me_ref[0], i, 0)),
                pl.BlockSpec((block, columns), lambda i, me_ref: (i, 0)),
            ]
            + [pl.BlockSpec(memory_space=pl.ANY)] * len(held),
            out_specs=pl.BlockSpec((block, columns), lambda i, me_ref: (i, 0)),
        ),
        out_shape=jax.ShapeDtypeStruct((rows, columns), BF),
        compiler_params=pltpu.CompilerParams(vmem_limit_bytes=VMEM_BYTES),
        cost_estimate=pl.CostEstimate(flops=0, bytes_accessed=6 * rows * columns, transcendentals=0),
    )(me.reshape(1), parts, arrived, *held)


def wide_step(grad, wide, bit, held=()):
    parts = grad.reshape(2, -1, grad.shape[1])
    me = wide_bit(bit)
    arrived = lax.ppermute(pick(parts, 1 - me), "wide", flip_pairs(wide, 1 << bit))
    return add_own(parts, me, arrived, held) if held else add(pick(parts, me), arrived)


def cut(grad, parts):
    first = -(-grad.shape[0] // (16 * parts)) * 8 * parts
    return [grad[:first], grad[first:]]


def wide_steps(shares, wide, i, held=()):
    orders = wide_orders(wide, len(shares))
    return [
        wide_step(a, wide, order[i], held if n == 0 else ())
        for n, (a, order) in enumerate(zip(shares, orders))
    ]


def narrow_step(shares, narrow):
    me = lax.axis_index("narrow")
    parts = [a.reshape(narrow, -1, a.shape[1]) for a in shares]

    def picked(index):
        return jnp.concatenate([pick(a, index) for a in parts], axis=0)

    arrived = [
        lax.ppermute(picked(me ^ k), "narrow", flip_pairs(narrow, k)) for k in range(1, narrow)
    ]
    return add(picked(me), *arrived)


def gather_narrow(part, narrow, lengths):
    parts = [part] + [
        lax.ppermute(part, "narrow", flip_pairs(narrow, k)) for k in range(1, narrow)
    ]
    parts = jnp.stack(parts)
    return [parts[:, : lengths[0]], parts[:, lengths[0] :]]


def gather_wide(shares, wide, i):
    return [
        jnp.concatenate([a, lax.ppermute(a, "wide", flip_pairs(wide, 1 << order[i]))], axis=0)
        for a, order in zip(shares, wide_orders(wide, len(shares)))
    ]


def gather_core(shares, wide):
    return shares + [lax.ppermute(a, "wide", flip_pairs(wide, 1)) for a in shares]


def finish_kernel(places, ways, cuts, index_ref, up_ref, down_ref, *refs):
    pieces, outs = refs[: 2 * ways], refs[2 * ways :]
    *outs, up_out, down_out = outs
    up_out[...] = up_ref[...].astype(F32)
    down_out[...] = down_ref[...].astype(F32)

    @pl.when(pl.program_id(0) == 0)
    def _():
        put_pieces(places, ways, cuts, index_ref, pieces, outs)


def put_pieces(places, ways, cuts, index_ref, pieces, outs):
    at = 0
    for core in range(2):
        for way in range(ways):
            rows = pieces[way].shape[1]
            for place in range(places):
                here = index_ref[way, place]
                for (start, stop), out in zip(cuts, outs):
                    low, high = max(at, start), min(at + rows, stop)
                    if low < high:
                        same = pieces[way][here].astype(F32)
                        other = pieces[ways + way][here].astype(F32)
                        block = jnp.where(index_ref[2, 0] == core, same, other)
                        out[low - start : high - start, :] = block[low - at : high - at]
                at += rows


def finish(totals, pieces, wide, narrow, lengths):
    places, _, columns = pieces[0].shape
    ways = len(pieces) // 2
    index = []
    for order in wide_orders(wide, 2):
        me = jnp.int32(0)
        for bit in order:
            me = me * 2 + wide_bit(bit)
        me = me * narrow + lax.axis_index("narrow")
        index.append(jnp.arange(places, dtype=jnp.int32) ^ me)
    index.append(jnp.full((places,), wide_bit(0), jnp.int32))
    cuts = []
    for length in lengths:
        start = cuts[-1][1] if cuts else 0
        cuts.append((start, start + length))
    blocks = [pl.BlockSpec((a.shape[0] // 2, a.shape[1]), lambda p: (p, 0)) for a in totals]

    def whole(shape):
        return pl.BlockSpec(shape, lambda p: (0,) * len(shape), pipeline_mode=pl.Buffered(1))

    return pl.pallas_call(
        partial(finish_kernel, places, ways, cuts),
        grid=(2,),
        in_specs=[pl.BlockSpec(memory_space=pltpu.SMEM)]
        + blocks
        + [whole(a.shape) for a in pieces],
        out_specs=[whole((length, columns)) for length in lengths] + blocks,
        out_shape=[jax.ShapeDtypeStruct((length, columns), F32) for length in lengths]
        + [jax.ShapeDtypeStruct(a.shape, F32) for a in totals],
        compiler_params=pltpu.CompilerParams(vmem_limit_bytes=VMEM_BYTES),
        cost_estimate=pl.CostEstimate(
            flops=0,
            bytes_accessed=8 * sum(lengths) * columns + 6 * sum(a.size for a in totals),
            transcendentals=0,
        ),
    )(jnp.stack(index), *totals, *pieces)


def room_for(rows, wide, narrow):
    return 32 + -(rows + 32) % (8 * wide * narrow)


def pack(grads, columns, rows):
    lines = []
    for grad in grads:
        flat = grad.reshape(-1)
        lines.append(jnp.pad(flat, (0, -flat.shape[0] % columns)).reshape(-1, columns))
    lines = jnp.concatenate(lines, axis=0)
    return jnp.pad(lines, ((0, -lines.shape[0] % rows), (0, 0)))


def unpack(lines, grads):
    columns = lines.shape[1]
    at = 0
    out = []
    for grad in grads:
        count = -(-grad.size // columns)
        out.append(lines[at : at + count].reshape(-1)[: grad.size].reshape(grad.shape))
        at += count
    return out


def body(
    text_in,
    patch_in,
    res_class,
    text_len,
    pos_line,
    pos_x,
    pos_y,
    query_weight,
    query_bias,
    key_weight,
    value_weight,
    value_bias,
    output_weight,
    output_bias,
    norm_gain,
    norm_shift,
    up_weight,
    up_bias,
    down_weight,
    down_bias,
    final_gain,
    final_shift,
    line_table,
    width_table,
    height_table,
    cot_text,
    cot_patch,
):
    text_shape = text_in.shape
    patch_shape = patch_in.shape
    dim = text_shape[3]
    seq = TEXT + PATCH
    lanes = -(-seq // 128) * 128
    wide = text_shape[0]
    narrow = patch_shape[1]
    pieces = [swap_text(text_in.reshape(wide, -1, dim)).reshape(-1, dim)]
    pieces += swap_patch(patch_in.reshape(narrow, -1, dim))
    cot_text, pieces[0] = lax.optimization_barrier((cot_text, pieces[0]))
    cot_patch, pieces = lax.optimization_barrier((cot_patch, pieces))
    cots = [swap_text(cot_text.reshape(wide, -1, dim)).reshape(-1, dim)]
    cots += swap_patch(cot_patch.reshape(narrow, -1, dim))
    index = jnp.arange(seq, dtype=jnp.int32)
    live_patch = jnp.where(res_class.reshape(()) == 1, PATCH, SMALL_PATCH)
    valid = jnp.where(index < TEXT, index < text_len.reshape(()), index - TEXT < live_patch)
    facts = jnp.concatenate(
        [pos_line.reshape(1, -1), pos_x.reshape(1, -1), pos_y.reshape(1, -1), valid.astype(jnp.int32)[None]]
    )
    patch_facts = facts[:, TEXT:].reshape(4, narrow, -1)
    facts = jnp.concatenate(
        [facts[:, :TEXT]]
        + [
            lax.dynamic_index_in_dim(patch_facts, i, 1, keepdims=False)
            for i in patch_order(narrow)
        ],
        axis=1,
    )
    line_spots, x_spots, y_spots = facts[0], facts[1], facts[2]
    valid = facts[3] == 1

    line = spread_table(line_table)
    width = spread_table(width_table)
    height = spread_table(height_table)
    hots = []
    hots_t = []
    hots_back = []
    for spots, table in ((line_spots, line_table), (x_spots, width_table), (y_spots, height_table)):
        span = jnp.arange(2 * (table.shape[0] - 1), dtype=jnp.int32)
        long = jnp.pad(spots, (0, lanes - seq), constant_values=-1)
        hots.append((long[:, None] == span[None, :]).astype(BF))
        hots_t.append((long[None, :] == span[:, None]).astype(BF))
        hots_back.append((long[None, :] == span[::-1, None]).astype(BF))
    hot = jnp.concatenate(hots, axis=1)
    hot_t = jnp.concatenate(hots_t, axis=0)
    hot_back = jnp.concatenate(hots_back, axis=0)
    column = jnp.arange(128, dtype=jnp.int32)
    mask = jnp.where((column[None, :] % 64 == 0) & ~valid[:, None], -1e30, 0.0).astype(BF)

    exps, ctx_t, ctx, inverse, q, k_t, v, rows_in = attend(
        pieces,
        query_weight,
        key_weight,
        value_weight,
        jnp.stack([query_bias, value_bias])[:, None],
        hot,
        mask,
        hot_t,
        line,
        width,
        height,
    )
    vectors = jnp.stack(
        [output_bias, norm_gain, norm_shift, down_bias, final_gain, final_shift] + [final_shift] * 2
    )
    final_low, d_mid, d_attn, up_low, down_low, out_low, sums, up_sum = rows_pass(
        cots, rows_in, ctx, ctx_t, output_weight, up_weight, down_weight, vectors, up_bias[None]
    )
    early = (sums[0], sums[1], sums[2], up_sum, sums[3], sums[4], sums[5])
    down_total, up_total = lax.psum((down_low, up_low), ("wide", "narrow"))
    qkv_weight = jnp.stack([query_weight, key_weight, value_weight])

    def backward():
        text_out = swap_text(final_low[:TEXT].reshape(wide, -1, dim)).reshape(text_shape)
        out_pieces = patch_away(final_low[TEXT:], narrow)
        levels = wide.bit_length() - 2
        d_qkv, spread = attend_back(
            0, HEADS // 2, [], exps, ctx_t, inverse, v, k_t, q, d_attn, output_weight, hot, hot_back
        )
        room = room_for(4 * dim, wide, narrow)
        tail, d_sums = qkv_sums(room, [text_out, *out_pieces[1:]], rows_in, d_qkv, out_low)
        d_rows = rows_grad(d_qkv, qkv_weight, d_mid)
        text_grad = swap_text(d_rows[:TEXT].reshape(wide, -1, dim)).reshape(text_shape)
        grad_pieces = patch_away(d_rows[TEXT:], narrow)
        late = (
            d_sums[0, 0],
            d_sums[2, 0],
            gather_table(spread[:, 2], line_table),
            gather_table(spread[:, 0], width_table),
            gather_table(spread[:, 1], height_table),
        )
        small = pack(early + late, dim, room).astype(BF)
        tail = lax.dynamic_update_slice(tail, small, (4 * dim, 0))
        halves = cut(wide_step(tail, wide, 0), wide * narrow // 2)
        for i in range(levels):
            moved = [text_grad, *grad_pieces[1:]] if i == levels - 1 else []
            halves = wide_steps(halves, wide, i, moved)
        lengths = [a.shape[0] // narrow for a in halves]
        halves = gather_narrow(narrow_step(halves, narrow), narrow, lengths)
        for i in range(levels - 1, -1, -1):
            halves = gather_wide(halves, wide, i)
        return (
            text_out, patch_set(out_pieces, patch_shape), text_grad,
            patch_set(grad_pieces, patch_shape), *gather_core(halves, wide),
        )

    def never():
        return jax.tree.map(lambda a: jnp.zeros(a.shape, a.dtype), jax.eval_shape(backward))

    text_out, patch_out, text_grad, patch_grad, *pieces = lax.cond(
        text_len.reshape(()) >= 0, backward, never
    )
    (
        query_weight_grad, key_weight_grad, value_weight_grad, output_weight_grad, small,
        up_weight_grad, down_weight_grad,
    ) = finish((up_total, down_total), pieces, wide, narrow, (dim,) * 4 + (32,))
    late = (query_bias, value_bias, line_table, width_table, height_table)
    (
        output_bias_grad, norm_gain_grad, norm_shift_grad, up_bias_grad, down_bias_grad,
        final_gain_grad, final_shift_grad, query_bias_grad, value_bias_grad, line_table_grad,
        width_table_grad, height_table_grad,
    ) = unpack(small, early + late)
    up_bias_grad = up_bias_grad.reshape(-1)
    return (
        text_out,
        patch_out,
        text_grad,
        patch_grad,
        query_weight_grad,
        query_bias_grad,
        key_weight_grad,
        value_weight_grad,
        value_bias_grad,
        output_weight_grad,
        output_bias_grad,
        norm_gain_grad,
        norm_shift_grad,
        up_weight_grad,
        up_bias_grad,
        down_weight_grad,
        down_bias_grad,
        final_gain_grad,
        final_shift_grad,
        line_table_grad,
        width_table_grad,
        height_table_grad,
    )


def solution(mesh):
    text = P(None, "narrow", "wide", None)
    patch = P("wide", None, "narrow", None)
    page = P("wide", "narrow")
    spots = P("wide", "narrow", None)
    in_specs = (text, patch, page, page, spots, spots, spots) + (P(),) * 18 + (text, patch)
    out_specs = (text, patch, text, patch) + (P(),) * 18
    return jax.shard_map(body, mesh=mesh, in_specs=in_specs, out_specs=out_specs, check_vma=False)
```

```python
from functools import partial

import jax
import jax.numpy as jnp
from jax import lax
from jax.experimental import pallas as pl
from jax.experimental.pallas import tpu as pltpu
from jax.sharding import PartitionSpec as P

HEADS = 12
TEXT = 512
PATCH = 576
SMALL_PATCH = 196
BF = jnp.bfloat16
F32 = jnp.float32
VMEM_BYTES = 60 * 2**20


def mm(left, right):
    return lax.dot_general(left, right, (((1,), (0,)), ((), ())), preferred_element_type=F32)


def inner(left, right):
    return lax.dot_general(left, right, (((0,), (0,)), ((), ())), preferred_element_type=F32)


def against(left, right):
    return lax.dot_general(left, right, (((1,), (1,)), ((), ())), preferred_element_type=F32)


def assemble(pieces, rows):
    at = 0
    for piece in pieces:
        rows[at : at + piece.shape[0], :] = piece[...]
        at += piece.shape[0]


def attend_kernel(count, *refs):
    pieces = refs[:count]
    (
        qw_ref, kw_ref, vw_ref, bias_ref, hot_ref, mask_ref, hott_ref, line_ref, width_ref,
        height_ref, exp_ref, ctxt_ref, ctx_ref, inv_ref, q_ref, kt_ref, v_ref, x_ref,
        keys, queries, values, rows,
    ) = refs[count:]
    seq = v_ref.shape[0]
    lanes = rows.shape[0]

    @pl.when(pl.program_id(0) == 0)
    def _():
        keys[:, 0:320] = hot_ref[0:seq, :]
        values[64:80, :] = jnp.ones((16, seq), BF)
        assemble(pieces, rows)
        rows[seq:lanes, :] = jnp.zeros((lanes - seq, rows.shape[1]), BF)
        x_ref[...] = rows[0:seq, :]

    both = mm(rows[...], jnp.concatenate([qw_ref[...], kw_ref[...]], axis=1))
    q = ((both[:, 0:128] + bias_ref[0]) * 0.125).astype(BF)
    k = both[:, 128:256].astype(BF)
    v = (mm(rows[...], vw_ref[...]) + bias_ref[1]).astype(BF)
    q_ref[...] = q
    v_ref[...] = v[0:seq]
    q_t = q.astype(F32).T.astype(BF)
    k = k.astype(F32)
    kt_ref[...] = k.T[:, 0:seq].astype(BF)
    v_t = v.astype(F32).T[:, 0:seq].astype(BF)
    lane = lax.broadcasted_iota(jnp.int32, (seq, 128), 1)
    contexts = []
    for h in range(2):
        mine = (lane < 64) if h == 0 else (lane >= 64)
        own, other = (320, 384) if h == 0 else (384, 320)
        keys[:, 320:448] = jnp.where(mine, k[0:seq], mask_ref[...].astype(F32)).astype(BF)
        queries[own : own + 64, :] = q_t[h * 64 : h * 64 + 64, :]
        queries[other : other + 64, :] = jnp.ones((64, lanes), BF)
        values[0:64, :] = v_t[h * 64 : h * 64 + 64, :]
        queries[0:64, :] = mm(line_ref[h], hott_ref[0:64, :]).astype(BF)
        queries[64:192, :] = mm(width_ref[h], hott_ref[64:192, :]).astype(BF)
        queries[192:320, :] = mm(height_ref[h], hott_ref[192:320, :]).astype(BF)
        scores = mm(keys[...], queries[...])
        peak = jnp.max(scores, axis=0, keepdims=True)
        weights = jnp.exp(scores - peak).astype(BF)
        exp_ref[h] = weights
        ctx = mm(values[...], weights)
        inverse = 1.0 / ctx[64:65]
        inv_ref[h] = inverse
        contexts.append(ctx[0:64] * inverse)
    ctx = jnp.concatenate(contexts, axis=0)
    ctxt_ref[...] = ctx.astype(BF)
    ctx_ref[...] = ctx.T[0:seq].astype(BF)


def attend(pieces, q_weight, k_weight, v_weight, bias, hot, mask, hot_t, line, width, height):
    seq = mask.shape[0]
    lanes, dim = hot.shape[0], q_weight.shape[0]

    def whole(a):
        return pl.BlockSpec(a.shape, lambda p: (0,) * a.ndim, pipeline_mode=pl.Buffered(1))

    def pair(a):
        return pl.BlockSpec((2,) + a.shape[1:], lambda p: (p, 0, 0))

    def columns(rows):
        return pl.BlockSpec((rows, 128), lambda p: (0, p))

    def rows(length):
        return pl.BlockSpec((128, length), lambda p: (p, 0))

    shape = jax.ShapeDtypeStruct
    return pl.pallas_call(
        partial(attend_kernel, len(pieces)),
        grid=(HEADS // 2,),
        in_specs=[whole(a) for a in pieces]
        + [
            columns(dim),
            columns(dim),
            columns(dim),
            pl.BlockSpec((2, 1, 128), lambda p: (0, 0, p)),
            whole(hot),
            whole(mask),
            whole(hot_t),
            pair(line),
            pair(width),
            pair(height),
        ],
        out_specs=[
            pl.BlockSpec((2, seq, lanes), lambda p: (p, 0, 0)),
            rows(lanes),
            columns(seq),
            pl.BlockSpec((2, 1, lanes), lambda p: (p, 0, 0)),
            columns(lanes),
            rows(seq),
            columns(seq),
            pl.BlockSpec((seq, dim), lambda p: (0, 0)),
        ],
        out_shape=[
            shape((HEADS, seq, lanes), BF),
            shape((dim, lanes), BF),
            shape((seq, dim), BF),
            shape((HEADS, 1, lanes), F32),
            shape((lanes, dim), BF),
            shape((dim, seq), BF),
            shape((seq, dim), BF),
            shape((seq, dim), BF),
        ],
        scratch_shapes=[
            pltpu.VMEM((seq, 448), BF),
            pltpu.VMEM((448, lanes), BF),
            pltpu.VMEM((80, seq), BF),
            pltpu.VMEM((lanes, dim), BF),
        ],
        compiler_params=pltpu.CompilerParams(vmem_limit_bytes=VMEM_BYTES),
        cost_estimate=pl.CostEstimate(
            flops=HEADS * seq * lanes * 4096, bytes_accessed=HEADS * seq * lanes * 2,
            transcendentals=HEADS * seq * lanes,
        ),
    )(*pieces, q_weight, k_weight, v_weight, bias, hot, mask, hot_t, line, width, height)


def by_distance(sums, turn):
    if sums.shape[0] == sums.shape[1]:
        sums = jnp.concatenate([sums, jnp.zeros_like(sums)], axis=1)
    sums = pltpu.roll(sums, turn, 1, stride=1, stride_axis=0)
    sums = jnp.sum(sums, axis=0, keepdims=True)
    if sums.shape[1] < 256:
        sums = jnp.concatenate([sums, jnp.zeros_like(sums)], axis=1)
    return sums


def attend_back_kernel(held, *refs):
    (
        exp_ref, ctxt_ref, inv_ref, v_ref, kt_ref, q_ref, dattn_ref, outw_ref, hot_ref, hott_ref,
        dqkv_ref, spread_ref, values, dctx, lefts, rights, ds, dattn,
    ) = refs[:10] + refs[10 + held :]
    seq = v_ref.shape[0]
    lanes = q_ref.shape[0]

    @pl.when(pl.program_id(0) == 0)
    def _():
        for h in range(2):
            lefts[h, 64:192, :] = hott_ref[64:192, 0:seq]
            rights[h, :, 128:256] = hot_ref[:, 192:320]
        dattn[0:seq, :] = dattn_ref[...]
        dattn[seq:lanes, :] = jnp.zeros((lanes - seq, dattn.shape[1]), BF)

    lane = lax.broadcasted_iota(jnp.int32, (seq, 128), 1)
    query_lane = lax.broadcasted_iota(jnp.int32, (lanes, 128), 1)
    row = lax.broadcasted_iota(jnp.int32, (64, lanes), 0)
    line_hot = jnp.concatenate([hot_ref[:, 0:64], hot_ref[:, 0:64]], axis=1).astype(F32)
    d_rows_t = against(outw_ref[...], dattn[...])
    d_rows_t = [d_rows_t[h * 64 : h * 64 + 64] * inv_ref[h] for h in range(2)]
    d_rows = jnp.concatenate(d_rows_t, axis=0).T.astype(BF)
    results = []
    by_queries = []
    for h in range(2):
        mine = (lane < 64) if h == 0 else (lane >= 64)
        query_mine = (query_lane < 64) if h == 0 else (query_lane >= 64)
        own, other = (0, 64) if h == 0 else (64, 0)
        part = slice(h * 64, h * 64 + 64)
        values[h] = jnp.where(mine, v_ref[...].astype(F32), 1.0).astype(BF)
        delta = -jnp.sum(d_rows_t[h] * ctxt_ref[part, :].astype(F32), axis=0, keepdims=True)
        high = delta.astype(BF).astype(F32)
        extra = jnp.where(row == 0, high, jnp.where(row == 1, delta - high, 0.0))
        dctx[h, own : own + 64, :] = d_rows_t[h].astype(BF)
        dctx[h, other : other + 64, :] = extra.astype(BF)
        lefts[h, 0:64, :] = kt_ref[part, :]
        rights[h, :, 0:128] = jnp.where(query_mine, q_ref[...].astype(F32), line_hot).astype(BF)
        d_scores = mm(values[h], dctx[h])
        ds[h] = (exp_ref[h].astype(F32) * d_scores).astype(BF)
        by_query = mm(lefts[h], ds[h])
        by_queries.append(by_query[0:64] * 0.125)
        by_key = mm(ds[h], rights[h])
        width = mm(by_query[64:192].astype(BF), hot_ref[:, 64:192])
        height = mm(hott_ref[192:320, 0:seq], by_key[:, 128:256].astype(BF))
        near = mm(hott_ref[0:64, 0:seq], by_key[:, 0:128].astype(BF))
        spread_ref[h, 0:1, :] = by_distance(width, 0)
        spread_ref[h, 1:2, :] = by_distance(height, 0)
        line_lane = lax.broadcasted_iota(jnp.int32, near.shape, 1)
        near = jnp.where((line_lane >= 64) if h == 0 else (line_lane < 64), near, 0.0)
        spread_ref[h, 2:3, :] = by_distance(near, 64 if h == 0 else 0)
        results.append((by_key[:, 0:128], mm(exp_ref[h], d_rows)))
    dqkv_ref[0] = jnp.concatenate(by_queries, axis=0).T[0:seq].astype(BF)
    dqkv_ref[1] = jnp.where(lane < 64, results[0][0], results[1][0]).astype(BF)
    dqkv_ref[2] = jnp.where(lane < 64, results[0][1], results[1][1]).astype(BF)


def attend_back(first, pairs, held, exps, ctx_t, inverse, v, k_t, q, d_attn, out_weight, hot, hot_t):
    seq, dim = v.shape
    lanes = q.shape[0]

    def whole(a):
        return pl.BlockSpec(a.shape, lambda p: (0,) * a.ndim, pipeline_mode=pl.Buffered(1))

    def columns(rows):
        return pl.BlockSpec((rows, 128), lambda p: (0, p + first))

    def rows(length):
        return pl.BlockSpec((128, length), lambda p: (p + first, 0))

    def pair(*shape, start=first):
        return pl.BlockSpec((2,) + shape, lambda p: (p + start, 0, 0))

    shape = jax.ShapeDtypeStruct
    return pl.pallas_call(
        partial(attend_back_kernel, len(held)),
        grid=(pairs,),
        in_specs=[
            pair(seq, lanes),
            rows(lanes),
            pair(1, lanes),
            columns(seq),
            rows(seq),
            columns(lanes),
            whole(d_attn),
            rows(dim),
            whole(hot),
            whole(hot_t),
        ]
        + [pl.BlockSpec(memory_space=pl.ANY)] * len(held),
        out_specs=[
            pl.BlockSpec((3, seq, 128), lambda p: (0, 0, p)),
            pair(3, 256, start=0),
        ],
        out_shape=[
            shape((3, seq, 128 * pairs), BF),
            shape((2 * pairs, 3, 256), F32),
        ],
        scratch_shapes=[
            pltpu.VMEM((2, seq, 128), BF),
            pltpu.VMEM((2, 128, lanes), BF),
            pltpu.VMEM((2, 192, seq), BF),
            pltpu.VMEM((2, lanes, 256), BF),
            pltpu.VMEM((2, seq, lanes), BF),
            pltpu.VMEM((lanes, dim), BF),
        ],
        compiler_params=pltpu.CompilerParams(vmem_limit_bytes=VMEM_BYTES),
        cost_estimate=pl.CostEstimate(
            flops=2 * pairs * seq * lanes * 4096, bytes_accessed=4 * pairs * seq * lanes,
            transcendentals=0,
        ),
    )(exps, ctx_t, inverse, v, k_t, q, d_attn, out_weight, hot, hot_t, *held)


def gelu_pair(x):
    bell = jnp.exp(x * x * -0.5)
    t = 1.0 / (1.0 + 0.23164189 * jnp.abs(x))
    poly = t * (0.127414796 + t * (-0.142248368 + t * (0.7107068705 + t * (-0.7265760135 + t * 0.5307027145))))
    upper = poly * bell
    phi = jnp.where(x < 0, upper, 1.0 - upper)
    return x * phi, phi + x * bell * 0.3989422804014327

def normalise(rows):
    mean = jnp.mean(rows, axis=-1, keepdims=True)
    centred = rows - mean
    scale = lax.rsqrt(jnp.mean(centred * centred, axis=-1, keepdims=True) + 1e-05)
    return centred * scale, scale

def normalise_back(hat, scale, d_hat):
    return scale * (d_hat - jnp.mean(d_hat, axis=-1, keepdims=True) - hat * jnp.mean(d_hat * hat, axis=-1, keepdims=True))

def total(rows):
    return jnp.sum(rows, axis=0, keepdims=True)


def rows_kernel(count, blocks, *refs):
    pieces = refs[:count]
    (
        x_ref, ctx_ref, ctxt_ref, out_w, up_w, down_w, bias_ref, up_b,
        final_ref, dmid_ref, dattn_ref, up_ref, down_ref, out_ref, sums_ref, upsum_ref,
        slope, cots, lows, acts, d_branches, d_pres, lows_t, d_attns,
    ) = refs[count:]
    step = pl.program_id(0)
    block = x_ref.shape[0]
    seq, dim = cots.shape
    parts = acts.shape[0]

    @pl.when(step == 0)
    def _():
        sums_ref[...] = jnp.zeros_like(sums_ref)
        upsum_ref[...] = jnp.zeros_like(upsum_ref)
        assemble(pieces, cots)

    @pl.when(step < blocks)
    def _():
        here = pl.ds(pl.multiple_of(step * block, 16), block)
        attn = mm(ctx_ref[...], out_w[...]) + bias_ref[0:1]
        hat, scale = normalise(x_ref[...].astype(F32) + attn)
        normed = hat * bias_ref[1:2] + bias_ref[2:3]
        low = normed.astype(BF)
        lows[here, :] = low
        branch = bias_ref[3:4]
        for n in range(parts):
            part = slice(n * dim, (n + 1) * dim)
            act, grad = gelu_pair(mm(low, up_w[:, part]) + up_b[:, part])
            slope[:, part] = grad
            act = act.astype(BF)
            acts[n, here, :] = act
            branch = branch + mm(act, down_w[part, :])
        final_hat, final_scale = normalise(normed + branch)
        final_ref[...] = (final_hat * bias_ref[4:5] + bias_ref[5:6]).astype(BF)
        cot = cots[here, :].astype(F32)
        d_sum = normalise_back(final_hat, final_scale, cot * bias_ref[4:5])
        d_branch = d_sum.astype(BF)
        d_branches[here, :] = d_branch
        d_normed = d_sum
        for n in range(parts):
            part = slice(n * dim, (n + 1) * dim)
            d_pre = (against(d_branch, down_w[part, :]) * slope[:, part]).astype(BF)
            d_pres[n, here, :] = d_pre
            upsum_ref[:, part] += total(d_pre.astype(F32))
            d_normed = d_normed + against(d_pre, up_w[:, part])
        d_mid = normalise_back(hat, scale, d_normed * bias_ref[1:2])
        dmid_ref[...] = d_mid
        d_attn = d_mid.astype(BF)
        dattn_ref[...] = d_attn
        d_attns[here, :] = d_attn
        sums_ref[...] += jnp.concatenate(
            [
                total(d_attn.astype(F32)),
                total(d_normed * hat),
                total(d_normed),
                total(d_branch.astype(F32)),
                total(cot * final_hat),
                total(cot),
                jnp.zeros((2, dim), F32),
            ],
            axis=0,
        )

    @pl.when(step == blocks)
    def _():
        lows_t[...] = lows[...].astype(F32).T.astype(BF)

    @pl.when((step >= blocks) & (step < blocks + parts))
    def _():
        n = step - blocks
        down_ref[...] = inner(acts[n], d_branches[...]).astype(BF)
        up_ref[...] = mm(lows_t[...], d_pres[n]).astype(BF)

    @pl.when(step == blocks + parts)
    def _():
        out_ref[...] = mm(ctxt_ref[:, 0:seq], d_attns[...]).astype(BF)


def rows_pass(pieces, x, ctx, ctx_t, out_w, up_w, down_w, bias, up_b):
    seq, dim = ctx.shape
    ff = up_w.shape[1]
    blocks = 4
    block = seq // blocks
    parts = ff // dim

    def row(width):
        return pl.BlockSpec((block, width), lambda p: (jnp.minimum(p, blocks - 1), 0))

    def whole(a):
        return pl.BlockSpec(a.shape, lambda p: (0,) * a.ndim, pipeline_mode=pl.Buffered(1))

    def part(p):
        return jnp.clip(p - blocks, 0, parts - 1)

    shape = jax.ShapeDtypeStruct
    return pl.pallas_call(
        partial(rows_kernel, len(pieces), blocks),
        grid=(blocks + parts + 1,),
        in_specs=[whole(a) for a in pieces]
        + [row(dim), row(dim)]
        + [whole(a) for a in (ctx_t, out_w, up_w, down_w, bias, up_b)],
        out_specs=[
            row(dim),
            row(dim),
            row(dim),
            pl.BlockSpec((dim, dim), lambda p: (0, part(p))),
            pl.BlockSpec((dim, dim), lambda p: (part(p), 0)),
            pl.BlockSpec((dim, dim), lambda p: (0, 0)),
            pl.BlockSpec((8, dim), lambda p: (0, 0)),
            pl.BlockSpec((1, ff), lambda p: (0, 0)),
        ],
        out_shape=[
            shape((seq, dim), BF),
            shape((seq, dim), F32),
            shape((seq, dim), BF),
            shape((dim, ff), BF),
            shape((ff, dim), BF),
            shape((dim, dim), BF),
            shape((8, dim), F32),
            shape((1, ff), F32),
        ],
        scratch_shapes=[
            pltpu.VMEM((block, ff), F32),
            pltpu.VMEM((seq, dim), BF),
            pltpu.VMEM((seq, dim), BF),
            pltpu.VMEM((parts, seq, dim), BF),
            pltpu.VMEM((seq, dim), BF),
            pltpu.VMEM((parts, seq, dim), BF),
            pltpu.VMEM((dim, seq), BF),
            pltpu.VMEM((seq, dim), BF),
        ],
        compiler_params=pltpu.CompilerParams(vmem_limit_bytes=VMEM_BYTES),
        cost_estimate=pl.CostEstimate(
            flops=56 * seq * dim * dim, bytes_accessed=64 * seq * dim, transcendentals=seq * ff
        ),
    )(*pieces, x, ctx, ctx_t, out_w, up_w, down_w, bias, up_b)


def qkv_kernel(held, x_ref, dqkv_ref, out_ref, *refs):
    grad_ref, sums_ref, x_t = refs[held:]
    step = pl.program_id(0)

    @pl.when(step == 0)
    def _():
        x_t[...] = x_ref[...].astype(F32).T.astype(BF)

    @pl.when(step < 3)
    def _():
        grad_ref[...] = mm(x_t[...], dqkv_ref[0]).astype(BF)
        sums_ref[0] = jnp.broadcast_to(total(dqkv_ref[0].astype(F32)), sums_ref.shape[1:])

    @pl.when(step == 3)
    def _():
        grad_ref[...] = out_ref[...]


def qkv_sums(room, held, x, d_qkv, out_low):
    _, seq, dim = d_qkv.shape

    def whole(a):
        return pl.BlockSpec(a.shape, lambda p: (0,) * a.ndim, pipeline_mode=pl.Buffered(1))

    shape = jax.ShapeDtypeStruct
    return pl.pallas_call(
        partial(qkv_kernel, len(held)),
        grid=(4,),
        in_specs=[
            whole(x),
            pl.BlockSpec((1, seq, dim), lambda p: (jnp.minimum(p, 2), 0, 0)),
            whole(out_low),
        ]
        + [pl.BlockSpec(memory_space=pl.ANY)] * len(held),
        out_specs=[
            pl.BlockSpec((dim, dim), lambda p: (p, 0)),
            pl.BlockSpec((1, 8, dim), lambda p: (jnp.minimum(p, 2), 0, 0)),
        ],
        out_shape=[shape((4 * dim + room, dim), BF), shape((3, 8, dim), F32)],
        scratch_shapes=[pltpu.VMEM((dim, seq), BF)],
        compiler_params=pltpu.CompilerParams(vmem_limit_bytes=VMEM_BYTES),
        cost_estimate=pl.CostEstimate(
            flops=8 * seq * dim * dim, bytes_accessed=24 * seq * dim, transcendentals=0
        ),
    )(x, d_qkv, out_low, *held)


def rows_grad_kernel(dqkv_ref, q_ref, k_ref, v_ref, dmid_ref, drows_ref, sum_ref):
    step = pl.program_id(0)

    @pl.when(step == 0)
    def _():
        sum_ref[...] = dmid_ref[...] + against(dqkv_ref[0], q_ref[...])

    @pl.when(step == 1)
    def _():
        sum_ref[...] += against(dqkv_ref[0], k_ref[...])

    @pl.when(step == 2)
    def _():
        drows_ref[...] = (sum_ref[...] + against(dqkv_ref[0], v_ref[...])).astype(BF)


def rows_grad(d_qkv, q_weight, k_weight, v_weight, d_mid):
    _, seq, dim = d_qkv.shape

    def whole(a):
        return pl.BlockSpec(a.shape, lambda p: (0,) * a.ndim, pipeline_mode=pl.Buffered(1))

    return pl.pallas_call(
        rows_grad_kernel,
        grid=(3,),
        in_specs=[pl.BlockSpec((1, seq, dim), lambda p: (p, 0, 0))]
        + [whole(a) for a in (q_weight, k_weight, v_weight, d_mid)],
        out_specs=pl.BlockSpec((seq, dim), lambda p: (0, 0)),
        out_shape=jax.ShapeDtypeStruct((seq, dim), BF),
        scratch_shapes=[pltpu.VMEM((seq, dim), F32)],
        compiler_params=pltpu.CompilerParams(vmem_limit_bytes=VMEM_BYTES),
        cost_estimate=pl.CostEstimate(
            flops=6 * seq * dim * dim, bytes_accessed=16 * seq * dim, transcendentals=0
        ),
    )(d_qkv, q_weight, k_weight, v_weight, d_mid)


def bucket_select(table):
    reach = (table.shape[0] - 1) // 2
    spots = jnp.arange(4 * reach, dtype=jnp.int32)
    bucket = jnp.clip(spots[None, :] - spots[:, None], -reach, reach) + reach
    return bucket[None] == jnp.arange(2 * reach + 1, dtype=jnp.int32)[:, None, None]


def spread_table(table):
    span = 2 * (table.shape[0] - 1)
    spread = lax.dot_general(
        table.astype(BF),
        bucket_select(table).astype(BF).reshape(table.shape[0], -1),
        (((0,), (0,)), ((), ())),
        preferred_element_type=F32,
    )
    return spread.astype(BF).reshape(HEADS, span, span)


def gather_table(spread, table):
    reach = (table.shape[0] - 1) // 2
    distance = jnp.arange(spread.shape[1], dtype=jnp.int32) - (4 * reach - 1)
    bucket = jnp.clip(distance, -reach, reach) + reach
    select = bucket[None, :] == jnp.arange(table.shape[0], dtype=jnp.int32)[:, None]
    return lax.dot_general(
        select.astype(F32),
        spread,
        (((1,), (1,)), ((), ())),
        precision=lax.Precision.HIGHEST,
        preferred_element_type=F32,
    )


def shift_pairs(size, step):
    return [(i, (i + step) % size) for i in range(size)]


def flip_pairs(size, step):
    return [(i, i ^ step) for i in range(size)]


def pick(array, index):
    return lax.dynamic_index_in_dim(array, index, 0, keepdims=False)


def swap_text(parts):
    return lax.all_to_all(parts, "wide", split_axis=0, concat_axis=0, tiled=True)


def patch_order(size):
    me = lax.axis_index("narrow")
    return [me ^ k for k in range(size)]


def swap_patch(parts):
    size = parts.shape[0]
    me = lax.axis_index("narrow")
    return [pick(parts, me)] + [
        lax.ppermute(pick(parts, me ^ k), "narrow", flip_pairs(size, k)) for k in range(1, size)
    ]


def flip_axis(array, axis, bit):
    return jnp.where(bit == 1, jnp.flip(array, axis), array)


def from_flipped(parts, me):
    size = parts.shape[0]
    bits = size.bit_length() - 1
    parts = parts.reshape((2,) * bits + parts.shape[1:])
    for b in range(bits):
        parts = flip_axis(parts, bits - 1 - b, (me >> b) & 1)
    return parts.reshape((size,) + parts.shape[bits:])


def patch_away(rows, size):
    parts = rows.reshape(size, -1, rows.shape[1])
    return [parts[0]] + [
        lax.ppermute(parts[k], "narrow", flip_pairs(size, k)) for k in range(1, size)
    ]


def patch_set(pieces, shape):
    return from_flipped(jnp.stack(pieces), lax.axis_index("narrow")).reshape(shape)


def add(*terms):
    total = terms[0].astype(F32)
    for term in terms[1:]:
        total = total + term.astype(F32)
    return total.astype(BF)


def wide_orders(wide, ways):
    bits = list(range(1, wide.bit_length() - 1))
    return [bits, bits[::-1]][:ways]


def wide_bit(bit):
    return (lax.axis_index("wide") >> bit) & 1


def add_kernel(me_ref, own_ref, arrived_ref, *refs):
    refs[-1][...] = (own_ref[0].astype(F32) + arrived_ref[...].astype(F32)).astype(BF)


def add_own(parts, me, arrived, held):
    rows, columns = arrived.shape
    steps = 2 if rows % 32 == 0 else 1
    block = rows // steps
    return pl.pallas_call(
        add_kernel,
        grid_spec=pltpu.PrefetchScalarGridSpec(
            num_scalar_prefetch=1,
            grid=(steps,),
            in_specs=[
                pl.BlockSpec((1, block, columns), lambda i, me_ref: (me_ref[0], i, 0)),
                pl.BlockSpec((block, columns), lambda i, me_ref: (i, 0)),
            ]
            + [pl.BlockSpec(memory_space=pl.ANY)] * len(held),
            out_specs=pl.BlockSpec((block, columns), lambda i, me_ref: (i, 0)),
        ),
        out_shape=jax.ShapeDtypeStruct((rows, columns), BF),
        compiler_params=pltpu.CompilerParams(vmem_limit_bytes=VMEM_BYTES),
        cost_estimate=pl.CostEstimate(flops=0, bytes_accessed=6 * rows * columns, transcendentals=0),
    )(me.reshape(1), parts, arrived, *held)


def wide_step(grad, wide, bit, held=()):
    parts = grad.reshape(2, -1, grad.shape[1])
    me = wide_bit(bit)
    arrived = lax.ppermute(pick(parts, 1 - me), "wide", flip_pairs(wide, 1 << bit))
    return add_own(parts, me, arrived, held) if held else add(pick(parts, me), arrived)


def cut(grad, parts):
    first = -(-grad.shape[0] // (16 * parts)) * 8 * parts
    return [grad[:first], grad[first:]]


def wide_steps(shares, wide, i, held=()):
    orders = wide_orders(wide, len(shares))
    return [
        wide_step(a, wide, order[i], held if n == 0 else ())
        for n, (a, order) in enumerate(zip(shares, orders))
    ]


def narrow_step(shares, narrow):
    me = lax.axis_index("narrow")
    parts = [a.reshape(narrow, -1, a.shape[1]) for a in shares]

    def picked(index):
        return jnp.concatenate([pick(a, index) for a in parts], axis=0)

    arrived = [
        lax.ppermute(picked(me ^ k), "narrow", flip_pairs(narrow, k)) for k in range(1, narrow)
    ]
    return add(picked(me), *arrived)


def gather_narrow(part, narrow, lengths):
    parts = [part] + [
        lax.ppermute(part, "narrow", flip_pairs(narrow, k)) for k in range(1, narrow)
    ]
    parts = jnp.stack(parts)
    return [parts[:, : lengths[0]], parts[:, lengths[0] :]]


def gather_wide(shares, wide, i):
    return [
        jnp.concatenate([a, lax.ppermute(a, "wide", flip_pairs(wide, 1 << order[i]))], axis=0)
        for a, order in zip(shares, wide_orders(wide, len(shares)))
    ]


def gather_core(shares, wide):
    return shares + [lax.ppermute(a, "wide", flip_pairs(wide, 1)) for a in shares]


def finish_kernel(places, ways, cuts, index_ref, up_ref, down_ref, *refs):
    pieces, outs = refs[: 2 * ways], refs[2 * ways :]
    *outs, up_out, down_out = outs
    up_out[...] = up_ref[...].astype(F32)
    down_out[...] = down_ref[...].astype(F32)

    @pl.when(pl.program_id(0) == 0)
    def _():
        put_pieces(places, ways, cuts, index_ref, pieces, outs)


def put_pieces(places, ways, cuts, index_ref, pieces, outs):
    at = 0
    for core in range(2):
        for way in range(ways):
            rows = pieces[way].shape[1]
            for place in range(places):
                here = index_ref[way, place]
                for (start, stop), out in zip(cuts, outs):
                    low, high = max(at, start), min(at + rows, stop)
                    if low < high:
                        same = pieces[way][here].astype(F32)
                        other = pieces[ways + way][here].astype(F32)
                        block = jnp.where(index_ref[2, 0] == core, same, other)
                        out[low - start : high - start, :] = block[low - at : high - at]
                at += rows


def finish(totals, pieces, wide, narrow, lengths):
    places, _, columns = pieces[0].shape
    ways = len(pieces) // 2
    index = []
    for order in wide_orders(wide, 2):
        me = jnp.int32(0)
        for bit in order:
            me = me * 2 + wide_bit(bit)
        me = me * narrow + lax.axis_index("narrow")
        index.append(jnp.arange(places, dtype=jnp.int32) ^ me)
    index.append(jnp.full((places,), wide_bit(0), jnp.int32))
    cuts = []
    for length in lengths:
        start = cuts[-1][1] if cuts else 0
        cuts.append((start, start + length))
    blocks = [pl.BlockSpec((a.shape[0] // 2, a.shape[1]), lambda p: (p, 0)) for a in totals]

    def whole(shape):
        return pl.BlockSpec(shape, lambda p: (0,) * len(shape), pipeline_mode=pl.Buffered(1))

    return pl.pallas_call(
        partial(finish_kernel, places, ways, cuts),
        grid=(2,),
        in_specs=[pl.BlockSpec(memory_space=pltpu.SMEM)]
        + blocks
        + [whole(a.shape) for a in pieces],
        out_specs=[whole((length, columns)) for length in lengths] + blocks,
        out_shape=[jax.ShapeDtypeStruct((length, columns), F32) for length in lengths]
        + [jax.ShapeDtypeStruct(a.shape, F32) for a in totals],
        compiler_params=pltpu.CompilerParams(vmem_limit_bytes=VMEM_BYTES),
        cost_estimate=pl.CostEstimate(
            flops=0,
            bytes_accessed=8 * sum(lengths) * columns + 6 * sum(a.size for a in totals),
            transcendentals=0,
        ),
    )(jnp.stack(index), *totals, *pieces)


def room_for(rows, wide, narrow):
    return 32 + -(rows + 32) % (8 * wide * narrow)


def pack(grads, columns, rows):
    lines = []
    for grad in grads:
        flat = grad.reshape(-1)
        lines.append(jnp.pad(flat, (0, -flat.shape[0] % columns)).reshape(-1, columns))
    lines = jnp.concatenate(lines, axis=0)
    return jnp.pad(lines, ((0, -lines.shape[0] % rows), (0, 0)))


def unpack(lines, grads):
    columns = lines.shape[1]
    at = 0
    out = []
    for grad in grads:
        count = -(-grad.size // columns)
        out.append(lines[at : at + count].reshape(-1)[: grad.size].reshape(grad.shape))
        at += count
    return out


def body(
    text_in,
    patch_in,
    res_class,
    text_len,
    pos_line,
    pos_x,
    pos_y,
    query_weight,
    query_bias,
    key_weight,
    value_weight,
    value_bias,
    output_weight,
    output_bias,
    norm_gain,
    norm_shift,
    up_weight,
    up_bias,
    down_weight,
    down_bias,
    final_gain,
    final_shift,
    line_table,
    width_table,
    height_table,
    cot_text,
    cot_patch,
):
    text_shape = text_in.shape
    patch_shape = patch_in.shape
    dim = text_shape[3]
    seq = TEXT + PATCH
    lanes = -(-seq // 128) * 128
    wide = text_shape[0]
    narrow = patch_shape[1]
    pieces = [swap_text(text_in.reshape(wide, -1, dim)).reshape(-1, dim)]
    pieces += swap_patch(patch_in.reshape(narrow, -1, dim))
    cot_text, pieces[0] = lax.optimization_barrier((cot_text, pieces[0]))
    cot_patch, pieces = lax.optimization_barrier((cot_patch, pieces))
    cots = [swap_text(cot_text.reshape(wide, -1, dim)).reshape(-1, dim)]
    cots += swap_patch(cot_patch.reshape(narrow, -1, dim))
    index = jnp.arange(seq, dtype=jnp.int32)
    live_patch = jnp.where(res_class.reshape(()) == 1, PATCH, SMALL_PATCH)
    valid = jnp.where(index < TEXT, index < text_len.reshape(()), index - TEXT < live_patch)
    facts = jnp.concatenate(
        [pos_line.reshape(1, -1), pos_x.reshape(1, -1), pos_y.reshape(1, -1), valid.astype(jnp.int32)[None]]
    )
    patch_facts = facts[:, TEXT:].reshape(4, narrow, -1)
    facts = jnp.concatenate(
        [facts[:, :TEXT]]
        + [
            lax.dynamic_index_in_dim(patch_facts, i, 1, keepdims=False)
            for i in patch_order(narrow)
        ],
        axis=1,
    )
    line_spots, x_spots, y_spots = facts[0], facts[1], facts[2]
    valid = facts[3] == 1

    line = spread_table(line_table)
    width = spread_table(width_table)
    height = spread_table(height_table)
    hots = []
    hots_t = []
    hots_back = []
    for spots, table in ((line_spots, line_table), (x_spots, width_table), (y_spots, height_table)):
        span = jnp.arange(2 * (table.shape[0] - 1), dtype=jnp.int32)
        long = jnp.pad(spots, (0, lanes - seq), constant_values=-1)
        hots.append((long[:, None] == span[None, :]).astype(BF))
        hots_t.append((long[None, :] == span[:, None]).astype(BF))
        hots_back.append((long[None, :] == span[::-1, None]).astype(BF))
    hot = jnp.concatenate(hots, axis=1)
    hot_t = jnp.concatenate(hots_t, axis=0)
    hot_back = jnp.concatenate(hots_back, axis=0)
    column = jnp.arange(128, dtype=jnp.int32)
    mask = jnp.where((column[None, :] % 64 == 0) & ~valid[:, None], -1e30, 0.0).astype(BF)

    exps, ctx_t, ctx, inverse, q, k_t, v, rows_in = attend(
        pieces,
        query_weight,
        key_weight,
        value_weight,
        jnp.stack([query_bias, value_bias])[:, None],
        hot,
        mask,
        hot_t,
        line,
        width,
        height,
    )
    vectors = jnp.stack(
        [output_bias, norm_gain, norm_shift, down_bias, final_gain, final_shift] + [final_shift] * 2
    )
    final_low, d_mid, d_attn, up_low, down_low, out_low, sums, up_sum = rows_pass(
        cots, rows_in, ctx, ctx_t, output_weight, up_weight, down_weight, vectors, up_bias[None]
    )
    early = (sums[0], sums[1], sums[2], up_sum, sums[3], sums[4], sums[5])
    down_total, up_total = lax.psum((down_low, up_low), ("wide", "narrow"))

    def backward():
        text_out = swap_text(final_low[:TEXT].reshape(wide, -1, dim)).reshape(text_shape)
        out_pieces = patch_away(final_low[TEXT:], narrow)
        levels = wide.bit_length() - 2
        d_qkv, spread = attend_back(
            0, HEADS // 2, [], exps, ctx_t, inverse, v, k_t, q, d_attn, output_weight, hot, hot_back
        )
        room = room_for(4 * dim, wide, narrow)
        tail, d_sums = qkv_sums(room, [text_out, *out_pieces[1:]], rows_in, d_qkv, out_low)
        d_rows = rows_grad(d_qkv, query_weight, key_weight, value_weight, d_mid)
        text_grad = swap_text(d_rows[:TEXT].reshape(wide, -1, dim)).reshape(text_shape)
        grad_pieces = patch_away(d_rows[TEXT:], narrow)
        late = (
            d_sums[0, 0],
            d_sums[2, 0],
            gather_table(spread[:, 2], line_table),
            gather_table(spread[:, 0], width_table),
            gather_table(spread[:, 1], height_table),
        )
        small = pack(early + late, dim, room).astype(BF)
        tail = lax.dynamic_update_slice(tail, small, (4 * dim, 0))
        halves = cut(wide_step(tail, wide, 0), wide * narrow // 2)
        for i in range(levels):
            moved = [text_grad, *grad_pieces[1:]] if i == levels - 1 else []
            halves = wide_steps(halves, wide, i, moved)
        lengths = [a.shape[0] // narrow for a in halves]
        halves = gather_narrow(narrow_step(halves, narrow), narrow, lengths)
        for i in range(levels - 1, -1, -1):
            halves = gather_wide(halves, wide, i)
        return (
            text_out, patch_set(out_pieces, patch_shape), text_grad,
            patch_set(grad_pieces, patch_shape), *gather_core(halves, wide),
        )

    def never():
        return jax.tree.map(lambda a: jnp.zeros(a.shape, a.dtype), jax.eval_shape(backward))

    text_out, patch_out, text_grad, patch_grad, *pieces = lax.cond(
        text_len.reshape(()) >= 0, backward, never
    )
    (
        query_weight_grad, key_weight_grad, value_weight_grad, output_weight_grad, small,
        up_weight_grad, down_weight_grad,
    ) = finish((up_total, down_total), pieces, wide, narrow, (dim,) * 4 + (32,))
    late = (query_bias, value_bias, line_table, width_table, height_table)
    (
        output_bias_grad, norm_gain_grad, norm_shift_grad, up_bias_grad, down_bias_grad,
        final_gain_grad, final_shift_grad, query_bias_grad, value_bias_grad, line_table_grad,
        width_table_grad, height_table_grad,
    ) = unpack(small, early + late)
    up_bias_grad = up_bias_grad.reshape(-1)
    return (
        text_out,
        patch_out,
        text_grad,
        patch_grad,
        query_weight_grad,
        query_bias_grad,
        key_weight_grad,
        value_weight_grad,
        value_bias_grad,
        output_weight_grad,
        output_bias_grad,
        norm_gain_grad,
        norm_shift_grad,
        up_weight_grad,
        up_bias_grad,
        down_weight_grad,
        down_bias_grad,
        final_gain_grad,
        final_shift_grad,
        line_table_grad,
        width_table_grad,
        height_table_grad,
    )


def solution(mesh):
    text = P(None, "narrow", "wide", None)
    patch = P("wide", None, "narrow", None)
    page = P("wide", "narrow")
    spots = P("wide", "narrow", None)
    in_specs = (text, patch, page, page, spots, spots, spots) + (P(),) * 18 + (text, patch)
    out_specs = (text, patch, text, patch) + (P(),) * 18
    return jax.shard_map(body, mesh=mesh, in_specs=in_specs, out_specs=out_specs, check_vma=False)
```
